32 devices in a mesh: section: 4 (over x, core), dp: 2 (over y), tensor: 4 (over z).
Axes of the slice: x: 2, y: 2, z: 4, core: 2. Of those that a mesh axis runs over, the one named last changes fastest.
Arguments:
- clean: bfloat16 [8, 256, 768], P('dp'), may hold values from -6 to 6
- noise: bfloat16 [8, 256, 768], P('dp'), may hold values from -6 to 6
- times: int32 [8], P('dp'), may hold values from 0 to 999
- flags: int32 [8], P('dp'), may hold values 0 or 1
- cotangent: bfloat16 [8, 256, 768], P('dp'), may hold values from -6 to 6
- w_main: bfloat16 [4, 768, 4, 768], P('section', None, None, 'tensor')
- w_half: bfloat16 [4, 1536, 768], P('section', 'tensor'), may hold values from -0.109375 to 0.109375
- w_mod: bfloat16 [4, 768, 3, 768], P('section', None, None, 'tensor'), may hold values from -0.15625 to 0.15625
Outputs:
- section_out: float32 [4, 8, 256, 768], P('section', 'dp', 'tensor')
- section_in_grad: float32 [4, 8, 256, 768], P('section', 'dp', 'tensor')
- grad_main: float32 [4, 768, 4, 768], P('section', None, None, 'tensor')
- grad_half: float32 [4, 1536, 768], P('section', 'tensor')
- grad_mod: float32 [4, 768, 3, 768], P('section', None, None, 'tensor')
The draws below stay inside these ranges and needn't reach their ends.
All inputs are finite; a program needn't handle non-finite values. No bound on the sum of `flags` on one device may be relied on, other than what follows from the above.
Results may differ from the reference program's by a relative error of at most 0.017.
Values may be sent and summed in bfloat16 or wider, within the bound.
No kernel may reach another device: no remote copies, remote signals or barrier semaphores. Data moves between devices by JAX's collectives and lax.ppermute only.
A program may use at most 192 MiB of HBM per device.

```python
import math
import jax
import jax.numpy as jnp
from jax import lax

HEADS = 12
HEAD_DIM = 64
D = 768
FF = 3072
SEQ_LEN = 256
QBLOCK = 256
TSTEPS = 1000
SEQS = 8
N_SECTION = 4
N_TENSOR = 4


def draw_w_main(key, part):
    key = jax.random.fold_in(key, 11)
    base = jax.random.normal(key, (N_SECTION, D, 4, D), jnp.float32) * D ** (-0.5)
    even_section = (jnp.arange(N_SECTION) % 2 == 0)[:, None, None, None]
    outward = (jnp.arange(4) == 3)[None, None, :, None]
    return (base * jnp.where(even_section & outward, 8.0, 1.0)).astype(jnp.bfloat16)


def set_ends(values, key, smallest, high):
    index_at = [jax.random.randint(jax.random.fold_in(key, axis), (), 0, length) for axis, length in enumerate(values.shape)]
    widest = values.shape.index(max(values.shape))
    next_to = index_at[:widest] + [(index_at[widest] + 1) % values.shape[widest]] + index_at[widest + 1:]
    return values.at[tuple(index_at)].set(smallest).at[tuple(next_to)].set(high)


def shard_levels(own_key, dims, cuts, least, high):
    factor_of = 1.0
    for dim, shards_of in cuts:
        heights = jax.random.uniform(jax.random.fold_in(jax.random.fold_in(own_key, 6), dim), (shards_of,), jnp.float32, least / len(cuts), high / len(cuts))
        factor_of = factor_of * jnp.repeat(jnp.exp(heights), dims[dim] // shards_of).reshape((-1,) + (1,) * (len(dims) - 1 - dim))
    return factor_of


def normal_values(stream_key, shape, deviation, limit, shards=(), kind=jnp.bfloat16):
    factor_of = shard_levels(stream_key, shape, shards, -0.22, 0.18) if shards else 1.0
    entries = jax.random.normal(stream_key, shape, jnp.float32) * deviation * factor_of
    return jnp.minimum(jnp.maximum(entries, -limit), limit).astype(kind)


def setup_inputs(seed: int = 0) -> dict:
    key_list = jax.random.split(jax.random.key(seed), 9)
    return {
        "clean": normal_values(key_list[0], (SEQS, SEQ_LEN, D), 1.0, 6.0, ((0, 2),)),
        "noise": normal_values(key_list[1], (SEQS, SEQ_LEN, D), 1.0, 6.0, ((0, 2),)),
        "times": set_ends(jax.random.randint(key_list[2], (SEQS,), 0, TSTEPS), jax.random.fold_in(key_list[2], 1), 0, TSTEPS - 1).astype(jnp.int32),
        "flags": set_ends((jax.random.randint(key_list[3], (SEQS,), 0, 2) < 1).astype(jnp.int32), jax.random.fold_in(key_list[3], 1), 0, 1),
        "cotangent": normal_values(key_list[4], (SEQS, SEQ_LEN, D), 1.0, 6.0, ((0, 2),)),
        "w_main": draw_w_main(jax.random.fold_in(key_list[8], 71), 0),
        "w_half": normal_values(key_list[6], (N_SECTION, FF // 2, D), FF ** -0.5, 0.109375, ((0, 4), (1, 4))),
        "w_mod": normal_values(key_list[7], (N_SECTION, D, 3, D), (2 * D) ** -0.5, 0.15625, ((0, 4), (3, 4))),
    }


epsilon = 1e-05
highest = lax.Precision.HIGHEST

@jax.custom_vjp
def low(v):
    return lax.optimization_barrier(v.astype(jnp.bfloat16)).astype(jnp.float32)

@jax.custom_vjp
def low_back(v):
    return v

def low_keep(v):
    return (low(v), None)

def low_pass(kept, grad):
    return (grad,)

def back_keep(v):
    return (v, None)

def back_low(kept, grad):
    return (low(grad),)
low.defvjp(low_keep, low_pass)
low_back.defvjp(back_keep, back_low)

def time_embed(times):
    halfwidth = D // 2
    freqs = jnp.exp(-math.log(10000.0) * jnp.arange(halfwidth, dtype=jnp.float32) / halfwidth)
    angles = times.astype(jnp.float32)[:, None] * freqs[None, :]
    return jnp.concatenate([jnp.sin(angles), jnp.cos(angles)], axis=1)

def rope_tables():
    halfdim = HEAD_DIM // 2
    inverse = jnp.exp(-math.log(10000.0) * 2.0 * jnp.arange(halfdim, dtype=jnp.float32) / HEAD_DIM)
    angles = jnp.arange(SEQ_LEN, dtype=jnp.float32)[:, None] * inverse[None, :]
    return (jnp.cos(angles), jnp.sin(angles))

def rotate(values, cosine, sine):
    halfdim = values.shape[-1] // 2
    first_half, second_half = (values[..., :halfdim], values[..., halfdim:])
    cosine = cosine[:, None, :]
    sine = sine[:, None, :]
    return jnp.concatenate([first_half * cosine - second_half * sine, first_half * sine + second_half * cosine], axis=-1)

def normalize(stream, shift, scale):
    centred = stream - lax.optimization_barrier(jnp.mean(stream, axis=-1, keepdims=True))
    variance = lax.optimization_barrier(jnp.mean(centred * centred, axis=-1, keepdims=True))
    return centred * lax.rsqrt(variance + epsilon) * (1.0 + scale[:, None, :]) + shift[:, None, :]

def product(left, right):
    return jnp.matmul(left, right, precision=highest)

def attention_half(stream, modes, weights):
    count = stream.shape[0]
    normed = low(normalize(stream, modes[:, 0], modes[:, 1]))
    cosine, sine = rope_tables()

    def split_heads(values):
        return values.reshape(count, SEQ_LEN, HEADS, HEAD_DIM)
    queries = low(rotate(split_heads(low_back(product(normed, weights[:, 0, :]))), cosine, sine))
    keys = low(rotate(split_heads(low_back(product(normed, weights[:, 1, :]))), cosine, sine))
    values = split_heads(low(low_back(product(normed, weights[:, 2, :]))))
    factor = HEAD_DIM ** (-0.5)
    blocks = queries.reshape(count, SEQ_LEN // QBLOCK, QBLOCK, HEADS, HEAD_DIM).transpose(1, 0, 2, 3, 4)

    def one_block(query_block):
        scores = low_back(factor * jnp.einsum('nqhd,nkhd->nhqk', query_block, keys, precision=highest))
        probs = low(jax.nn.softmax(scores, axis=-1))
        return jnp.einsum('nhqk,nkhd->nqhd', probs, values, precision=highest)
    attended = lax.map(jax.checkpoint(one_block), blocks)
    attended = attended.transpose(1, 0, 2, 3, 4).reshape(count, SEQ_LEN, D)
    attended = low(low_back(attended))
    branch = low_back(product(attended, weights[:, 3, :].T))
    return stream + modes[:, 2][:, None, :] * branch

def mlp_half(stream, modes, first_matrix, second_matrix):
    normed = low(normalize(stream, modes[:, 0], modes[:, 1]))
    hidden = low_back(product(normed, first_matrix))
    act = low(jax.nn.gelu(hidden, approximate=True))
    branch = low_back(product(act, second_matrix))
    return stream + modes[:, 2][:, None, :] * branch

def mlp_rows(first, second):
    quarter = D // N_TENSOR

    def spread(half):
        return half.reshape(N_TENSOR, 2, quarter, D).transpose(1, 0, 2, 3).reshape(2 * D, D)
    return jnp.concatenate([spread(first), spread(second)], axis=0)

def stack_forward(start, probes, w_main, w_half, w_mod, temb):
    results = []
    stream = start + probes[0]
    result = stream
    for section in range(N_SECTION):
        modes = jnp.einsum('nd,dpe->npe', temb, w_mod[section], precision=highest)
        if section % 2 == 0:
            result = attention_half(stream, modes, w_main[section])
        else:
            result = mlp_half(stream, modes, w_main[section].reshape(D, FF), mlp_rows(w_half[section - 1], w_half[section]))
        results.append(result)
        if section + 1 < N_SECTION:
            stream = low_back(low(result)) + probes[section + 1]
    return (result, jnp.stack(results))

def reference(clean, noise, times, flags, cotangent, w_main, w_half, w_mod):
    main_f = w_main.astype(jnp.float32)
    half_f = w_half.astype(jnp.float32)
    mod_f = w_mod.astype(jnp.float32)
    group = 4
    count = SEQS // group

    def split(values):
        return values.reshape((count, group) + values.shape[1:])

    def one_group(carry, inputs):
        clean_g, noise_g, times_g, flags_g, cot_g = inputs
        theta = math.pi / 2 * (times_g.astype(jnp.float32) + 1.0) / (TSTEPS + 1.0)
        noisy = jnp.cos(theta)[:, None, None] * clean_g.astype(jnp.float32) + jnp.sin(theta)[:, None, None] * noise_g.astype(jnp.float32)
        temb = time_embed(times_g)
        zeros = jnp.zeros((N_SECTION,) + noisy.shape, jnp.float32)
        guess = low(stack_forward(noisy, zeros, main_f, half_f, mod_f, temb)[0])
        start = noisy + flags_g.astype(jnp.float32)[:, None, None] * guess

        def forward(probes, main_w, half_w, mod_w):
            return stack_forward(start, probes, main_w, half_w, mod_w, temb)
        final, pull, results = jax.vjp(forward, zeros, main_f, half_f, mod_f, has_aux=True)
        probe_grad, main_grad, half_grad, mod_grad = pull(cot_g.astype(jnp.float32))
        carry = (carry[0] + main_grad, carry[1] + half_grad, carry[2] + mod_grad)
        return (carry, (results, probe_grad))
    start_carry = (jnp.zeros(main_f.shape, jnp.float32), jnp.zeros(half_f.shape, jnp.float32), jnp.zeros(mod_f.shape, jnp.float32))
    totals, stacked = lax.scan(one_group, start_carry, (split(clean), split(noise), split(times), split(flags), split(cotangent)))
    outs = stacked[0].transpose(1, 0, 2, 3, 4).reshape(N_SECTION, SEQS, SEQ_LEN, D)
    grads = stacked[1].transpose(1, 0, 2, 3, 4).reshape(N_SECTION, SEQS, SEQ_LEN, D)
    return (outs, grads, totals[0], totals[1], totals[2])
```

```python
import functools
import math

import jax
import jax.numpy as jnp
from jax import lax
from jax.experimental import pallas as pl
from jax.experimental.pallas import tpu as pltpu
from jax.sharding import PartitionSpec as P

HEAD_DIM = 64
TSTEPS = 1000
EPSILON = 1e-05
HIGHEST = lax.Precision.HIGHEST
BF = jnp.bfloat16
F32 = jnp.float32
VMEM_BYTES = 48 * 1024 * 1024
GELU_C = math.sqrt(2.0 / math.pi)
GELU_A = 0.044715


def cyclic(value, axis, by):
    size = lax.axis_size(axis)
    return lax.ppermute(value, axis, [(i, (i + by) % size) for i in range(size)])


def swap(value, axis, bit):
    size = lax.axis_size(axis)
    return lax.ppermute(value, axis, [(i, i ^ bit) for i in range(size)])


def within(value, axis, which, route):
    size = lax.axis_size(axis)
    pairs = [(s * size + i, s * size + route(i, size)) for s in which for i in range(size)]
    return lax.ppermute(value, ("section", axis), pairs)


def section_hop(value, source, by):
    target = source + by
    if source // 2 == target // 2:
        return swap(value, "section", 1)
    return cyclic(value, "section", by)


def dot(left, right):
    return lax.dot_general(left, right, (((1,), (0,)), ((), ())), preferred_element_type=F32)


def dot_nt(left, right):
    return lax.dot_general(left, right, (((1,), (1,)), ((), ())), preferred_element_type=F32)


def dot_tn(left, right):
    return lax.dot_general(left, right, (((0,), (0,)), ((), ())), preferred_element_type=F32)


def standardize(stream):
    centred = stream - jnp.mean(stream, axis=-1, keepdims=True)
    variance = jnp.mean(centred * centred, axis=-1, keepdims=True)
    inverse = lax.rsqrt(variance + EPSILON)
    return centred * inverse, inverse


def swap_halves(block, first):
    return jnp.where(first, pltpu.roll(block, 96, 1), pltpu.roll(block, 32, 1))


def first_mask(rows):
    lane = lax.broadcasted_iota(jnp.int32, (rows, 128), 1)
    return (lane % HEAD_DIM) < HEAD_DIM // 2


def softmax(scores):
    top = jnp.max(scores, axis=-1, keepdims=True)
    raised = jnp.exp(scores - top)
    return raised * (1.0 / jnp.sum(raised, axis=-1, keepdims=True))


def load_stream(base_ref, arrived_ref, flag_ref):
    if base_ref is None:
        return arrived_ref[...].astype(F32)
    if arrived_ref is None:
        return base_ref[...]
    return base_ref[...] + flag_ref[0].astype(F32) * arrived_ref[...].astype(F32)


def start_copies(source, target, sems):
    for j in range(4):
        pltpu.make_async_copy(source.at[j], target.at[j], sems.at[j]).start()


def wait_copy(source, target, sems, j):
    pltpu.make_async_copy(source.at[j], target.at[j], sems.at[j]).wait()


def norm_back(normed_grad, stream, scale, grad):
    hat, inverse = standardize(stream)
    shift_grad = jnp.sum(normed_grad, axis=0, keepdims=True)
    scale_grad = jnp.sum(normed_grad * hat, axis=0, keepdims=True)
    hat_grad = normed_grad * (1.0 + scale)
    mean_one = jnp.mean(hat_grad, axis=-1, keepdims=True)
    mean_two = jnp.mean(hat_grad * hat, axis=-1, keepdims=True)
    in_grad = grad + inverse * (hat_grad - mean_one - hat * mean_two)
    return in_grad, shift_grad, scale_grad


def attention_forward_kernel(has_base, has_arrived, keep, *refs):
    refs = list(refs)
    active = refs.pop(0)
    flag = refs.pop(0)
    base = refs.pop(0) if has_base else None
    arrived = refs.pop(0) if has_arrived else None
    modes, cosine, sine, weights = refs[:4]
    refs = refs[4:]
    result = refs.pop(0)
    if keep:
        normed_out, heads_out, attended_out, branch_out = refs[:4]
        refs = refs[4:]
    w, normed_ref, branch_ref, sems = refs

    @pl.when(active[0] == 1)
    def _():
        start_copies(weights, w, sems)
        stream = load_stream(base, arrived, flag)
        hat, _ = standardize(stream)
        normed_ref[...] = (hat * (1.0 + modes[1:2, :]) + modes[0:1, :]).astype(BF)
        branch_ref[...] = jnp.zeros_like(branch_ref)
        rows = normed_ref.shape[0]
        first = first_mask(rows)
        low = lax.broadcasted_iota(jnp.int32, (rows, 128), 1) < HEAD_DIM

        def shard(j, carry):
            wait_copy(weights, w, sems, j)
            raw = dot(normed_ref[...], w[j, :, :576])
            turned = []
            for unit in range(3):
                block = raw[:, unit * 128 : (unit + 1) * 128]
                block = block * cosine[...] + swap_halves(block, first) * sine[...]
                if unit == 0:
                    block = block * 0.125
                if unit == 1:
                    block = jnp.where(low, block * 0.125, block)
                turned.append(block)
            joined = jnp.concatenate(turned + [raw[:, 384:576]], axis=1).astype(BF)
            if keep:
                heads_out[j] = joined
            pieces = [jnp.zeros((rows, HEAD_DIM), BF)]
            for head in range(3):
                q = joined[:, head * 64 : head * 64 + 64]
                k = joined[:, 192 + head * 64 : 192 + head * 64 + 64]
                v = joined[:, 384 + head * 64 : 384 + head * 64 + 64]
                probs = softmax(dot_nt(q, k)).astype(BF)
                pieces.append(dot(probs, v).astype(BF))
            attended = jnp.concatenate(pieces, axis=1)
            if keep:
                attended_out[j] = attended
            branch_ref[...] += dot_nt(attended, w[j, :, 512:768])
            return carry

        lax.fori_loop(0, 4, shard, 0)
        result[...] = (load_stream(base, arrived, flag) + modes[2:3, :] * branch_ref[...]).astype(BF)
        if keep:
            normed_out[...] = normed_ref[...]
            branch_out[...] = branch_ref[...]


def vmem():
    return pl.BlockSpec(memory_space=pltpu.VMEM)


def smem():
    return pl.BlockSpec(memory_space=pltpu.SMEM)


def anywhere():
    return pl.BlockSpec(memory_space=pl.ANY)


def params():
    return pltpu.CompilerParams(vmem_limit_bytes=VMEM_BYTES)


def cost(flops, nbytes):
    return pl.CostEstimate(flops=flops, bytes_accessed=nbytes, transcendentals=0)


def attention_forward(active, flag, base, arrived, modes, cosine, sine, weights, keep):
    width = modes.shape[1]
    rows = cosine.shape[0]
    shape = jax.ShapeDtypeStruct
    outs = [shape((rows, width), BF)]
    if keep:
        outs += [
            shape((rows, width), BF),
            shape((4, rows, 576), BF),
            shape((4, rows, 256), BF),
            shape((rows, width), F32),
        ]
    operands = [active, flag]
    specs = [smem(), smem()]
    for value in (base, arrived):
        if value is not None:
            operands.append(value)
            specs.append(vmem())
    operands += [modes, cosine, sine, weights]
    specs += [vmem()] * 3 + [anywhere()]
    return pl.pallas_call(
        functools.partial(
            attention_forward_kernel, base is not None, arrived is not None, keep
        ),
        out_shape=outs,
        in_specs=specs,
        out_specs=[vmem()] * len(outs),
        scratch_shapes=[
            pltpu.VMEM(weights.shape, BF),
            pltpu.VMEM((rows, width), BF),
            pltpu.VMEM((rows, width), F32),
            pltpu.SemaphoreType.DMA((4,)),
        ],
        compiler_params=params(),
        cost_estimate=cost(2_000_000_000, 6_000_000),
    )(*operands)


def attention_back_kernel(has_base, *refs):
    refs = list(refs)
    active = refs.pop(0)
    flag = refs.pop(0)
    base = refs.pop(0) if has_base else None
    arrived, grad, branch, heads_in, attended_in, modes, cosine, sine, weights = refs[:9]
    in_grad, mode_grad, pack, branch_grad_out = refs[9:13]
    w, bg_ref, ng_ref, sems = refs[13:]

    @pl.when(active[0] == 1)
    def _():
        start_copies(weights, w, sems)
        g = grad[...].astype(F32)
        rows = g.shape[0]
        mode_grad[2:3, :] = jnp.sum(g * branch[...], axis=0, keepdims=True)
        bg_ref[...] = (modes[2:3, :] * g).astype(BF)
        branch_grad_out[...] = bg_ref[...]
        ng_ref[...] = jnp.zeros_like(ng_ref)
        first = first_mask(rows)

        def shard(j, carry):
            wait_copy(weights, w, sems, j)
            joined = heads_in[j]
            att_grad = dot(bg_ref[...], w[j, :, 512:768]).astype(BF)
            dq, dk, dv = [], [], []
            for head in range(3):
                q = joined[:, head * 64 : head * 64 + 64]
                k = joined[:, 192 + head * 64 : 192 + head * 64 + 64]
                v = joined[:, 384 + head * 64 : 384 + head * 64 + 64]
                da = att_grad[:, 64 + head * 64 : 128 + head * 64]
                probs = softmax(dot_nt(q, k))
                prob_grad = dot_nt(da, v)
                dv.append(dot_tn(probs.astype(BF), da))
                inner = jnp.sum(prob_grad * probs, axis=-1, keepdims=True)
                ds = (probs * (prob_grad - inner)).astype(BF)
                dq.append(dot(ds, k) * 0.125)
                dk.append(dot_tn(ds, q))
            both = jnp.concatenate(dq + dk, axis=1)
            turned = []
            for unit in range(3):
                block = both[:, unit * 128 : (unit + 1) * 128]
                turned.append(block * cosine[...] - swap_halves(block, first) * sine[...])
            raw = jnp.concatenate(turned + dv, axis=1).astype(BF)
            pack[j, :, :512] = raw[:, :512]
            pack[j, :, 512:768] = jnp.concatenate(
                [raw[:, 512:576], attended_in[j, :, 64:256]], axis=1
            )
            ng_ref[...] += dot_nt(raw, w[j, :, :576])
            return carry

        lax.fori_loop(0, 4, shard, 0)
        stream = load_stream(base, arrived, flag)
        total, shift_grad, scale_grad = norm_back(
            ng_ref[...], stream, modes[1:2, :], grad[...].astype(F32)
        )
        in_grad[...] = total.astype(BF)
        mode_grad[0:1, :] = shift_grad
        mode_grad[1:2, :] = scale_grad


def attention_back(
    active, flag, base, arrived, grad, branch, heads, attended, modes, cosine, sine, weights
):
    rows, width = grad.shape
    shape = jax.ShapeDtypeStruct
    outs = [
        shape((rows, width), BF),
        shape((3, width), F32),
        shape((4, rows, width), BF),
        shape((rows, width), BF),
    ]
    operands = [active, flag]
    specs = [smem(), smem()]
    if base is not None:
        operands.append(base)
        specs.append(vmem())
    operands += [arrived, grad, branch, heads, attended, modes, cosine, sine, weights]
    specs += [vmem()] * 8 + [anywhere()]
    return pl.pallas_call(
        functools.partial(attention_back_kernel, base is not None),
        out_shape=outs,
        in_specs=specs,
        out_specs=[vmem()] * len(outs),
        scratch_shapes=[
            pltpu.VMEM(weights.shape, BF),
            pltpu.VMEM((rows, width), BF),
            pltpu.VMEM((rows, width), F32),
            pltpu.SemaphoreType.DMA((4,)),
        ],
        compiler_params=params(),
        cost_estimate=cost(3_000_000_000, 10_000_000),
    )(*operands)


def mlp_forward_kernel(keep, *refs):
    active, arrived, modes, first, second_a, second_b = refs[:6]
    refs = refs[6:]
    result = refs[0]
    refs = refs[1:]
    if keep:
        normed_out, act_out, slope_out, branch_out = refs[:4]
        refs = refs[4:]
    w1, w2, normed_ref, branch_ref, sems = refs
    half = second_a.shape[1]

    def seconds(j):
        return (
            pltpu.make_async_copy(second_a.at[j], w2.at[j, pl.ds(0, half)], sems.at[1, j]),
            pltpu.make_async_copy(second_b.at[j], w2.at[j, pl.ds(half, half)], sems.at[2, j]),
        )

    @pl.when(active[0] == 1)
    def _():
        for j in range(4):
            pltpu.make_async_copy(first.at[j], w1.at[j], sems.at[0, j]).start()
            for copy in seconds(j):
                copy.start()
        stream = arrived[...].astype(F32)
        hat, _ = standardize(stream)
        normed_ref[...] = (hat * (1.0 + modes[1:2, :]) + modes[0:1, :]).astype(BF)
        branch_ref[...] = jnp.zeros_like(branch_ref)

        def shard(j, carry):
            pltpu.make_async_copy(first.at[j], w1.at[j], sems.at[0, j]).wait()
            hidden = dot(normed_ref[...], w1[j])
            square = hidden * hidden
            bend = jnp.tanh(GELU_C * hidden * (1.0 + GELU_A * square))
            act = (0.5 * hidden * (1.0 + bend)).astype(BF)
            if keep:
                act_out[j] = act
                slope = 0.5 * (1.0 + bend) + 0.5 * hidden * (1.0 - bend * bend) * GELU_C * (
                    1.0 + 3.0 * GELU_A * square
                )
                slope_out[j] = slope.astype(BF)
            for copy in seconds(j):
                copy.wait()
            branch_ref[...] += dot(act, w2[j])
            return carry

        lax.fori_loop(0, 4, shard, 0)
        result[...] = (arrived[...].astype(F32) + modes[2:3, :] * branch_ref[...]).astype(BF)
        if keep:
            normed_out[...] = normed_ref[...]
            branch_out[...] = branch_ref[...]


def mlp_scratch(first, rows, width):
    return [
        pltpu.VMEM(first.shape, BF),
        pltpu.VMEM((4, width, width), BF),
        pltpu.VMEM((rows, width), BF),
        pltpu.VMEM((rows, width), F32),
        pltpu.SemaphoreType.DMA((3, 4)),
    ]


def mlp_forward(active, arrived, modes, first, second_a, second_b, keep):
    rows, width = arrived.shape
    shape = jax.ShapeDtypeStruct
    outs = [shape((rows, width), BF)]
    if keep:
        outs += [
            shape((rows, width), BF),
            shape((4, rows, width), BF),
            shape((4, rows, width), BF),
            shape((rows, width), F32),
        ]
    return pl.pallas_call(
        functools.partial(mlp_forward_kernel, keep),
        out_shape=outs,
        in_specs=[smem(), vmem(), vmem(), anywhere(), anywhere(), anywhere()],
        out_specs=[vmem()] * len(outs),
        scratch_shapes=mlp_scratch(first, rows, width),
        compiler_params=params(),
        cost_estimate=cost(2_400_000_000, 10_000_000),
    )(active, arrived, modes, first, second_a, second_b)


def mlp_back_kernel(*refs):
    active, arrived, grad, branch, slope, modes, first, second_a, second_b = refs[:9]
    in_grad, mode_grad, hidden_grad_out, branch_grad_out = refs[9:13]
    w1, w2, bg_ref, ng_ref, sems = refs[13:]
    half = second_a.shape[1]

    def seconds(j):
        return (
            pltpu.make_async_copy(second_a.at[j], w2.at[j, pl.ds(0, half)], sems.at[1, j]),
            pltpu.make_async_copy(second_b.at[j], w2.at[j, pl.ds(half, half)], sems.at[2, j]),
        )

    @pl.when(active[0] == 1)
    def _():
        for j in range(4):
            for copy in seconds(j):
                copy.start()
            pltpu.make_async_copy(first.at[j], w1.at[j], sems.at[0, j]).start()
        g = grad[...].astype(F32)
        mode_grad[2:3, :] = jnp.sum(g * branch[...], axis=0, keepdims=True)
        bg_ref[...] = (modes[2:3, :] * g).astype(BF)
        branch_grad_out[...] = bg_ref[...]
        ng_ref[...] = jnp.zeros_like(ng_ref)

        def shard(j, carry):
            for copy in seconds(j):
                copy.wait()
            act_grad = dot_nt(bg_ref[...], w2[j])
            hidden_grad = (act_grad * slope[j].astype(F32)).astype(BF)
            hidden_grad_out[j] = hidden_grad
            pltpu.make_async_copy(first.at[j], w1.at[j], sems.at[0, j]).wait()
            ng_ref[...] += dot_nt(hidden_grad, w1[j])
            return carry

        lax.fori_loop(0, 4, shard, 0)
        total, shift_grad, scale_grad = norm_back(
            ng_ref[...], arrived[...].astype(F32), modes[1:2, :], grad[...].astype(F32)
        )
        in_grad[...] = total.astype(BF)
        mode_grad[0:1, :] = shift_grad
        mode_grad[1:2, :] = scale_grad


def mlp_back(active, arrived, grad, branch, slope, modes, first, second_a, second_b):
    rows, width = grad.shape
    shape = jax.ShapeDtypeStruct
    outs = [
        shape((rows, width), BF),
        shape((3, width), F32),
        shape((4, rows, width), BF),
        shape((rows, width), BF),
    ]
    return pl.pallas_call(
        mlp_back_kernel,
        out_shape=outs,
        in_specs=[smem()] + [vmem()] * 5 + [anywhere()] * 3,
        out_specs=[vmem()] * len(outs),
        scratch_shapes=mlp_scratch(first, rows, width),
        compiler_params=params(),
        cost_estimate=cost(2_400_000_000, 12_000_000),
    )(active, arrived, grad, branch, slope, modes, first, second_a, second_b)


def gather_rows(parts, target, sems, row):
    copies = []
    for i, part in enumerate(parts):
        rows = part.shape[0]
        copies.append(
            pltpu.make_async_copy(part, target.at[pl.ds(i * rows, rows)], sems.at[row, i])
        )
    return copies


def attention_grads_kernel(*refs):
    active = refs[0]
    normed, bg, pack = refs[1:5], refs[5:9], refs[9:13]
    out = refs[13]
    n_ref, b_ref, p_ref, sems = refs[14:]

    @pl.when(active[0] == 1)
    def _():
        pack_parts = [pack[0].at[0]] + list(pack[1:])
        copies = (
            gather_rows(normed, n_ref, sems, 0)
            + gather_rows(pack_parts, p_ref, sems, 1)
            + gather_rows(bg, b_ref, sems, 2)
        )
        for copy in copies:
            copy.start()
        for copy in copies:
            copy.wait()
        low = lax.broadcasted_iota(jnp.int32, (256, 256), 1) < HEAD_DIM

        def chunk(c, carry):
            rows = pl.ds(c * 256, 256)
            left = n_ref[:, rows]
            out[rows, :512] = dot_tn(left, p_ref[:, :512]).astype(BF)
            inward = dot_tn(left, p_ref[:, 512:])
            outward = dot_tn(b_ref[:, rows], p_ref[:, 512:])
            out[rows, 512:] = jnp.where(low, inward, outward).astype(BF)
            return carry

        for c in range(out.shape[0] // 256):
            chunk(c, 0)


def mlp_grads_kernel(*refs):
    active = refs[0]
    normed, bg, hidden, act = refs[1:5], refs[5:9], refs[9:13], refs[13:17]
    out_first, out_second = refs[17:19]
    n_ref, b_ref, h_ref, a_ref, sems = refs[19:]

    @pl.when(active[0] == 1)
    def _():
        copies = (
            gather_rows(normed, n_ref, sems, 0)
            + gather_rows([hidden[0].at[0]] + list(hidden[1:]), h_ref, sems, 1)
            + gather_rows(bg, b_ref, sems, 2)
            + gather_rows([act[0].at[0]] + list(act[1:]), a_ref, sems, 3)
        )
        for copy in copies:
            copy.start()
        for copy in copies:
            copy.wait()
        for c in range(out_first.shape[0] // 256):
            rows = pl.ds(c * 256, 256)
            out_first[rows, :] = dot_tn(n_ref[:, rows], h_ref[...]).astype(BF)
            out_second[rows, :] = dot_tn(a_ref[:, rows], b_ref[...]).astype(BF)


def weight_grads(kernel, active, groups, count):
    rows, width = groups[0][0].shape[-2:]
    operands = [active]
    for group in groups:
        operands += list(group)
    return pl.pallas_call(
        kernel,
        out_shape=[jax.ShapeDtypeStruct((width, width), BF)] * count,
        in_specs=[smem()] + [anywhere()] * (len(operands) - 1),
        out_specs=[vmem()] * count,
        scratch_shapes=[pltpu.VMEM((4 * rows, width), BF)] * len(groups)
        + [pltpu.SemaphoreType.DMA((len(groups), 4))],
        compiler_params=params(),
        cost_estimate=cost(1_300_000_000 * count, 8_000_000),
    )(*operands)


def tensor_back(i, n):
    return (i - 1) % n


def tensor_on(i, n):
    return (i + 1) % n


def tensor_far(i, n):
    return i ^ 2


def gather_weight(local, part, dp_part):
    rows, columns = local.shape
    half = rows // 2
    mine = lax.dynamic_slice_in_dim(local, dp_part % 2 * half, half, 0)
    before = cyclic(mine, "tensor", 1)
    after = cyclic(mine, "tensor", -1)
    far = swap(jnp.where(part % 2 == 0, before, after), "tensor", 1)
    total = jnp.zeros((4, rows, columns), local.dtype)
    total = total.at[0].set(local)
    here = dp_part % 2 * half
    there = half - here
    for slot, piece in enumerate((before, after, far)):
        other = swap(piece, "dp", 1)
        total = lax.dynamic_update_slice(total, piece[None], (slot + 1, here, 0))
        total = lax.dynamic_update_slice(total, other[None], (slot + 1, there, 0))
    return total


def exchange_part(value, part):
    block = value.shape[0] // 4

    def rows_for(target):
        return lax.dynamic_slice_in_dim(value, target % 4 * block, block, 0)

    own = rows_for(part)
    from_after = cyclic(rows_for(part + 3), "tensor", -1)
    from_before = cyclic(rows_for(part + 1), "tensor", 1)
    from_far = swap(rows_for(part + 2), "tensor", 2)
    in_turn = jnp.stack([own, from_after, from_far, from_before])
    twice = jnp.concatenate([in_turn, in_turn], axis=0)
    return lax.dynamic_slice_in_dim(twice, (4 - part) % 4, 4, 0)


def dp_gather(value):
    index = lax.axis_index("dp")
    size = lax.axis_size("dp")
    bit = 1
    while bit < size:
        other = swap(value, "dp", bit)
        lower = index // bit % 2 == 0
        value = jnp.where(
            lower, jnp.concatenate([value, other]), jnp.concatenate([other, value])
        )
        bit *= 2
    return value


def dp_total(value, which):
    size = lax.axis_size("dp")
    total = value
    bit = 1
    while bit < size:
        low = total.astype(BF)
        other = within(low, "dp", which, lambda i, n: i ^ bit)
        total = low.astype(F32) + other.astype(F32)
        bit *= 2
    return total.astype(F32)


def body(clean, noise, times, flags, cotangent, w_main, w_half, w_mod):
    section = lax.axis_index("section")
    part = lax.axis_index("tensor")
    dp_part = lax.axis_index("dp")
    local_seqs, length, width = clean.shape
    columns = w_main.shape[3]
    halfdim = HEAD_DIM // 2

    main_local = w_main[0].reshape(width, 4 * columns)
    weights = gather_weight(main_local, part, dp_part)
    second_own = gather_weight(w_half[0], part, dp_part)
    second_other = swap(second_own, "section", 1)

    def mine(values):
        return lax.dynamic_index_in_dim(values, part, 0, keepdims=False)

    theta = math.pi / 2 * (mine(times).astype(F32) + 1.0) / (TSTEPS + 1.0)
    noisy = jnp.cos(theta) * mine(clean).astype(F32) + jnp.sin(theta) * mine(noise).astype(F32)
    target = mine(cotangent)
    flag = mine(flags).astype(jnp.int32).reshape(1)

    halfwidth = width // 2
    freqs = jnp.exp(-math.log(10000.0) * jnp.arange(halfwidth, dtype=F32) / halfwidth)
    angles = times.astype(F32)[:, None] * freqs[None, :]
    temb = jnp.concatenate([jnp.sin(angles), jnp.cos(angles)], axis=1)
    mode_part = jnp.einsum("nd,dpc->npc", temb, w_mod[0].astype(F32), precision=HIGHEST)

    def for_part(target_part):
        return lax.dynamic_index_in_dim(mode_part, target_part % 4, 0, keepdims=False)

    mode_turn = jnp.stack(
        [
            for_part(part),
            cyclic(for_part(part + 3), "tensor", -1),
            swap(for_part(part + 2), "tensor", 2),
            cyclic(for_part(part + 1), "tensor", 1),
        ],
        axis=1,
    )
    mode_twice = jnp.concatenate([mode_turn, mode_turn], axis=1)
    modes = lax.dynamic_slice_in_dim(mode_twice, (4 - part) % 4, 4, 1).reshape(3, width)

    inverse = jnp.exp(-math.log(10000.0) * 2.0 * jnp.arange(halfdim, dtype=F32) / HEAD_DIM)
    turn = jnp.arange(length, dtype=F32)[:, None] * inverse[None, :]
    cosine = jnp.tile(jnp.cos(turn), (1, 4))
    sine = jnp.tile(jnp.concatenate([-jnp.sin(turn), jnp.sin(turn)], axis=1), (1, 2))

    active = [(section == s).astype(jnp.int32).reshape(1) for s in range(4)]

    def attend(s, base, arrived, keep):
        return attention_forward(
            active[s], flag, base, arrived, modes, cosine, sine, weights, keep
        )

    def feed(s, arrived, keep):
        return mlp_forward(active[s], arrived, modes, weights, second_other, second_own, keep)

    value = attend(0, noisy, None, False)[0]
    value = feed(1, section_hop(value, 0, 1), False)[0]
    value = attend(2, None, section_hop(value, 1, 1), False)[0]
    value = feed(3, section_hop(value, 2, 1), False)[0]
    guess = cyclic(value, "section", 1)

    kept_0 = attend(0, noisy, guess, True)
    stream_1 = section_hop(kept_0[0], 0, 1)
    kept_1 = feed(1, stream_1, True)
    stream_2 = section_hop(kept_1[0], 1, 1)
    kept_2 = attend(2, None, stream_2, True)
    stream_3 = section_hop(kept_2[0], 2, 1)
    kept_3 = feed(3, stream_3, True)

    def feed_back(s, stream, grad, kept):
        return mlp_back(
            active[s], stream, grad, kept[4], kept[3], modes, weights, second_other, second_own
        )

    def attend_back(s, base, stream, grad, kept):
        return attention_back(
            active[s], flag, base, stream, grad, kept[4], kept[2], kept[3], modes,
            cosine, sine, weights,
        )

    back_3 = feed_back(3, stream_3, target, kept_3)
    grad_2 = section_hop(back_3[0], 3, -1)
    back_2 = attend_back(2, None, stream_2, grad_2, kept_2)
    grad_1 = section_hop(back_2[0], 2, -1)
    back_1 = feed_back(1, stream_1, grad_1, kept_1)
    grad_0 = section_hop(back_1[0], 1, -1)
    back_0 = attend_back(0, noisy, guess, grad_0, kept_0)

    def everywhere(value, s):
        return (
            value,
            within(value, "tensor", (s,), tensor_on),
            within(value, "tensor", (s,), tensor_back),
            within(value, "tensor", (s,), tensor_far),
        )

    def blocks(values, s):
        return (
            values,
            within(values[2], "tensor", (s,), tensor_on),
            within(values[1], "tensor", (s,), tensor_back),
            within(values[3], "tensor", (s,), tensor_far),
        )

    def mlp_weight_grads(s, kept, back):
        groups = (
            everywhere(kept[1], s),
            everywhere(back[3], s),
            blocks(back[2], s),
            blocks(kept[2], s),
        )
        return weight_grads(mlp_grads_kernel, active[s], groups, 2)

    def attention_weight_grads(s, kept, back):
        groups = (everywhere(kept[1], s), everywhere(back[3], s), blocks(back[2], s))
        return weight_grads(attention_grads_kernel, active[s], groups, 1)

    main_3, second_3 = mlp_weight_grads(3, kept_3, back_3)
    (main_2,) = attention_weight_grads(2, kept_2, back_2)
    main_1, second_1 = mlp_weight_grads(1, kept_1, back_1)
    (main_0,) = attention_weight_grads(0, kept_0, back_0)

    def pick(values):
        chosen = values[0]
        for s in range(1, 4):
            chosen = jnp.where(section == s, values[s], chosen)
        return chosen

    main_total = pick([dp_total(v, (s,)) for s, v in enumerate((main_0, main_1, main_2, main_3))])
    second_total = jnp.where(
        section == 1, dp_total(second_1, (1,)), dp_total(second_3, (3,))
    )
    halfway = 2 * columns
    returned = swap(second_total[:halfway].astype(BF), "section", 1).astype(F32)
    half_total = jnp.where(section % 2 == 0, returned, second_total[halfway:])

    mode_grad = pick([back_0[1], back_1[1], back_2[1], back_3[1]])

    def grad_for(target_part):
        return lax.dynamic_slice_in_dim(mode_grad, target_part % 4 * columns, columns, 1)

    grad_turn = jnp.stack(
        [
            grad_for(part),
            cyclic(grad_for(part + 3), "tensor", -1),
            swap(grad_for(part + 2), "tensor", 2),
            cyclic(grad_for(part + 1), "tensor", 1),
        ]
    )
    temb_twice = jnp.concatenate([temb, temb], axis=0)
    temb_turn = lax.dynamic_slice_in_dim(temb_twice, part, 4, 0)
    grad_all = dp_gather(grad_turn)
    temb_all = dp_gather(temb_turn)
    mode_total = jnp.einsum("nd,npc->dpc", temb_all, grad_all, precision=HIGHEST)

    outputs = exchange_part(pick([kept_0[0], kept_1[0], kept_2[0], kept_3[0]]), part).astype(F32)
    in_grads = exchange_part(pick([back_0[0], back_1[0], back_2[0], back_3[0]]), part).astype(F32)
    return (
        outputs[None],
        in_grads[None],
        main_total.reshape(1, width, 4, columns),
        half_total[None],
        mode_total[None],
    )


def solution(mesh):
    in_specs = (
        P("dp", None, None),
        P("dp", None, None),
        P("dp"),
        P("dp"),
        P("dp", None, None),
        P("section", None, None, "tensor"),
        P("section", "tensor", None),
        P("section", None, None, "tensor"),
    )
    out_specs = (
        P("section", "dp", "tensor", None),
        P("section", "dp", "tensor", None),
        P("section", None, None, "tensor"),
        P("section", "tensor", None),
        P("section", None, None, "tensor"),
    )
    return jax.shard_map(body, mesh=mesh, in_specs=in_specs, out_specs=out_specs, check_vma=False)
```

```python
import functools
import math

import jax
import jax.numpy as jnp
from jax import lax
from jax.experimental import pallas as pl
from jax.experimental.pallas import tpu as pltpu
from jax.sharding import PartitionSpec as P

HEAD_DIM = 64
TSTEPS = 1000
EPSILON = 1e-05
HIGHEST = lax.Precision.HIGHEST
BF = jnp.bfloat16
F32 = jnp.float32
VMEM_BYTES = 32 * 1024 * 1024
GELU_C = math.sqrt(2.0 / math.pi)
GELU_A = 0.044715


def cyclic(value, axis, by):
    size = lax.axis_size(axis)
    return lax.ppermute(value, axis, [(i, (i + by) % size) for i in range(size)])


def swap(value, axis, bit):
    size = lax.axis_size(axis)
    return lax.ppermute(value, axis, [(i, i ^ bit) for i in range(size)])


def within(value, axis, which, route):
    size = lax.axis_size(axis)
    pairs = [(s * size + i, s * size + route(i, size)) for s in which for i in range(size)]
    return lax.ppermute(value, ("section", axis), pairs)


def section_hop(value, source, by):
    target = source + by
    if source // 2 == target // 2:
        return swap(value, "section", 1)
    return cyclic(value, "section", by)


def dot(left, right):
    return lax.dot_general(left, right, (((1,), (0,)), ((), ())), preferred_element_type=F32)


def dot_nt(left, right):
    return lax.dot_general(left, right, (((1,), (1,)), ((), ())), preferred_element_type=F32)


def dot_tn(left, right):
    return lax.dot_general(left, right, (((0,), (0,)), ((), ())), preferred_element_type=F32)


def standardize(stream):
    centred = stream - jnp.mean(stream, axis=-1, keepdims=True)
    variance = jnp.mean(centred * centred, axis=-1, keepdims=True)
    inverse = lax.rsqrt(variance + EPSILON)
    return centred * inverse, inverse


def swap_halves(block, first):
    return jnp.where(first, pltpu.roll(block, 96, 1), pltpu.roll(block, 32, 1))


def first_mask(rows):
    lane = lax.broadcasted_iota(jnp.int32, (rows, 128), 1)
    return (lane % HEAD_DIM) < HEAD_DIM // 2


def norm_back(normed_grad, stream, scale, grad):
    hat, inverse = standardize(stream)
    shift_grad = jnp.sum(normed_grad, axis=0, keepdims=True)
    scale_grad = jnp.sum(normed_grad * hat, axis=0, keepdims=True)
    hat_grad = normed_grad * (1.0 + scale)
    mean_one = jnp.mean(hat_grad, axis=-1, keepdims=True)
    mean_two = jnp.mean(hat_grad * hat, axis=-1, keepdims=True)
    in_grad = grad + inverse * (hat_grad - mean_one - hat * mean_two)
    return in_grad, shift_grad, scale_grad


def weight_copies(pieces, target, row, info, sems, slot):
    own = pieces[0]
    rows = own.shape[0]
    half = rows // 2
    if slot == 0:
        return [pltpu.make_async_copy(own, target.at[0, pl.ds(row, rows)], sems.at[0, 0])]
    here = pl.multiple_of(row + info[2] * half, half)
    there = pl.multiple_of(row + (1 - info[2]) * half, half)
    near, across = pieces[2 * slot - 1], pieces[2 * slot]
    return [
        pltpu.make_async_copy(near, target.at[slot, pl.ds(here, half)], sems.at[slot, 0]),
        pltpu.make_async_copy(across, target.at[slot, pl.ds(there, half)], sems.at[slot, 1]),
    ]


def start_all(copies):
    for copy in copies:
        copy.start()


def wait_all(copies):
    for copy in copies:
        copy.wait()


def slot_rows(info, slot, block):
    return pl.ds(pl.multiple_of(slot_part(info, slot) * block, block), block)


def send_halves(send, source, target, at):
    for k in range(2):
        send(source.at[k], target.at[at + k])


def put_halves(ref, value):
    half = ref.shape[2]
    ref[0] = value[:, :half]
    ref[1] = value[:, half:]


MODE_ROWS = 16


def put_mode_grads(ref, values):
    joined = jnp.concatenate(values, axis=0)
    high = joined.astype(BF)
    rest = (joined - high.astype(F32)).astype(BF)
    filler = jnp.zeros((MODE_ROWS - 6, joined.shape[1]), BF)
    both = jnp.concatenate([high, rest, filler], axis=0)
    columns = both.shape[1] // 4
    ref[...] = jnp.zeros_like(ref)
    for part in range(4):
        ref[part, :, :columns] = both[:, part * columns : (part + 1) * columns]


def slot_part(info, slot):
    return lax.rem(info[1] + (0, 3, 1, 2)[slot], 4)


def vmem():
    return pl.BlockSpec(memory_space=pltpu.VMEM)


def smem():
    return pl.BlockSpec(memory_space=pltpu.SMEM)


def hbm():
    return pl.BlockSpec(memory_space=pltpu.HBM)


def anywhere():
    return pl.BlockSpec(memory_space=pl.ANY)


def params():
    return pltpu.CompilerParams(vmem_limit_bytes=VMEM_BYTES)


def cost(flops, nbytes):
    return pl.CostEstimate(flops=flops, bytes_accessed=nbytes, transcendentals=0)


def call(kernel, ins, outs, scratch, aliases, estimate):
    def placed(value, spec):
        if spec.memory_space is pltpu.HBM:
            return pltpu.with_memory_space_constraint(value, pltpu.HBM)
        return value

    def result(value, spec):
        if spec.memory_space is pltpu.HBM:
            return pltpu.HBM(value.shape, value.dtype)
        return value

    return pl.pallas_call(
        kernel,
        out_shape=[result(*pair) for pair in outs],
        in_specs=[spec for _, spec in ins],
        out_specs=[spec for _, spec in outs],
        scratch_shapes=scratch,
        input_output_aliases=aliases,
        compiler_params=params(),
        cost_estimate=estimate,
    )(*[placed(*pair) for pair in ins])


def shape(dims, dtype):
    return jax.ShapeDtypeStruct(dims, dtype)


DMA = pltpu.SemaphoreType.DMA


def attention_forward_kernel(s, has_base, has_arrived, keep, *refs):
    refs = list(refs)
    info = refs.pop(0)
    base = refs.pop(0) if has_base else None
    arrived = refs.pop(0) if has_arrived else None
    modes, cosine, sine = refs[:3]
    pieces = refs[3:10]
    refs = refs[10:]
    result = refs.pop(0)
    if keep:
        heads_out, lse_out, attended_out, branch_out, stream_out = refs[:5]
        normed_out, result_out, message = refs[5:8]
        refs = refs[8:]
    w, normed, branch, wsems = refs[:4]
    if keep:
        stream_ref, heads, lse, attended_ref, halves, osems = refs[4:]

    def load_stream():
        if not has_base:
            return arrived[...].astype(F32)
        if not has_arrived:
            return base[...]
        return base[...] + info[3].astype(F32) * arrived[...].astype(F32)

    @pl.when(info[0] == s)
    def _():
        for j in range(4):
            start_all(weight_copies(pieces, w, 0, info, wsems, j))
        outs = []

        def send(source, target):
            copy = pltpu.make_async_copy(source, target, osems.at[len(outs)])
            copy.start()
            outs.append(copy)

        stream = load_stream()
        hat, _ = standardize(stream)
        normed[...] = (hat * (1.0 + modes[1:2, :]) + modes[0:1, :]).astype(BF)
        rows = normed.shape[0]
        if keep:
            stream_ref[...] = stream
            send(stream_ref, stream_out)
            put_halves(halves, normed[...])
            send_halves(send, halves, normed_out, 0)
            send_halves(send, halves, message, 0)
        first = first_mask(rows)
        low = lax.broadcasted_iota(jnp.int32, (rows, 128), 1) < HEAD_DIM
        for j in range(4):
            wait_all(weight_copies(pieces, w, 0, info, wsems, j))
            raw = dot(normed[...], w[j, :, :576])
            turned = []
            for unit in range(3):
                block = raw[:, unit * 128 : (unit + 1) * 128]
                block = block * cosine[...] + swap_halves(block, first) * sine[...]
                if unit == 0:
                    block = block * 0.125
                if unit == 1:
                    block = jnp.where(low, block * 0.125, block)
                turned.append(block)
            joined = jnp.concatenate(turned + [raw[:, 384:576]], axis=1).astype(BF)
            if keep:
                heads[j] = joined
                send(heads.at[j], heads_out.at[j])
            pieces_t = [jnp.zeros((HEAD_DIM, rows), BF)]
            for head in range(3):
                q = joined[:, head * 64 : head * 64 + 64]
                k = joined[:, 192 + head * 64 : 192 + head * 64 + 64]
                v = joined[:, 384 + head * 64 : 384 + head * 64 + 64]
                scores = dot_nt(k, q)
                top = jnp.max(scores, axis=0, keepdims=True)
                raised = jnp.exp(scores - top)
                total = jnp.sum(raised, axis=0, keepdims=True)
                if keep:
                    lse[3 * j + head : 3 * j + head + 1, :] = top + jnp.log(total)
                mixed = dot_tn(v, raised.astype(BF)) * (1.0 / total)
                pieces_t.append(mixed.astype(BF))
            attended = jnp.concatenate(pieces_t, axis=0).T
            if keep:
                attended_ref[j] = attended
                send(attended_ref.at[j], attended_out.at[j])
            part = dot_nt(attended, w[j, :, 512:768])
            branch[...] = part if j == 0 else branch[...] + part
        result[...] = (load_stream() + modes[2:3, :] * branch[...]).astype(BF)
        if keep:
            send(lse, lse_out)
            send(branch, branch_out)
            send(result, result_out)
            wait_all(outs)


def attention_forward(s, info, base, arrived, modes, cosine, sine, pieces, keep):
    width = modes.shape[1]
    rows = cosine.shape[0]
    ins = [(info, smem())]
    for value in (base, arrived):
        if value is not None:
            ins.append((value, vmem()))
    ins += [(modes, vmem()), (cosine, vmem()), (sine, vmem())]
    ins += [(piece, hbm()) for piece in pieces]
    outs = [(shape((rows, width), BF), vmem())]
    scratch = [
        pltpu.VMEM((4, width, width), BF),
        pltpu.VMEM((rows, width), BF),
        pltpu.VMEM((rows, width), F32),
        DMA((4, 2)),
    ]
    if keep:
        outs += [
            (shape((4, rows, 576), BF), hbm()),
            (shape((12, rows), F32), hbm()),
            (shape((4, rows, 256), BF), hbm()),
            (shape((rows, width), F32), hbm()),
            (shape((rows, width), F32), hbm()),
            (shape((2, rows, width // 2), BF), hbm()),
            (shape((rows, width), BF), hbm()),
            (shape((8, rows, width // 2), BF), hbm()),
        ]
        scratch += [
            pltpu.VMEM((rows, width), F32),
            pltpu.VMEM((4, rows, 576), BF),
            pltpu.VMEM((12, rows), F32),
            pltpu.VMEM((4, rows, 256), BF),
            pltpu.VMEM((2, rows, width // 2), BF),
            DMA((16,)),
        ]
    kernel = functools.partial(
        attention_forward_kernel, s, base is not None, arrived is not None, keep
    )
    return call(kernel, ins, outs, scratch, {}, cost(2_000_000_000, 6_000_000))


def attention_back_kernel(s, *refs):
    info, grad, modes, cosine, sine = refs[:5]
    heads_in, lse_in, attended_in, branch_in, stream_in = refs[5:10]
    pieces = refs[10:17]
    in_grad, mode_out, message, pack_out, bg_out, in_out = refs[18:24]
    w, heads, lse, attended_ref, branch, stream, bg, ng, halves, pack_ref = refs[24:34]
    mode_ref, wsems, isems, osems = refs[34:]

    @pl.when(info[0] == s)
    def _():
        loads = []
        for source, target in (
            (branch_in, branch),
            (lse_in, lse),
            (heads_in, heads),
            (attended_in, attended_ref),
            (stream_in, stream),
        ):
            copy = pltpu.make_async_copy(source, target, isems.at[len(loads)])
            loads.append(copy)
        start_all(loads[:3])
        for j in range(4):
            start_all(weight_copies(pieces, w, 0, info, wsems, j))
        start_all(loads[3:])
        outs = []

        def send(source, target):
            copy = pltpu.make_async_copy(source, target, osems.at[len(outs)])
            copy.start()
            outs.append(copy)

        g = grad[...].astype(F32)
        rows = g.shape[0]
        bg[...] = (modes[2:3, :] * g).astype(BF)
        put_halves(halves, bg[...])
        send_halves(send, halves, bg_out, 0)
        send_halves(send, halves, message, 2)
        first = first_mask(rows)
        wait_all(loads[:3])
        for j in range(4):
            wait_all(weight_copies(pieces, w, 0, info, wsems, j))
            joined = heads[j]
            att_grad = dot(bg[...], w[j, :, 512:768]).astype(BF)
            dq, dk, dv = [], [], []
            for head in range(3):
                q = joined[:, head * 64 : head * 64 + 64]
                k = joined[:, 192 + head * 64 : 192 + head * 64 + 64]
                v = joined[:, 384 + head * 64 : 384 + head * 64 + 64]
                da = att_grad[:, 64 + head * 64 : 128 + head * 64]
                row = 3 * j + head
                probs = jnp.exp(dot_nt(k, q) - lse[row : row + 1, :])
                prob_grad = dot_nt(v, da)
                inner = jnp.sum(prob_grad * probs, axis=0, keepdims=True)
                ds = (probs * (prob_grad - inner)).astype(BF)
                dv.append(dot(probs.astype(BF), da))
                dk.append(dot(ds, q))
                dq.append(dot_tn(k, ds))
            dq_all = (jnp.concatenate(dq, axis=0) * 0.125).T
            both = jnp.concatenate([dq_all] + dk, axis=1)
            turned = []
            for unit in range(3):
                block = both[:, unit * 128 : (unit + 1) * 128]
                turned.append(block * cosine[...] - swap_halves(block, first) * sine[...])
            raw = jnp.concatenate(turned + dv, axis=1).astype(BF)
            if j == 0:
                wait_all(loads[3:])
            pack_ref[j, 0] = raw[:, :384]
            pack_ref[j, 1] = jnp.concatenate([raw[:, 384:576], attended_ref[j, :, 64:256]], axis=1)
            send(pack_ref.at[j, info[2]], pack_out.at[j])
            send(pack_ref.at[j, 1 - info[2]], message.at[4 + j])
            part = dot_nt(raw, w[j, :, :576])
            ng[...] = part if j == 0 else ng[...] + part
        total, shift_grad, scale_grad = norm_back(
            ng[...], stream[...], modes[1:2, :], grad[...].astype(F32)
        )
        in_grad[...] = total.astype(BF)
        send(in_grad, in_out)
        gate_grad = jnp.sum(grad[...].astype(F32) * branch[...], axis=0, keepdims=True)
        put_mode_grads(mode_ref, (shift_grad, scale_grad, gate_grad))
        send(mode_ref, mode_out)
        wait_all(outs)


def attention_back(s, info, grad, modes, cosine, sine, kept, pieces):
    rows, width = grad.shape
    ins = [(info, smem()), (grad, vmem()), (modes, vmem()), (cosine, vmem()), (sine, vmem())]
    ins += [(value, hbm()) for value in kept[1:6]]
    ins += [(piece, hbm()) for piece in pieces]
    aliases = {len(ins): 2}
    ins += [(kept[8], hbm())]
    outs = [
        (shape((rows, width), BF), vmem()),
        (shape((4, MODE_ROWS, 256), BF), hbm()),
        (shape(kept[8].shape, BF), hbm()),
        (shape((4, rows, width // 2), BF), hbm()),
        (shape((2, rows, width // 2), BF), hbm()),
        (shape((rows, width), BF), hbm()),
    ]
    scratch = [
        pltpu.VMEM((4, width, width), BF),
        pltpu.VMEM((4, rows, 576), BF),
        pltpu.VMEM((12, rows), F32),
        pltpu.VMEM((4, rows, 256), BF),
        pltpu.VMEM((rows, width), F32),
        pltpu.VMEM((rows, width), F32),
        pltpu.VMEM((rows, width), BF),
        pltpu.VMEM((rows, width), F32),
        pltpu.VMEM((2, rows, width // 2), BF),
        pltpu.VMEM((4, 2, rows, width // 2), BF),
        pltpu.VMEM((4, MODE_ROWS, 256), BF),
        DMA((4, 2)),
        DMA((5,)),
        DMA((14,)),
    ]
    kernel = functools.partial(attention_back_kernel, s)
    return call(kernel, ins, outs, scratch, aliases, cost(3_000_000_000, 10_000_000))


def mlp_weight_copies(first, other, own, w1, w2, info, sems, j):
    half = other[0].shape[0]
    return (
        weight_copies(first, w1, 0, info, sems.at[0], j),
        weight_copies(other, w2, 0, info, sems.at[1], j)
        + weight_copies(own, w2, half, info, sems.at[2], j),
    )


def mlp_forward_kernel(s, keep, *refs):
    info, arrived, modes = refs[:3]
    first, other, own = refs[3:10], refs[10:17], refs[17:24]
    result = refs[24]
    refs = refs[25:]
    if keep:
        slope_out, branch_out, stream_out = refs[:3]
        refs = refs[3:]
    if keep == "packs":
        packs = refs[:4]
        refs = refs[4:]
    if keep == "message":
        act_out, normed_out, result_out, message = refs[:4]
        refs = refs[4:]
    w1, w2, normed, branch, wsems = refs[:5]
    if keep:
        act_ref, slope_ref, halves, osems = refs[5:]

    @pl.when(info[0] == s)
    def _():
        weights = [
            mlp_weight_copies(first, other, own, w1, w2, info, wsems, j) for j in range(4)
        ]
        for one, two in weights:
            start_all(one)
            start_all(two)
        outs = []

        def send(source, target):
            copy = pltpu.make_async_copy(source, target, osems.at[len(outs)])
            copy.start()
            outs.append(copy)

        hat, _ = standardize(arrived[...].astype(F32))
        normed[...] = (hat * (1.0 + modes[1:2, :]) + modes[0:1, :]).astype(BF)
        rows = normed.shape[0]
        if keep:
            send(arrived, stream_out)
        if keep == "packs":
            for pack in packs:
                send(normed, pack.at[pl.ds(rows, rows)])
        if keep == "message":
            put_halves(halves, normed[...])
            send_halves(send, halves, normed_out, 0)
            send_halves(send, halves, message, 0)
        for j in range(4):
            wait_all(weights[j][0])
            hidden = dot(normed[...], w1[j])
            square = hidden * hidden
            bend = jnp.tanh(GELU_C * hidden * (1.0 + GELU_A * square))
            act = (0.5 * hidden * (1.0 + bend)).astype(BF)
            if keep:
                slope = 0.5 * (1.0 + bend) + (0.5 * GELU_C) * hidden * (1.0 - bend * bend) * (
                    1.0 + (3.0 * GELU_A) * square
                )
                slope_ref[j] = slope.astype(BF)
                send(slope_ref.at[j], slope_out.at[j])
            if keep == "packs":
                act_ref[j] = act
                send(act_ref.at[j], packs[j].at[pl.ds(0, rows)])
            if keep == "message":
                put_halves(act_ref.at[j], act)
                send(act_ref.at[j, info[2]], act_out.at[j])
                send(act_ref.at[j, 1 - info[2]], message.at[8 + j])
            wait_all(weights[j][1])
            part = dot(act, w2[j])
            branch[...] = part if j == 0 else branch[...] + part
        result[...] = (arrived[...].astype(F32) + modes[2:3, :] * branch[...]).astype(BF)
        if keep:
            send(branch, branch_out)
            block = rows // 4
            if keep == "packs":
                for slot, pack in enumerate(packs):
                    send(result.at[slot_rows(info, slot, block)], pack.at[pl.ds(2 * rows, block)])
            else:
                send(result, result_out)
            wait_all(outs)


def mlp_forward(s, info, arrived, modes, first, other, own, keep):
    rows, width = arrived.shape
    ins = [(info, smem()), (arrived, vmem()), (modes, vmem())]
    ins += [(piece, hbm()) for piece in first + other + own]
    outs = [(shape((rows, width), BF), vmem())]
    scratch = [
        pltpu.VMEM((4, width, width), BF),
        pltpu.VMEM((4, width, width), BF),
        pltpu.VMEM((rows, width), BF),
        pltpu.VMEM((rows, width), F32),
        DMA((3, 4, 2)),
    ]
    if keep:
        outs += [
            (shape((4, rows, width), BF), hbm()),
            (shape((rows, width), F32), hbm()),
            (shape((rows, width), BF), hbm()),
        ]
        if keep == "packs":
            outs += [(shape((2 * rows + rows // 4, width), BF), hbm())] * 4
        else:
            outs += [
                (shape((4, rows, width // 2), BF), hbm()),
                (shape((2, rows, width // 2), BF), hbm()),
                (shape((rows, width), BF), hbm()),
                (shape((12, rows, width // 2), BF), hbm()),
            ]
        wide = (4, rows, width) if keep == "packs" else (4, 2, rows, width // 2)
        scratch += [
            pltpu.VMEM(wide, BF),
            pltpu.VMEM((4, rows, width), BF),
            pltpu.VMEM((2, rows, width // 2), BF),
            DMA((20,)),
        ]
    kernel = functools.partial(mlp_forward_kernel, s, keep)
    return call(kernel, ins, outs, scratch, {}, cost(2_400_000_000, 10_000_000))


def mlp_back_kernel(s, keep, *refs):
    info, grad, modes, slope_in, branch_in, stream_in = refs[:6]
    first, other, own = refs[6:13], refs[13:20], refs[20:27]
    if keep == "packs":
        in_grad, mode_out = refs[27:29]
        packs = refs[29:33]
        refs = refs[33:]
    else:
        in_grad, mode_out, message, hidden_out, bg_out, in_out = refs[28:34]
        refs = refs[34:]
    w1, w2, slope, branch, stream, bg, ng, halves, hidden_ref = refs[:9]
    mode_ref, wsems, isems, osems = refs[9:]

    @pl.when(info[0] == s)
    def _():
        weights = [
            mlp_weight_copies(first, other, own, w1, w2, info, wsems, j) for j in range(4)
        ]
        loads = [
            pltpu.make_async_copy(source, target, isems.at[i])
            for i, (source, target) in enumerate(
                ((slope_in, slope), (branch_in, branch), (stream_in, stream))
            )
        ]
        for j, (one, two) in enumerate(weights):
            start_all(two)
            if j == 0:
                loads[0].start()
            start_all(one)
        start_all(loads[1:])
        outs = []

        def send(source, target):
            copy = pltpu.make_async_copy(source, target, osems.at[len(outs)])
            copy.start()
            outs.append(copy)

        g = grad[...].astype(F32)
        rows = g.shape[0]
        bg[...] = (modes[2:3, :] * g).astype(BF)
        if keep == "packs":
            for pack in packs:
                send(bg, pack.at[pl.ds(rows, rows)])
        else:
            put_halves(halves, bg[...])
            send_halves(send, halves, bg_out, 0)
            send_halves(send, halves, message, 2)
        for j in range(4):
            wait_all(weights[j][1])
            act_grad = dot_nt(bg[...], w2[j])
            if j == 0:
                loads[0].wait()
            hidden_grad = (act_grad * slope[j].astype(F32)).astype(BF)
            if keep == "packs":
                hidden_ref[j] = hidden_grad
                send(hidden_ref.at[j], packs[j].at[pl.ds(0, rows)])
            else:
                put_halves(hidden_ref.at[j], hidden_grad)
                send(hidden_ref.at[j, info[2]], hidden_out.at[j])
                send(hidden_ref.at[j, 1 - info[2]], message.at[4 + j])
            wait_all(weights[j][0])
            part = dot_nt(hidden_grad, w1[j])
            ng[...] = part if j == 0 else ng[...] + part
        wait_all(loads[1:])
        total, shift_grad, scale_grad = norm_back(
            ng[...], stream[...].astype(F32), modes[1:2, :], grad[...].astype(F32)
        )
        in_grad[...] = total.astype(BF)
        block = rows // 4
        if keep == "packs":
            for slot, pack in enumerate(packs):
                send(in_grad.at[slot_rows(info, slot, block)], pack.at[pl.ds(2 * rows, block)])
        else:
            send(in_grad, in_out)
        gate_grad = jnp.sum(grad[...].astype(F32) * branch[...], axis=0, keepdims=True)
        put_mode_grads(mode_ref, (shift_grad, scale_grad, gate_grad))
        send(mode_ref, mode_out)
        if keep == "packs":
            for slot, pack in enumerate(packs):
                send(
                    mode_ref.at[slot_part(info, slot)],
                    pack.at[pl.ds(2 * rows + block, MODE_ROWS), pl.ds(0, 256)],
                )
        wait_all(outs)


def mlp_back(s, info, grad, modes, kept, first, other, own, keep):
    rows, width = grad.shape
    ins = [(info, smem()), (grad, vmem()), (modes, vmem())]
    ins += [(value, hbm()) for value in kept[1:4]]
    ins += [(piece, hbm()) for piece in first + other + own]
    outs = [
        (shape((rows, width), BF), vmem()),
        (shape((4, MODE_ROWS, 256), BF), hbm()),
    ]
    aliases = {}
    if keep == "packs":
        outs += [(shape((2 * rows + rows // 4 + MODE_ROWS, width), BF), hbm())] * 4
    else:
        aliases = {len(ins): 2}
        ins += [(kept[7], hbm())]
        outs += [
            (shape(kept[7].shape, BF), hbm()),
            (shape((4, rows, width // 2), BF), hbm()),
            (shape((2, rows, width // 2), BF), hbm()),
            (shape((rows, width), BF), hbm()),
        ]
    wide = (4, rows, width) if keep == "packs" else (4, 2, rows, width // 2)
    scratch = [
        pltpu.VMEM((4, width, width), BF),
        pltpu.VMEM((4, width, width), BF),
        pltpu.VMEM((4, rows, width), BF),
        pltpu.VMEM((rows, width), F32),
        pltpu.VMEM((rows, width), BF),
        pltpu.VMEM((rows, width), BF),
        pltpu.VMEM((rows, width), F32),
        pltpu.VMEM((2, rows, width // 2), BF),
        pltpu.VMEM(wide, BF),
        pltpu.VMEM((4, MODE_ROWS, 256), BF),
        DMA((3, 4, 2)),
        DMA((3,)),
        DMA((17,)),
    ]
    kernel = functools.partial(mlp_back_kernel, s, keep)
    return call(kernel, ins, outs, scratch, aliases, cost(2_400_000_000, 12_000_000))


def row_copies(group, row, target, sems):
    rows = target.shape[0] // 4
    return [
        pltpu.make_async_copy(
            pack.at[pl.ds(row, rows)], target.at[pl.ds(i * rows, rows)], sems.at[i]
        )
        for i, pack in enumerate(group)
    ]


def rows_to_slots(held, mode_ref, outs, at, info, sems):
    block = held.shape[1] // 4
    copies = []
    for slot, out in enumerate(outs):
        part = slot_rows(info, slot, block)
        for i in range(2):
            target = out.at[pl.ds(at + i * block, block)]
            copies.append(pltpu.make_async_copy(held.at[i, part], target, sems.at[i, slot]))
        target = out.at[pl.ds(at + 2 * block, MODE_ROWS), pl.ds(0, 256)]
        copies.append(
            pltpu.make_async_copy(mode_ref.at[slot_part(info, slot)], target, sems.at[2, slot])
        )
    return copies


def row_loads(result_in, in_in, mode_in, held, mode_ref, sems):
    return [
        pltpu.make_async_copy(result_in, held.at[0], sems.at[0]),
        pltpu.make_async_copy(in_in, held.at[1], sems.at[1]),
        pltpu.make_async_copy(mode_in, mode_ref, sems.at[2]),
    ]


def two_sequences(own, other, at, target, sems):
    count, rows = own.shape[:2]
    copies = []
    for j in range(count):
        copies += [
            pltpu.make_async_copy(own.at[j], target.at[j, pl.ds(0, rows)], sems.at[j, 0]),
            pltpu.make_async_copy(
                other.at[at + j], target.at[j, pl.ds(rows, rows)], sems.at[j, 1]
            ),
        ]
    return copies


def attention_sums_kernel(s, *refs):
    info, normed_in, bg_in, pack_in, other, result_in, in_in, mode_in = refs[:8]
    outs = refs[8:12]
    n_ref, b_ref, p_ref, held, row_ref, mode_ref = refs[12:18]
    nsems, bsems, psems, osems, lsems, rsems = refs[18:]
    half = held.shape[1]

    @pl.when(info[0] == s)
    def _():
        loads = row_loads(result_in, in_in, mode_in, row_ref, mode_ref, lsems)
        moves = rows_to_slots(row_ref, mode_ref, outs, half, info, rsems)
        copies = (
            two_sequences(normed_in, other, 0, n_ref, nsems)
            + two_sequences(bg_in, other, 2, b_ref, bsems)
            + two_sequences(pack_in, other, 4, p_ref, psems)
        )
        start_all(copies + loads)
        wait_all(copies + loads)
        start_all(moves)
        tokens = jnp.concatenate([n_ref[0], n_ref[1]], axis=1)
        branch = jnp.concatenate([b_ref[0], b_ref[1]], axis=1)
        for j in range(4):
            held[j] = dot_tn(p_ref[j], tokens).astype(BF)

            @pl.when(info[2] == 1)
            def _():
                outward = dot_tn(p_ref[j, :, 128:], branch)
                held[j, half // 2 :, :] = outward[half // 2 - 128 :].astype(BF)

            copy = pltpu.make_async_copy(
                held.at[j], outs[j].at[pl.ds(0, half)], osems.at[j]
            )
            copy.start()
            moves.append(copy)
        wait_all(moves)


def attention_sums(s, info, kept, back, other):
    rows, width = kept[7].shape
    half = width // 2
    ins = [(info, smem())]
    ins += [
        (value, hbm())
        for value in (kept[6], back[4], back[3], other, kept[7], back[5], back[1])
    ]
    outs = [(shape((half + rows // 2 + MODE_ROWS, width), BF), hbm())] * 4
    scratch = [
        pltpu.VMEM((2, 2 * rows, half), BF),
        pltpu.VMEM((2, 2 * rows, half), BF),
        pltpu.VMEM((4, 2 * rows, half), BF),
        pltpu.VMEM((4, half, width), BF),
        pltpu.VMEM((2, rows, width), BF),
        pltpu.VMEM((4, MODE_ROWS, 256), BF),
        DMA((2, 2)),
        DMA((2, 2)),
        DMA((4, 2)),
        DMA((4,)),
        DMA((3,)),
        DMA((3, 4)),
    ]
    kernel = functools.partial(attention_sums_kernel, s)
    return call(kernel, ins, outs, scratch, {}, cost(1_300_000_000, 8_000_000))


def mlp_sums_kernel(s, *refs):
    info, normed_in, bg_in, hidden_in, act_in, other, result_in, in_in, mode_in = refs[:9]
    outs = refs[9:13]
    n_ref, b_ref, h_ref, a_ref, held, row_ref, mode_ref = refs[13:20]
    nsems, bsems, hsems, asems, osems, lsems, rsems = refs[20:]
    half = held.shape[1] // 2

    @pl.when(info[0] == s)
    def _():
        loads = row_loads(result_in, in_in, mode_in, row_ref, mode_ref, lsems)
        moves = rows_to_slots(row_ref, mode_ref, outs, 2 * half, info, rsems)
        copies = (
            two_sequences(normed_in, other, 0, n_ref, nsems)
            + two_sequences(hidden_in, other, 4, h_ref, hsems)
            + two_sequences(bg_in, other, 2, b_ref, bsems)
            + two_sequences(act_in, other, 8, a_ref, asems)
        )
        start_all(copies + loads)
        wait_all(copies + loads)
        start_all(moves)
        tokens = jnp.concatenate([n_ref[0], n_ref[1]], axis=1)
        branch = jnp.concatenate([b_ref[0], b_ref[1]], axis=1)
        for j in range(4):
            held[j, :half] = dot_tn(h_ref[j], tokens).astype(BF)
            held[j, half:] = dot_tn(a_ref[j], branch).astype(BF)
            copy = pltpu.make_async_copy(
                held.at[j], outs[j].at[pl.ds(0, 2 * half)], osems.at[j]
            )
            copy.start()
            moves.append(copy)
        wait_all(moves)


def mlp_sums(s, info, kept, back, other):
    rows, width = kept[6].shape
    half = width // 2
    ins = [(info, smem())]
    ins += [
        (value, hbm())
        for value in (kept[5], back[4], back[3], kept[4], other, kept[6], back[5], back[1])
    ]
    outs = [(shape((width + rows // 2 + MODE_ROWS, width), BF), hbm())] * 4
    scratch = [
        pltpu.VMEM((2, 2 * rows, half), BF),
        pltpu.VMEM((2, 2 * rows, half), BF),
        pltpu.VMEM((4, 2 * rows, half), BF),
        pltpu.VMEM((4, 2 * rows, half), BF),
        pltpu.VMEM((4, width, width), BF),
        pltpu.VMEM((2, rows, width), BF),
        pltpu.VMEM((4, MODE_ROWS, 256), BF),
        DMA((2, 2)),
        DMA((2, 2)),
        DMA((4, 2)),
        DMA((4, 2)),
        DMA((4,)),
        DMA((3,)),
        DMA((3, 4)),
    ]
    kernel = functools.partial(mlp_sums_kernel, s)
    return call(kernel, ins, outs, scratch, {}, cost(2_600_000_000, 12_000_000))


def join_modes(held, columns):
    return jnp.concatenate([held[i, :, :columns] for i in range(4)], axis=1)


def total_kernel(s, at, *refs):
    info = refs[0]
    parts = refs[1:5]
    out, held, mode_ref, sems = refs[5:]
    rows = held.shape[1]

    @pl.when(info[0] == s)
    def _():
        copies = []
        for i, part in enumerate(parts):
            modes = part.at[pl.ds(at, MODE_ROWS), pl.ds(0, 256)]
            copies += [
                pltpu.make_async_copy(part.at[pl.ds(0, rows)], held.at[i], sems.at[0, i]),
                pltpu.make_async_copy(modes, mode_ref.at[i], sems.at[1, i]),
            ]
        start_all(copies)
        wait_all(copies)
        total = held[0].astype(F32) + held[1].astype(F32)
        out[:rows] = (total + held[2].astype(F32) + held[3].astype(F32)).astype(BF)
        out[rows:] = join_modes(mode_ref, out.shape[1] // 4)


def total_parts(s, info, group, rows):
    width = group[0].shape[1]
    at = group[0].shape[0] - MODE_ROWS
    ins = [(info, smem())] + [(value, hbm()) for value in group]
    outs = [(shape((rows + MODE_ROWS, width), BF), vmem())]
    scratch = [
        pltpu.VMEM((4, rows, width), BF),
        pltpu.VMEM((4, MODE_ROWS, 256), BF),
        DMA((2, 4)),
    ]
    kernel = functools.partial(total_kernel, s, at)
    return call(kernel, ins, outs, scratch, {}, cost(10_000_000, 5_000_000))[0]


def mlp_grads_kernel(s, *refs):
    info = refs[0]
    early, late = refs[1:5], refs[5:9]
    out = refs[9]
    a_ref, n_ref, h_ref, b_ref, mode_ref, sems = refs[10:]
    rows = n_ref.shape[0] // 4
    at = late[0].shape[0] - MODE_ROWS

    @pl.when(info[0] == s)
    def _():
        copies = (
            row_copies(early, 0, a_ref, sems.at[0])
            + row_copies(early, rows, n_ref, sems.at[1])
            + row_copies(late, 0, h_ref, sems.at[2])
            + row_copies(late, rows, b_ref, sems.at[3])
        )
        for i, pack in enumerate(late):
            modes = pack.at[pl.ds(at, MODE_ROWS), pl.ds(0, 256)]
            copies.append(pltpu.make_async_copy(modes, mode_ref.at[i], sems.at[4, i]))
        start_all(copies)
        wait_all(copies)
        width = n_ref.shape[1]
        out[pl.ds(2 * width, MODE_ROWS), :] = join_modes(mode_ref, width // 4)
        for c in range(width // 256):
            part = pl.ds(c * 256, 256)
            out[part, :] = dot_tn(h_ref[:, part], n_ref[...]).astype(BF)
            out[pl.ds(width + c * 256, 256), :] = dot_tn(a_ref[:, part], b_ref[...]).astype(BF)


def mlp_grads(s, info, early, late, rows):
    width = late[0].shape[1]
    ins = [(info, smem())]
    ins += [(value, hbm()) for value in (*early, *late)]
    outs = [(shape((2 * width + MODE_ROWS, width), BF), vmem())]
    scratch = [pltpu.VMEM((4 * rows, width), BF)] * 4
    scratch += [pltpu.VMEM((4, MODE_ROWS, 256), BF), DMA((5, 4))]
    kernel = functools.partial(mlp_grads_kernel, s)
    return call(kernel, ins, outs, scratch, {}, cost(2_600_000_000, 10_000_000))[0]


def finish_kernel(*refs):
    info = refs[0]
    pairs = [refs[1 + 2 * s : 3 + 2 * s] for s in range(4)]
    main, second, modes, held, mode_ref, sems = refs[9:]
    width = main.shape[0]
    half = width // 2
    here = pl.ds(pl.multiple_of(info[2] * half, half), half)
    there = pl.ds(pl.multiple_of((1 - info[2]) * half, half), half)

    def mode_copies(s):
        copies = []
        for i, value in enumerate(pairs[s]):
            rows = value.at[pl.ds(value.shape[0] - MODE_ROWS, MODE_ROWS)]
            which = info[2] if i == 0 else 1 - info[2]
            copies.append(pltpu.make_async_copy(rows, mode_ref.at[which], sems.at[4 + i]))
        return copies

    def halves(s):
        own, other = pairs[s]
        copies = mode_copies(s)
        for k in range(own.shape[0] // half):
            part = pl.ds(k * half, half)
            copies += [
                pltpu.make_async_copy(own.at[part], held.at[k, here], sems.at[2 * k]),
                pltpu.make_async_copy(other.at[part], held.at[k, there], sems.at[2 * k + 1]),
            ]
        start_all(copies)
        wait_all(copies)
        main[...] = held[0].astype(F32).T
        if own.shape[0] > width:
            second[...] = held[1].astype(F32)

    for s in (0, 2, 3):

        @pl.when(info[0] == s)
        def _():
            halves(s)

    @pl.when(info[0] == 1)
    def _():
        copies = mode_copies(1)
        for i, value in enumerate(pairs[1]):
            for k in range(2):
                part = value.at[pl.ds(k * width, width)]
                copies.append(
                    pltpu.make_async_copy(part, held.at[2 * i + k], sems.at[2 * i + k])
                )
        start_all(copies)
        wait_all(copies)
        main[...] = (held[0].astype(F32) + held[2].astype(F32)).T
        second[...] = held[1].astype(F32) + held[3].astype(F32)

    columns = width // 4
    for i in range(2):
        value = mode_ref[i].astype(F32)
        value = value[0:3] + value[3:6]
        for j in range(4):
            modes[4 * i + j] = value[:, j * columns : (j + 1) * columns]


def finish(info, pairs, width):
    ins = [(info, smem())] + [(value, hbm()) for pair in pairs for value in pair]
    outs = [
        (shape((width, width), F32), vmem()),
        (shape((width, width), F32), vmem()),
        (shape((8, 3, width // 4), F32), vmem()),
    ]
    scratch = [
        pltpu.VMEM((4, width, width), BF),
        pltpu.VMEM((2, MODE_ROWS, width), BF),
        DMA((6,)),
    ]
    return call(finish_kernel, ins, outs, scratch, {}, cost(10_000_000, 10_000_000))


def collect_kernel(rows_at, *refs):
    info = refs[0]
    groups = [refs[1 + 4 * s : 5 + 4 * s] for s in range(4)]
    out, held, sems = refs[17:]
    block = held.shape[1]
    for s in range(4):

        @pl.when(info[0] == s)
        def _():
            copies = [
                pltpu.make_async_copy(
                    pack.at[pl.ds(rows_at[s], block)], held.at[i], sems.at[i]
                )
                for i, pack in enumerate(groups[s])
            ]
            start_all(copies)
            wait_all(copies)

    for i in range(4):
        out[lax.rem(info[1] + (0, 3, 1, 2)[i], 4)] = held[i].astype(F32)


def collect(info, groups, rows_at, block):
    width = groups[0][0].shape[1]
    ins = [(info, smem())] + [(value, hbm()) for group in groups for value in group]
    outs = [(shape((4, block, width), F32), vmem())]
    scratch = [pltpu.VMEM((4, block, width), BF), DMA((4,))]
    kernel = functools.partial(collect_kernel, rows_at)
    return call(kernel, ins, outs, scratch, {}, cost(1_000_000, 2_000_000))[0]


def tensor_back(i, n):
    return (i - 1) % n


def tensor_on(i, n):
    return (i + 1) % n


def tensor_far(i, n):
    return i ^ 2


def gather_weight(local, part, dp_part):
    half = local.shape[0] // 2
    mine = lax.dynamic_slice_in_dim(local, dp_part % 2 * half, half, 0)
    before = cyclic(mine, "tensor", 1)
    after = cyclic(mine, "tensor", -1)
    far = swap(jnp.where(part % 2 == 0, before, after), "tensor", 1)
    pieces = [local]
    for piece in (before, after, far):
        pieces += [piece, swap(piece, "dp", 1)]
    return pieces


def trade(packs, which):
    own, back, on, far = packs
    return (
        own,
        within(on, "tensor", which, tensor_on),
        within(back, "tensor", which, tensor_back),
        within(far, "tensor", which, tensor_far),
    )


def body(clean, noise, times, flags, cotangent, w_main, w_half, w_mod):
    section = lax.axis_index("section")
    part = lax.axis_index("tensor")
    dp_part = lax.axis_index("dp")
    local_seqs, length, width = clean.shape
    columns = w_main.shape[3]
    halfdim = HEAD_DIM // 2

    main_local = w_main[0].reshape(width, 4 * columns)
    weights = gather_weight(main_local, part, dp_part)
    second_own = gather_weight(w_half[0], part, dp_part)
    second_other = [swap(piece, "section", 1) for piece in second_own]

    def mine(values):
        return lax.dynamic_index_in_dim(values, part, 0, keepdims=False)

    theta = math.pi / 2 * (mine(times).astype(F32) + 1.0) / (TSTEPS + 1.0)
    noisy = jnp.cos(theta) * mine(clean).astype(F32) + jnp.sin(theta) * mine(noise).astype(F32)
    target = mine(cotangent)
    info = jnp.stack([section, part, dp_part % 2, mine(flags)]).astype(jnp.int32)

    halfwidth = width // 2
    freqs = jnp.exp(-math.log(10000.0) * jnp.arange(halfwidth, dtype=F32) / halfwidth)
    angles = times.astype(F32)[:, None] * freqs[None, :]
    temb = jnp.concatenate([jnp.sin(angles), jnp.cos(angles)], axis=1)
    temb_turn = jnp.stack(
        [lax.dynamic_index_in_dim(temb, (part + i) % 4, 0, keepdims=False) for i in (0, 3, 1, 2)]
    )
    temb_other = swap(temb_turn, "dp", 1)
    temb_pair = jnp.where(
        dp_part % 2 == 0,
        jnp.concatenate([temb_turn, temb_other]),
        jnp.concatenate([temb_other, temb_turn]),
    )
    mode_part = jnp.einsum("nd,dpc->npc", temb, w_mod[0].astype(F32), precision=HIGHEST)

    def for_part(target_part):
        return lax.dynamic_index_in_dim(mode_part, target_part % 4, 0, keepdims=False)

    mode_turn = jnp.stack(
        [
            for_part(part),
            cyclic(for_part(part + 3), "tensor", -1),
            swap(for_part(part + 2), "tensor", 2),
            cyclic(for_part(part + 1), "tensor", 1),
        ],
        axis=1,
    )
    mode_twice = jnp.concatenate([mode_turn, mode_turn], axis=1)
    modes = lax.dynamic_slice_in_dim(mode_twice, (4 - part) % 4, 4, 1).reshape(3, width)

    inverse = jnp.exp(-math.log(10000.0) * 2.0 * jnp.arange(halfdim, dtype=F32) / HEAD_DIM)
    turn = jnp.arange(length, dtype=F32)[:, None] * inverse[None, :]
    cosine = jnp.tile(jnp.cos(turn), (1, 4))
    sine = jnp.tile(jnp.concatenate([-jnp.sin(turn), jnp.sin(turn)], axis=1), (1, 2))

    def attend(s, base, arrived, keep):
        return attention_forward(s, info, base, arrived, modes, cosine, sine, weights, keep)

    def feed(s, arrived, keep):
        return mlp_forward(s, info, arrived, modes, weights, second_other, second_own, keep)

    def feed_back(s, grad, kept, keep):
        return mlp_back(s, info, grad, modes, kept, weights, second_other, second_own, keep)

    def attend_back(s, grad, kept):
        return attention_back(s, info, grad, modes, cosine, sine, kept, weights)

    def after(value, earlier):
        return lax.optimization_barrier((value, earlier))

    def across(value, s):
        return within(value, "dp", (s,), lambda i, n: i ^ 1)

    value = attend(0, noisy, None, False)[0]
    value = feed(1, section_hop(value, 0, 1), None)[0]
    value = attend(2, None, section_hop(value, 1, 1), False)[0]
    value = feed(3, section_hop(value, 2, 1), None)[0]
    guess = cyclic(value, "section", 1)

    kept_0 = attend(0, noisy, guess, True)
    kept_1 = feed(1, section_hop(kept_0[0], 0, 1), "packs")
    stream_2 = section_hop(kept_1[0], 1, 1)
    pack_1, stream_2 = after(kept_1[4:], stream_2)
    early_1 = trade(pack_1, (1,))
    kept_2 = attend(2, None, stream_2, True)
    kept_3 = feed(3, section_hop(kept_2[0], 2, 1), "message")

    back_3 = feed_back(3, target, kept_3, "message")
    grad_2 = section_hop(back_3[0], 3, -1)
    (message_3, grad_2), early_1 = after((back_3[2], grad_2), early_1)
    other_3 = across(message_3, 3)
    back_2 = attend_back(2, grad_2, kept_2)
    grad_1 = lax.ppermute(back_2[0], "section", [(2, 1)])
    message_2, grad_1 = after(back_2[2], grad_1)
    other_2 = across(message_2, 2)
    back_1 = feed_back(1, grad_1, kept_1, "packs")
    grad_0 = section_hop(back_1[0], 1, -1)
    pack_1, grad_0 = after(back_1[2:], grad_0)
    late_1 = trade(pack_1, (1,))
    back_0 = attend_back(0, grad_0, kept_0)
    message_0, other_3 = after(back_0[2], other_3)
    other_0 = across(message_0, 0)
    other_2, message_0 = after(other_2, message_0)

    sums_3 = mlp_sums(3, info, kept_3, back_3, other_3)
    sums_0 = attention_sums(0, info, kept_0, back_0, other_0)
    sums_2 = attention_sums(2, info, kept_2, back_2, other_2)
    sums_0, late_1 = after(sums_0, late_1)
    group_0 = trade(sums_0, (0,))
    own_1 = mlp_grads(1, info, early_1, late_1, length)
    own_0 = total_parts(0, info, group_0, width // 2)
    sums_3, own_0 = after(sums_3, own_0)
    group_3 = trade(sums_3, (3,))
    sums_2, group_3 = after(sums_2, group_3)
    group_2 = trade(sums_2, (2,))
    own_3 = total_parts(3, info, group_3, width)
    own_2 = total_parts(2, info, group_2, width // 2)

    def other_pairs(value, s):
        size = lax.axis_size("dp")
        bit = 2
        while bit < size:
            partner = within(value, "dp", (s,), lambda i, n: i ^ bit)
            value = (value.astype(F32) + partner.astype(F32)).astype(BF)
            bit *= 2
        return value

    pairs = []
    for s, own in enumerate((own_0, own_1, own_2, own_3)):
        own = other_pairs(own, s)
        pairs.append((own, across(own, s)))
    block = length // 4
    groups = (group_0, early_1, group_2, group_3)
    outputs = collect(info, groups, (width // 2, 2 * length, width // 2, width), block)
    groups = (group_0, late_1, group_2, group_3)
    at = width // 2 + block
    in_grads = collect(info, groups, (at, 2 * length, at, width + block), block)
    pairs, outputs, in_grads = lax.optimization_barrier((pairs, outputs, in_grads))
    main_total, second_total, mode_grads = finish(info, pairs, width)
    mode_total = jnp.einsum("nd,npc->dpc", temb_pair, mode_grads, precision=HIGHEST)
    bit = 2
    while bit < lax.axis_size("dp"):
        mode_total = mode_total + swap(mode_total, "dp", bit)
        bit *= 2
    is_even = section % 2 == 0
    halfway = 2 * columns
    returned = swap(second_total[:halfway].astype(BF), "section", 1).astype(F32)
    half_total = jnp.where(is_even, returned, second_total[halfway:])

    return (
        outputs[None],
        in_grads[None],
        main_total.reshape(1, width, 4, columns),
        half_total[None],
        mode_total[None],
    )


def solution(mesh):
    in_specs = (
        P("dp", None, None),
        P("dp", None, None),
        P("dp"),
        P("dp"),
        P("dp", None, None),
        P("section", None, None, "tensor"),
        P("section", "tensor", None),
        P("section", None, None, "tensor"),
    )
    out_specs = (
        P("section", "dp", "tensor", None),
        P("section", "dp", "tensor", None),
        P("section", None, None, "tensor"),
        P("section", "tensor", None),
        P("section", None, None, "tensor"),
    )
    return jax.shard_map(body, mesh=mesh, in_specs=in_specs, out_specs=out_specs, check_vma=False)
```

```python
import functools
import math

import jax
import jax.numpy as jnp
import numpy as np
from jax import lax
from jax.experimental import pallas as pl
from jax.experimental.pallas import tpu as pltpu
from jax.sharding import PartitionSpec as P

HEAD_DIM = 64
TSTEPS = 1000
EPSILON = 1e-05
HIGHEST = lax.Precision.HIGHEST
BF = jnp.bfloat16
F32 = jnp.float32
VMEM_BYTES = 32 * 1024 * 1024
WEIGHT_SIZE = 4 * 768 * 768
FLIPS = (0, 1, 3, 2)
GELU_C = math.sqrt(2.0 / math.pi)
GELU_A = 0.044715


def cyclic(value, axis, by):
    size = lax.axis_size(axis)
    return lax.ppermute(value, axis, [(i, (i + by) % size) for i in range(size)])


def swap(value, axis, bit):
    size = lax.axis_size(axis)
    return lax.ppermute(value, axis, [(i, i ^ bit) for i in range(size)])


def within(value, axis, which, route):
    size = lax.axis_size(axis)
    pairs = [(s * size + i, s * size + route(i, size)) for s in which for i in range(size)]
    return lax.ppermute(value, ("section", axis), pairs)


def section_hop(value, source, by):
    target = source + by
    if source // 2 == target // 2:
        return swap(value, "section", 1)
    return cyclic(value, "section", by)


def dot(left, right):
    return lax.dot_general(left, right, (((1,), (0,)), ((), ())), preferred_element_type=F32)


def dot_nt(left, right):
    return lax.dot_general(left, right, (((1,), (1,)), ((), ())), preferred_element_type=F32)


def dot_tn(left, right):
    return lax.dot_general(left, right, (((0,), (0,)), ((), ())), preferred_element_type=F32)


def standardize(stream):
    centred = stream - jnp.mean(stream, axis=-1, keepdims=True)
    variance = jnp.mean(centred * centred, axis=-1, keepdims=True)
    inverse = lax.rsqrt(variance + EPSILON)
    return centred * inverse, inverse


def swap_halves(block, first):
    return jnp.where(first, pltpu.roll(block, 96, 1), pltpu.roll(block, 32, 1))


def first_mask(rows):
    lane = lax.broadcasted_iota(jnp.int32, (rows, 128), 1)
    return (lane % HEAD_DIM) < HEAD_DIM // 2


def norm_back(normed_grad, stream, scale, grad):
    hat, inverse = standardize(stream)
    shift_grad = jnp.sum(normed_grad, axis=0, keepdims=True)
    scale_grad = jnp.sum(normed_grad * hat, axis=0, keepdims=True)
    hat_grad = normed_grad * (1.0 + scale)
    mean_one = jnp.mean(hat_grad, axis=-1, keepdims=True)
    mean_two = jnp.mean(hat_grad * hat, axis=-1, keepdims=True)
    in_grad = grad + inverse * (hat_grad - mean_one - hat * mean_two)
    return in_grad, shift_grad, scale_grad


def start_all(copies):
    for copy in copies:
        copy.start()


def wait_all(copies):
    for copy in copies:
        copy.wait()


def slot_rows(info, slot, block):
    return pl.ds(pl.multiple_of(slot_part(info, slot) * block, block), block)


def send_halves(send, source, target, at):
    for k in range(2):
        send(source.at[k], target.at[at + k])


def put_halves(ref, value):
    half = ref.shape[2]
    ref[0] = value[:, :half]
    ref[1] = value[:, half:]


MODE_ROWS = 16


def put_mode_grads(ref, values):
    joined = jnp.concatenate(values, axis=0)
    high = joined.astype(BF)
    rest = (joined - high.astype(F32)).astype(BF)
    filler = jnp.zeros((MODE_ROWS - 6, joined.shape[1]), BF)
    both = jnp.concatenate([high, rest, filler], axis=0)
    columns = both.shape[1] // 4
    ref[...] = jnp.zeros_like(ref)
    for part in range(4):
        ref[part, :, :columns] = both[:, part * columns : (part + 1) * columns]


def slot_part(info, slot):
    return info[1] ^ FLIPS[slot]


def vmem():
    return pl.BlockSpec(memory_space=pltpu.VMEM)


def smem():
    return pl.BlockSpec(memory_space=pltpu.SMEM)


def hbm():
    return pl.BlockSpec(memory_space=pltpu.HBM)


def anywhere():
    return pl.BlockSpec(memory_space=pl.ANY)


def params(limit):
    return pltpu.CompilerParams(vmem_limit_bytes=limit)


def cost(flops, nbytes):
    return pl.CostEstimate(flops=flops, bytes_accessed=nbytes, transcendentals=0)


def call(kernel, ins, outs, scratch, aliases, estimate, limit=VMEM_BYTES):
    def placed(value, spec):
        if spec.memory_space is pltpu.HBM:
            return pltpu.with_memory_space_constraint(value, pltpu.HBM)
        if value.size >= WEIGHT_SIZE:
            return pltpu.with_memory_space_constraint(value, pltpu.VMEM)
        return value

    def result(value, spec):
        if spec.memory_space is pltpu.HBM:
            return pltpu.HBM(value.shape, value.dtype)
        if math.prod(value.shape) >= WEIGHT_SIZE:
            return pltpu.VMEM(value.shape, value.dtype)
        return value

    return pl.pallas_call(
        kernel,
        out_shape=[result(*pair) for pair in outs],
        in_specs=[spec for _, spec in ins],
        out_specs=[spec for _, spec in outs],
        scratch_shapes=scratch,
        input_output_aliases=aliases,
        compiler_params=params(limit),
        cost_estimate=estimate,
    )(*[placed(*pair) for pair in ins])


def shape(dims, dtype):
    return jax.ShapeDtypeStruct(dims, dtype)


DMA = pltpu.SemaphoreType.DMA


def place_kernel(slot, odd_only, *refs):
    info, pieces, (out, sems) = refs[0], refs[1:-3], refs[-2:]
    rows = out.shape[1] // len(pieces)

    def copy_all():
        copies = []
        for i, piece in enumerate(pieces):
            begin = 0
            if len(pieces) == 2:
                begin = pl.multiple_of((info[2] if i == 0 else 1 - info[2]) * rows, rows)
            target = out.at[slot, pl.ds(begin, rows)]
            copies.append(pltpu.make_async_copy(piece.at[pl.ds(0, rows)], target, sems.at[i]))
        start_all(copies)
        wait_all(copies)

    if odd_only:
        pl.when(info[0] % 2 == 1)(copy_all)
    else:
        copy_all()


def first_kernel(odd_only, info, piece, out, sems):
    place_kernel(0, odd_only, info, piece, None, out, sems)


def place(info, weight, slot, pieces, odd_only):
    ins = [(info, smem())] + [(piece, anywhere()) for piece in pieces]
    width = pieces[0].shape[1]
    aliases = {}
    if weight is None:
        kernel = functools.partial(first_kernel, odd_only)
    else:
        kernel = functools.partial(place_kernel, slot, odd_only)
        aliases = {len(ins): 0}
        ins.append((weight, vmem()))
    outs = [(shape((4, width, width), BF), vmem())]
    estimate = cost(1_000_000, 2_000_000)
    return call(kernel, ins, outs, [DMA((2,))], aliases, estimate, 1024 * 1024)[0]


def modes_kernel(*refs):
    info, pieces, (modes, mode_ref, sems) = refs[0], refs[1:5], refs[5:]
    copies = [
        pltpu.make_async_copy(
            piece.at[pl.ds(piece.shape[0] - MODE_ROWS, MODE_ROWS)], mode_ref.at[i], sems.at[i]
        )
        for i, piece in enumerate(pieces)
    ]
    start_all(copies)
    wait_all(copies)
    columns = modes.shape[1] // 4
    for part in range(4):
        bits = info[1] ^ part
        block = mode_ref[bits ^ (bits >> 1)].astype(F32)
        value = block[0:3] + block[3:6]
        chosen = jnp.zeros((3, columns), F32)
        for sequence in range(4):
            here = value[:, sequence * columns : (sequence + 1) * columns]
            chosen = jnp.where(info[1] == sequence, here, chosen)
        modes[:, part * columns : (part + 1) * columns] = chosen


def pick_modes(info, pieces):
    width = pieces[0].shape[1]
    ins = [(info, smem())] + [(piece, anywhere()) for piece in pieces]
    outs = [(shape((3, width), F32), vmem())]
    scratch = [pltpu.VMEM((4, MODE_ROWS, width), BF), DMA((4,))]
    estimate = cost(1_000_000, 1_000_000)
    return call(modes_kernel, ins, outs, scratch, {}, estimate, 2 * 1024 * 1024)[0]


def head_parts(heads, head):
    j, at = head // 3, head % 3 * HEAD_DIM
    return tuple(heads[j, :, at + 192 * i : at + 192 * i + HEAD_DIM] for i in range(3))


def attention_forward_kernel(s, has_base, has_arrived, keep, *refs):
    refs = list(refs)
    info = refs.pop(0)
    base = refs.pop(0) if has_base else None
    arrived = refs.pop(0) if has_arrived else None
    modes, cosine, sine, w = refs[:4]
    refs = refs[4:]
    result = refs.pop(0)
    if keep:
        heads_out, lse_out, attended_out, branch_out, stream_out = refs[:5]
        normed_out, result_out, message = refs[5:8]
        refs = refs[8:]
    normed, branch, heads, attended_ref, scores_ref = refs[:5]
    if keep:
        stream_ref, lse, halves, osems = refs[5:]

    def load_stream():
        if not has_base:
            return arrived[...].astype(F32)
        if not has_arrived:
            return base[...]
        return base[...] + info[3].astype(F32) * arrived[...].astype(F32)

    @pl.when(info[0] == s)
    def _():
        outs = []

        def send(source, target):
            copy = pltpu.make_async_copy(source, target, osems.at[len(outs)])
            copy.start()
            outs.append(copy)

        stream = load_stream()
        hat, _ = standardize(stream)
        normed[...] = (hat * (1.0 + modes[1:2, :]) + modes[0:1, :]).astype(BF)
        rows = normed.shape[0]
        if keep:
            stream_ref[...] = stream
            send(stream_ref, stream_out)
            put_halves(halves, normed[...])
            send_halves(send, halves, normed_out, 0)
            send_halves(send, halves, message, 0)
        first = first_mask(rows)
        low = lax.broadcasted_iota(jnp.int32, (rows, 128), 1) < HEAD_DIM
        for j in range(4):
            raw = dot(normed[...], w[j, :, :576])
            turned = []
            for unit in range(3):
                block = raw[:, unit * 128 : (unit + 1) * 128]
                block = block * cosine[...] + swap_halves(block, first) * sine[...]
                if unit == 0:
                    block = block * 0.125
                if unit == 1:
                    block = jnp.where(low, block * 0.125, block)
                turned.append(block)
            heads[j] = jnp.concatenate(turned + [raw[:, 384:576]], axis=1).astype(BF)
            if keep:
                send(heads.at[j], heads_out.at[j])
        for head in range(12):
            q, k, _ = head_parts(heads, head)
            scores_ref[head] = dot_nt(k, q)
        for j in range(4):
            pieces_t = [jnp.zeros((HEAD_DIM, rows), BF)]
            for head in range(3 * j, 3 * j + 3):
                _, _, v = head_parts(heads, head)
                scores = scores_ref[head]
                top = jnp.max(scores, axis=0, keepdims=True)
                raised = jnp.exp(scores - top)
                total = jnp.sum(raised, axis=0, keepdims=True)
                if keep:
                    lse[head : head + 1, :] = top + jnp.log(total)
                mixed = dot_tn(v, raised.astype(BF)) * (1.0 / total)
                pieces_t.append(mixed.astype(BF))
            attended_ref[j] = jnp.concatenate(pieces_t, axis=0).T
            if keep:
                send(attended_ref.at[j], attended_out.at[j])
        for j in range(4):
            part = dot_nt(attended_ref[j], w[j, :, 512:768])
            branch[...] = part if j == 0 else branch[...] + part
        result[...] = (load_stream() + modes[2:3, :] * branch[...]).astype(BF)
        if keep:
            send(lse, lse_out)
            send(branch, branch_out)
            send(result, result_out)
            wait_all(outs)


def attention_forward(s, info, base, arrived, modes, cosine, sine, weights, keep):
    width = modes.shape[1]
    rows = cosine.shape[0]
    ins = [(info, smem())]
    for value in (base, arrived):
        if value is not None:
            ins.append((value, vmem()))
    ins += [(modes, vmem()), (cosine, vmem()), (sine, vmem()), (weights, vmem())]
    outs = [(shape((rows, width), BF), vmem())]
    scratch = [
        pltpu.VMEM((rows, width), BF),
        pltpu.VMEM((rows, width), F32),
        pltpu.VMEM((4, rows, 576), BF),
        pltpu.VMEM((4, rows, 256), BF),
        pltpu.VMEM((12, rows, rows), F32),
    ]
    if keep:
        outs += [
            (shape((4, rows, 576), BF), hbm()),
            (shape((12, rows), F32), hbm()),
            (shape((4, rows, 256), BF), hbm()),
            (shape((rows, width), F32), hbm()),
            (shape((rows, width), F32), hbm()),
            (shape((2, rows, width // 2), BF), hbm()),
            (shape((rows, width), BF), hbm()),
            (shape((8, rows, width // 2), BF), hbm()),
        ]
        scratch += [
            pltpu.VMEM((rows, width), F32),
            pltpu.VMEM((12, rows), F32),
            pltpu.VMEM((2, rows, width // 2), BF),
            DMA((16,)),
        ]
    kernel = functools.partial(
        attention_forward_kernel, s, base is not None, arrived is not None, keep
    )
    return call(kernel, ins, outs, scratch, {}, cost(2_000_000_000, 6_000_000))


def attention_back_kernel(s, *refs):
    info, grad, modes, cosine, sine, w = refs[:6]
    heads_in, lse_in, attended_in, branch_in, stream_in = refs[6:11]
    in_grad, mode_out, message, pack_out, bg_out, in_out = refs[12:18]
    heads, lse, attended_ref, branch, stream, bg, ng, halves, pack_ref = refs[18:27]
    att_grad, scores_ref, prob_grads, probs_ref, ds_ref, raw_ref = refs[27:33]
    mode_ref, isems, osems = refs[33:]

    @pl.when(info[0] == s)
    def _():
        loads = []
        for source, target in (
            (heads_in, heads),
            (lse_in, lse),
            (attended_in, attended_ref),
            (stream_in, stream),
            (branch_in, branch),
        ):
            copy = pltpu.make_async_copy(source, target, isems.at[len(loads)])
            loads.append(copy)
        start_all(loads)
        outs = []

        def send(source, target):
            copy = pltpu.make_async_copy(source, target, osems.at[len(outs)])
            copy.start()
            outs.append(copy)

        g = grad[...].astype(F32)
        rows = g.shape[0]
        bg[...] = (modes[2:3, :] * g).astype(BF)
        put_halves(halves, bg[...])
        send_halves(send, halves, bg_out, 0)
        send_halves(send, halves, message, 2)
        first = first_mask(rows)
        for j in range(4):
            att_grad[j] = dot(bg[...], w[j, :, 512:768]).astype(BF)
        wait_all(loads[:2])
        for head in range(12):
            q, k, _ = head_parts(heads, head)
            scores_ref[head] = dot_nt(k, q)
        for head in range(12):
            _, _, v = head_parts(heads, head)
            at = 64 + head % 3 * HEAD_DIM
            prob_grads[head] = dot_nt(v, att_grad[head // 3, :, at : at + HEAD_DIM])
        for head in range(12):
            probs = jnp.exp(scores_ref[head] - lse[head : head + 1, :])
            inner = jnp.sum(prob_grads[head] * probs, axis=0, keepdims=True)
            probs_ref[head] = probs.astype(BF)
            ds_ref[head] = (probs * (prob_grads[head] - inner)).astype(BF)
        wait_all(loads[2:])
        for j in range(4):
            dq, dk, dv = [], [], []
            for head in range(3 * j, 3 * j + 3):
                q, k, _ = head_parts(heads, head)
                at = 64 + head % 3 * HEAD_DIM
                dv.append(dot(probs_ref[head], att_grad[j, :, at : at + HEAD_DIM]))
                dk.append(dot(ds_ref[head], q))
                dq.append(dot_tn(k, ds_ref[head]))
            dq_all = (jnp.concatenate(dq, axis=0) * 0.125).T
            both = jnp.concatenate([dq_all] + dk, axis=1)
            turned = []
            for unit in range(3):
                block = both[:, unit * 128 : (unit + 1) * 128]
                turned.append(block * cosine[...] - swap_halves(block, first) * sine[...])
            raw = jnp.concatenate(turned + dv, axis=1).astype(BF)
            raw_ref[j] = raw
            pack_ref[j, 0] = raw[:, :384]
            pack_ref[j, 1] = jnp.concatenate([raw[:, 384:576], attended_ref[j, :, 64:256]], axis=1)
            send(pack_ref.at[j, info[2]], pack_out.at[j])
            send(pack_ref.at[j, 1 - info[2]], message.at[4 + j])
        for j in range(4):
            part = dot_nt(raw_ref[j], w[j, :, :576])
            ng[...] = part if j == 0 else ng[...] + part
        total, shift_grad, scale_grad = norm_back(
            ng[...], stream[...], modes[1:2, :], grad[...].astype(F32)
        )
        in_grad[...] = total.astype(BF)
        send(in_grad, in_out)
        gate_grad = jnp.sum(grad[...].astype(F32) * branch[...], axis=0, keepdims=True)
        put_mode_grads(mode_ref, (shift_grad, scale_grad, gate_grad))
        send(mode_ref, mode_out)
        wait_all(outs)


def attention_back(s, info, grad, modes, cosine, sine, kept, weights):
    rows, width = grad.shape
    ins = [(info, smem()), (grad, vmem()), (modes, vmem()), (cosine, vmem()), (sine, vmem())]
    ins += [(weights, vmem())]
    ins += [(value, hbm()) for value in kept[1:6]]
    aliases = {len(ins): 2}
    ins += [(kept[8], hbm())]
    outs = [
        (shape((rows, width), BF), vmem()),
        (shape((4, MODE_ROWS, 256), BF), hbm()),
        (shape(kept[8].shape, BF), hbm()),
        (shape((4, rows, width // 2), BF), hbm()),
        (shape((2, rows, width // 2), BF), hbm()),
        (shape((rows, width), BF), hbm()),
    ]
    scratch = [
        pltpu.VMEM((4, rows, 576), BF),
        pltpu.VMEM((12, rows), F32),
        pltpu.VMEM((4, rows, 256), BF),
        pltpu.VMEM((rows, width), F32),
        pltpu.VMEM((rows, width), F32),
        pltpu.VMEM((rows, width), BF),
        pltpu.VMEM((rows, width), F32),
        pltpu.VMEM((2, rows, width // 2), BF),
        pltpu.VMEM((4, 2, rows, width // 2), BF),
        pltpu.VMEM((4, rows, 256), BF),
        pltpu.VMEM((12, rows, rows), F32),
        pltpu.VMEM((12, rows, rows), F32),
        pltpu.VMEM((12, rows, rows), BF),
        pltpu.VMEM((12, rows, rows), BF),
        pltpu.VMEM((4, rows, 576), BF),
        pltpu.VMEM((4, MODE_ROWS, 256), BF),
        DMA((5,)),
        DMA((14,)),
    ]
    kernel = functools.partial(attention_back_kernel, s)
    return call(kernel, ins, outs, scratch, aliases, cost(3_000_000_000, 10_000_000))


def mlp_forward_kernel(s, keep, *refs):
    info, arrived, modes, w1, w2, result = refs[:6]
    refs = refs[6:]
    if keep:
        slope_out, branch_out, stream_out = refs[:3]
        refs = refs[3:]
    if keep == "packs":
        packs = refs[:4]
        refs = refs[4:]
    if keep == "message":
        act_out, normed_out, result_out, message = refs[:4]
        refs = refs[4:]
    normed, branch = refs[:2]
    if keep:
        act_ref, slope_ref, halves, osems = refs[2:]

    @pl.when(info[0] == s)
    def _():
        outs = []

        def send(source, target):
            copy = pltpu.make_async_copy(source, target, osems.at[len(outs)])
            copy.start()
            outs.append(copy)

        hat, _ = standardize(arrived[...].astype(F32))
        normed[...] = (hat * (1.0 + modes[1:2, :]) + modes[0:1, :]).astype(BF)
        rows = normed.shape[0]
        if keep:
            send(arrived, stream_out)
        if keep == "packs":
            for pack in packs:
                send(normed, pack.at[pl.ds(rows, rows)])
        if keep == "message":
            put_halves(halves, normed[...])
            send_halves(send, halves, normed_out, 0)
            send_halves(send, halves, message, 0)
        hidden_next = dot(normed[...], w1[0])
        for j in range(4):
            hidden = hidden_next
            if j < 3:
                hidden_next = dot(normed[...], w1[j + 1])
            square = hidden * hidden
            bend = jnp.tanh(GELU_C * hidden * (1.0 + GELU_A * square))
            act = (0.5 * hidden * (1.0 + bend)).astype(BF)
            if keep:
                slope = 0.5 * (1.0 + bend) + (0.5 * GELU_C) * hidden * (1.0 - bend * bend) * (
                    1.0 + (3.0 * GELU_A) * square
                )
                slope_ref[j] = slope.astype(BF)
                send(slope_ref.at[j], slope_out.at[j])
            if keep == "packs":
                act_ref[j] = act
                send(act_ref.at[j], packs[j].at[pl.ds(0, rows)])
            if keep == "message":
                put_halves(act_ref.at[j], act)
                send(act_ref.at[j, info[2]], act_out.at[j])
                send(act_ref.at[j, 1 - info[2]], message.at[8 + j])
            part = dot(act, w2[j])
            branch[...] = part if j == 0 else branch[...] + part
        result[...] = (arrived[...].astype(F32) + modes[2:3, :] * branch[...]).astype(BF)
        if keep:
            send(branch, branch_out)
            block = rows // 4
            if keep == "packs":
                for slot, pack in enumerate(packs):
                    send(result.at[slot_rows(info, slot, block)], pack.at[pl.ds(2 * rows, block)])
            else:
                send(result, result_out)
            wait_all(outs)


def mlp_forward(s, info, arrived, modes, first, second, keep):
    rows, width = arrived.shape
    ins = [(info, smem()), (arrived, vmem()), (modes, vmem())]
    ins += [(first, vmem()), (second, vmem())]
    outs = [(shape((rows, width), BF), vmem())]
    scratch = [
        pltpu.VMEM((rows, width), BF),
        pltpu.VMEM((rows, width), F32),
    ]
    if keep:
        outs += [
            (shape((4, rows, width), BF), hbm()),
            (shape((rows, width), F32), hbm()),
            (shape((rows, width), BF), hbm()),
        ]
        if keep == "packs":
            outs += [(shape((2 * rows + rows // 4, width), BF), hbm())] * 4
        else:
            outs += [
                (shape((4, rows, width // 2), BF), hbm()),
                (shape((2, rows, width // 2), BF), hbm()),
                (shape((rows, width), BF), hbm()),
                (shape((12, rows, width // 2), BF), hbm()),
            ]
        wide = (4, rows, width) if keep == "packs" else (4, 2, rows, width // 2)
        scratch += [
            pltpu.VMEM(wide, BF),
            pltpu.VMEM((4, rows, width), BF),
            pltpu.VMEM((2, rows, width // 2), BF),
            DMA((20,)),
        ]
    kernel = functools.partial(mlp_forward_kernel, s, keep)
    return call(kernel, ins, outs, scratch, {}, cost(2_400_000_000, 10_000_000))


def mlp_back_kernel(s, keep, *refs):
    info, grad, modes, slope_in, branch_in, stream_in, w1, w2 = refs[:8]
    if keep == "packs":
        in_grad, mode_out = refs[8:10]
        packs = refs[10:14]
        refs = refs[14:]
    else:
        in_grad, mode_out, message, hidden_out, bg_out, in_out = refs[9:15]
        refs = refs[15:]
    slope, branch, stream, bg, ng, halves, hidden_ref = refs[:7]
    mode_ref, isems, osems = refs[7:]

    @pl.when(info[0] == s)
    def _():
        loads = [
            pltpu.make_async_copy(source, target, isems.at[i])
            for i, (source, target) in enumerate(
                ((slope_in, slope), (stream_in, stream), (branch_in, branch))
            )
        ]
        start_all(loads)
        outs = []

        def send(source, target):
            copy = pltpu.make_async_copy(source, target, osems.at[len(outs)])
            copy.start()
            outs.append(copy)

        g = grad[...].astype(F32)
        rows = g.shape[0]
        bg[...] = (modes[2:3, :] * g).astype(BF)
        if keep == "packs":
            for pack in packs:
                send(bg, pack.at[pl.ds(rows, rows)])
        else:
            put_halves(halves, bg[...])
            send_halves(send, halves, bg_out, 0)
            send_halves(send, halves, message, 2)
        act_grad_next = dot_nt(bg[...], w2[0])
        for j in range(4):
            act_grad = act_grad_next
            if j < 3:
                act_grad_next = dot_nt(bg[...], w2[j + 1])
            if j == 0:
                loads[0].wait()
            hidden_grad = (act_grad * slope[j].astype(F32)).astype(BF)
            if keep == "packs":
                hidden_ref[j] = hidden_grad
                send(hidden_ref.at[j], packs[j].at[pl.ds(0, rows)])
            else:
                put_halves(hidden_ref.at[j], hidden_grad)
                send(hidden_ref.at[j, info[2]], hidden_out.at[j])
                send(hidden_ref.at[j, 1 - info[2]], message.at[4 + j])
            part = dot_nt(hidden_grad, w1[j])
            ng[...] = part if j == 0 else ng[...] + part
        wait_all(loads[1:])
        total, shift_grad, scale_grad = norm_back(
            ng[...], stream[...].astype(F32), modes[1:2, :], grad[...].astype(F32)
        )
        in_grad[...] = total.astype(BF)
        block = rows // 4
        if keep == "packs":
            for slot, pack in enumerate(packs):
                send(in_grad.at[slot_rows(info, slot, block)], pack.at[pl.ds(2 * rows, block)])
        else:
            send(in_grad, in_out)
        gate_grad = jnp.sum(grad[...].astype(F32) * branch[...], axis=0, keepdims=True)
        put_mode_grads(mode_ref, (shift_grad, scale_grad, gate_grad))
        send(mode_ref, mode_out)
        if keep == "packs":
            for slot, pack in enumerate(packs):
                send(
                    mode_ref.at[slot_part(info, slot)],
                    pack.at[pl.ds(2 * rows + block, MODE_ROWS), pl.ds(0, 256)],
                )
        wait_all(outs)


def mlp_back(s, info, grad, modes, kept, first, second, keep):
    rows, width = grad.shape
    ins = [(info, smem()), (grad, vmem()), (modes, vmem())]
    ins += [(value, hbm()) for value in kept[1:4]]
    ins += [(first, vmem()), (second, vmem())]
    outs = [
        (shape((rows, width), BF), vmem()),
        (shape((4, MODE_ROWS, 256), BF), hbm()),
    ]
    aliases = {}
    if keep == "packs":
        outs += [(shape((2 * rows + rows // 4 + MODE_ROWS, width), BF), hbm())] * 4
    else:
        aliases = {len(ins): 2}
        ins += [(kept[7], hbm())]
        outs += [
            (shape(kept[7].shape, BF), hbm()),
            (shape((4, rows, width // 2), BF), hbm()),
            (shape((2, rows, width // 2), BF), hbm()),
            (shape((rows, width), BF), hbm()),
        ]
    wide = (4, rows, width) if keep == "packs" else (4, 2, rows, width // 2)
    scratch = [
        pltpu.VMEM((4, rows, width), BF),
        pltpu.VMEM((rows, width), F32),
        pltpu.VMEM((rows, width), BF),
        pltpu.VMEM((rows, width), BF),
        pltpu.VMEM((rows, width), F32),
        pltpu.VMEM((2, rows, width // 2), BF),
        pltpu.VMEM(wide, BF),
        pltpu.VMEM((4, MODE_ROWS, 256), BF),
        DMA((3,)),
        DMA((17,)),
    ]
    kernel = functools.partial(mlp_back_kernel, s, keep)
    return call(kernel, ins, outs, scratch, aliases, cost(2_400_000_000, 12_000_000))


def row_copies(group, row, target, sems):
    rows = target.shape[0] // 4
    return [
        pltpu.make_async_copy(
            pack.at[pl.ds(row, rows)], target.at[pl.ds(i * rows, rows)], sems.at[i]
        )
        for i, pack in enumerate(group)
    ]


def rows_to_slots(held, mode_ref, outs, at, info, sems):
    block = held.shape[1] // 4
    copies = []
    for slot, out in enumerate(outs):
        part = slot_rows(info, slot, block)
        for i in range(2):
            target = out.at[pl.ds(at + i * block, block)]
            copies.append(pltpu.make_async_copy(held.at[i, part], target, sems.at[i, slot]))
        target = out.at[pl.ds(at + 2 * block, MODE_ROWS), pl.ds(0, 256)]
        copies.append(
            pltpu.make_async_copy(mode_ref.at[slot_part(info, slot)], target, sems.at[2, slot])
        )
    return copies


def row_loads(result_in, in_in, mode_in, held, mode_ref, sems):
    return [
        pltpu.make_async_copy(result_in, held.at[0], sems.at[0]),
        pltpu.make_async_copy(in_in, held.at[1], sems.at[1]),
        pltpu.make_async_copy(mode_in, mode_ref, sems.at[2]),
    ]


def two_sequences(own, other, at, target, sems):
    count, rows = own.shape[:2]
    copies = []
    for j in range(count):
        copies += [
            pltpu.make_async_copy(own.at[j], target.at[j, pl.ds(0, rows)], sems.at[j, 0]),
            pltpu.make_async_copy(
                other.at[at + j], target.at[j, pl.ds(rows, rows)], sems.at[j, 1]
            ),
        ]
    return copies


def attention_sums_kernel(s, *refs):
    info, normed_in, bg_in, pack_in, other, result_in, in_in, mode_in = refs[:8]
    outs = refs[8:12]
    n_ref, b_ref, p_ref, held, row_ref, mode_ref = refs[12:18]
    nsems, bsems, psems, osems, lsems, rsems = refs[18:]
    half = held.shape[1]

    @pl.when(info[0] == s)
    def _():
        loads = row_loads(result_in, in_in, mode_in, row_ref, mode_ref, lsems)
        moves = rows_to_slots(row_ref, mode_ref, outs, half, info, rsems)
        copies = (
            two_sequences(normed_in, other, 0, n_ref, nsems)
            + two_sequences(bg_in, other, 2, b_ref, bsems)
            + two_sequences(pack_in, other, 4, p_ref, psems)
        )
        start_all(copies + loads)
        wait_all(copies + loads)
        start_all(moves)
        tokens = jnp.concatenate([n_ref[0], n_ref[1]], axis=1)
        branch = jnp.concatenate([b_ref[0], b_ref[1]], axis=1)
        for j in range(4):
            held[j] = dot_tn(p_ref[j], tokens).astype(BF)

            @pl.when(info[2] == 1)
            def _():
                outward = dot_tn(p_ref[j, :, 128:], branch)
                held[j, half // 2 :, :] = outward[half // 2 - 128 :].astype(BF)

            copy = pltpu.make_async_copy(
                held.at[j], outs[j].at[pl.ds(0, half)], osems.at[j]
            )
            copy.start()
            moves.append(copy)
        wait_all(moves)


def attention_sums(s, info, kept, back, other):
    rows, width = kept[7].shape
    half = width // 2
    ins = [(info, smem())]
    ins += [
        (value, anywhere() if value is other else hbm())
        for value in (kept[6], back[4], back[3], other, kept[7], back[5], back[1])
    ]
    outs = [(shape((half + rows // 2 + MODE_ROWS, width), BF), hbm())] * 4
    scratch = [
        pltpu.VMEM((2, 2 * rows, half), BF),
        pltpu.VMEM((2, 2 * rows, half), BF),
        pltpu.VMEM((4, 2 * rows, half), BF),
        pltpu.VMEM((4, half, width), BF),
        pltpu.VMEM((2, rows, width), BF),
        pltpu.VMEM((4, MODE_ROWS, 256), BF),
        DMA((2, 2)),
        DMA((2, 2)),
        DMA((4, 2)),
        DMA((4,)),
        DMA((3,)),
        DMA((3, 4)),
    ]
    kernel = functools.partial(attention_sums_kernel, s)
    return call(kernel, ins, outs, scratch, {}, cost(1_300_000_000, 8_000_000))


def mlp_sums_kernel(s, *refs):
    info, normed_in, bg_in, hidden_in, act_in, other, result_in, in_in, mode_in = refs[:9]
    outs = refs[9:13]
    n_ref, b_ref, h_ref, a_ref, held, row_ref, mode_ref = refs[13:20]
    nsems, bsems, hsems, asems, osems, lsems, rsems = refs[20:]
    half = held.shape[1] // 2

    @pl.when(info[0] == s)
    def _():
        loads = row_loads(result_in, in_in, mode_in, row_ref, mode_ref, lsems)
        moves = rows_to_slots(row_ref, mode_ref, outs, 2 * half, info, rsems)
        copies = (
            two_sequences(normed_in, other, 0, n_ref, nsems)
            + two_sequences(hidden_in, other, 4, h_ref, hsems)
            + two_sequences(bg_in, other, 2, b_ref, bsems)
            + two_sequences(act_in, other, 8, a_ref, asems)
        )
        start_all(copies + loads)
        wait_all(copies + loads)
        start_all(moves)
        tokens = jnp.concatenate([n_ref[0], n_ref[1]], axis=1)
        branch = jnp.concatenate([b_ref[0], b_ref[1]], axis=1)
        for j in range(4):
            held[j, :half] = dot_tn(h_ref[j], tokens).astype(BF)
            held[j, half:] = dot_tn(a_ref[j], branch).astype(BF)
            copy = pltpu.make_async_copy(
                held.at[j], outs[j].at[pl.ds(0, 2 * half)], osems.at[j]
            )
            copy.start()
            moves.append(copy)
        wait_all(moves)


def mlp_sums(s, info, kept, back, other):
    rows, width = kept[6].shape
    half = width // 2
    ins = [(info, smem())]
    ins += [
        (value, anywhere() if value is other else hbm())
        for value in (kept[5], back[4], back[3], kept[4], other, kept[6], back[5], back[1])
    ]
    outs = [(shape((width + rows // 2 + MODE_ROWS, width), BF), hbm())] * 4
    scratch = [
        pltpu.VMEM((2, 2 * rows, half), BF),
        pltpu.VMEM((2, 2 * rows, half), BF),
        pltpu.VMEM((4, 2 * rows, half), BF),
        pltpu.VMEM((4, 2 * rows, half), BF),
        pltpu.VMEM((4, width, width), BF),
        pltpu.VMEM((2, rows, width), BF),
        pltpu.VMEM((4, MODE_ROWS, 256), BF),
        DMA((2, 2)),
        DMA((2, 2)),
        DMA((4, 2)),
        DMA((4, 2)),
        DMA((4,)),
        DMA((3,)),
        DMA((3, 4)),
    ]
    kernel = functools.partial(mlp_sums_kernel, s)
    return call(kernel, ins, outs, scratch, {}, cost(2_600_000_000, 12_000_000))


def join_modes(held, columns):
    return jnp.concatenate([held[i, :, :columns] for i in range(4)], axis=1)


def add_passed_kernel(s, *refs):
    info, own, passed, out, held, total, sems = refs
    rows = total.shape[0]
    rest = own.shape[0] - rows

    @pl.when(info[0] == s)
    def _():
        copies = [
            pltpu.make_async_copy(value, held.at[i], sems.at[i])
            for i, value in enumerate((own, passed))
        ]
        start_all(copies)
        wait_all(copies)
        moves = [
            pltpu.make_async_copy(
                held.at[i, pl.ds(rows, rest)], out.at[pl.ds(rows + i * rest, rest)], sems.at[2 + i]
            )
            for i in range(2)
        ]
        start_all(moves)
        total[...] = (held[0, :rows].astype(F32) + held[1, :rows].astype(F32)).astype(BF)
        moves.append(pltpu.make_async_copy(total, out.at[pl.ds(0, rows)], sems.at[4]))
        moves[2].start()
        wait_all(moves)


def add_passed(s, info, own, passed, rows):
    length, width = own.shape
    ins = [(info, smem()), (own, hbm()), (passed, anywhere())]
    outs = [(shape((2 * length - rows, width), BF), hbm())]
    scratch = [pltpu.VMEM((2, length, width), BF), pltpu.VMEM((rows, width), BF), DMA((5,))]
    kernel = functools.partial(add_passed_kernel, s)
    return call(kernel, ins, outs, scratch, {}, cost(10_000_000, 5_000_000))[0]


def find_rows(group, rows, at):
    if len(group) == 4:
        return [(part, rows + at) for part in group]
    rest = group[0].shape[0] - rows
    own, near, mirror = group
    return [(own, rows + at), (near, rows + at), (mirror, rows + at), (mirror, rows + rest + at)]


def join_modes(held, columns):
    return jnp.concatenate([held[i, :, :columns] for i in range(4)], axis=1)


def total_kernel(s, at, *refs):
    info = refs[0]
    parts = refs[1:-4]
    out, held, mode_ref, sems = refs[-4:]
    rows = held.shape[1]

    @pl.when(info[0] == s)
    def _():
        copies = []
        for i, part in enumerate(parts):
            copies.append(
                pltpu.make_async_copy(part.at[pl.ds(0, rows)], held.at[i], sems.at[0, i])
            )
        for i, (part, row) in enumerate(find_rows(parts, rows, at)):
            modes = part.at[pl.ds(row, MODE_ROWS), pl.ds(0, 256)]
            copies.append(pltpu.make_async_copy(modes, mode_ref.at[i], sems.at[1, i]))
        start_all(copies)
        wait_all(copies)
        total = held[0].astype(F32)
        for i in range(1, len(parts)):
            total = total + held[i].astype(F32)
        out[:rows] = total.astype(BF)
        out[rows:] = join_modes(mode_ref, out.shape[1] // 4)


def total_parts(s, info, group, rows):
    width = group[0].shape[1]
    at = group[0].shape[0] - MODE_ROWS - rows
    ins = [(info, smem())] + [(value, anywhere()) for value in group]
    outs = [(shape((rows + MODE_ROWS, width), BF), vmem())]
    scratch = [
        pltpu.VMEM((len(group), rows, width), BF),
        pltpu.VMEM((4, MODE_ROWS, 256), BF),
        DMA((2, 4)),
    ]
    kernel = functools.partial(total_kernel, s, at)
    return call(kernel, ins, outs, scratch, {}, cost(10_000_000, 5_000_000))[0]


def mlp_grads_kernel(s, *refs):
    info = refs[0]
    early, late = refs[1:5], refs[5:9]
    out = refs[9]
    a_ref, n_ref, h_ref, b_ref, mode_ref, sems = refs[10:]
    rows = n_ref.shape[0] // 4
    at = late[0].shape[0] - MODE_ROWS

    @pl.when(info[0] == s)
    def _():
        copies = (
            row_copies(early, 0, a_ref, sems.at[0])
            + row_copies(early, rows, n_ref, sems.at[1])
            + row_copies(late, 0, h_ref, sems.at[2])
            + row_copies(late, rows, b_ref, sems.at[3])
        )
        for i, pack in enumerate(late):
            modes = pack.at[pl.ds(at, MODE_ROWS), pl.ds(0, 256)]
            copies.append(pltpu.make_async_copy(modes, mode_ref.at[i], sems.at[4, i]))
        start_all(copies)
        wait_all(copies)
        width = n_ref.shape[1]
        out[pl.ds(2 * width, MODE_ROWS), :] = join_modes(mode_ref, width // 4)
        for c in range(width // 256):
            part = pl.ds(c * 256, 256)
            out[part, :] = dot_tn(h_ref[:, part], n_ref[...]).astype(BF)
            out[pl.ds(width + c * 256, 256), :] = dot_tn(a_ref[:, part], b_ref[...]).astype(BF)


def mlp_grads(s, info, early, late, rows):
    width = late[0].shape[1]
    ins = [(info, smem())]
    ins += [(value, anywhere()) for value in (*early, *late)]
    outs = [(shape((2 * width + MODE_ROWS, width), BF), vmem())]
    scratch = [pltpu.VMEM((4 * rows, width), BF)] * 4
    scratch += [pltpu.VMEM((4, MODE_ROWS, 256), BF), DMA((5, 4))]
    kernel = functools.partial(mlp_grads_kernel, s)
    return call(kernel, ins, outs, scratch, {}, cost(2_600_000_000, 10_000_000))[0]


def finish_kernel(*refs):
    info = refs[0]
    pairs = [refs[1 + 2 * s : 3 + 2 * s] for s in range(4)]
    main, lent, second, modes, held, mode_ref, sems = refs[9:]
    width = main.shape[0]
    half = width // 2
    here = pl.ds(pl.multiple_of(info[2] * half, half), half)
    there = pl.ds(pl.multiple_of((1 - info[2]) * half, half), half)

    def mode_copies(s):
        copies = []
        for i, value in enumerate(pairs[s]):
            rows = value.at[pl.ds(value.shape[0] - MODE_ROWS, MODE_ROWS)]
            which = info[2] if i == 0 else 1 - info[2]
            copies.append(pltpu.make_async_copy(rows, mode_ref.at[which], sems.at[4 + i]))
        return copies

    def halves(s):
        own, other = pairs[s]
        copies = mode_copies(s)
        for k in range(own.shape[0] // half):
            part = pl.ds(k * half, half)
            copies += [
                pltpu.make_async_copy(own.at[part], held.at[k, here], sems.at[2 * k]),
                pltpu.make_async_copy(other.at[part], held.at[k, there], sems.at[2 * k + 1]),
            ]
        start_all(copies)
        wait_all(copies)
        main[...] = held[0].astype(F32).T
        if own.shape[0] > width:
            lent[...] = held[1, :half]
            second[...] = held[1, half:].astype(F32)

    for s in (0, 2, 3):

        @pl.when(info[0] == s)
        def _():
            halves(s)

    @pl.when(info[0] == 1)
    def _():
        copies = mode_copies(1)
        for i, value in enumerate(pairs[1]):
            for k in range(2):
                part = value.at[pl.ds(k * width, width)]
                copies.append(
                    pltpu.make_async_copy(part, held.at[2 * i + k], sems.at[2 * i + k])
                )
        start_all(copies)
        wait_all(copies)
        main[...] = (held[0].astype(F32) + held[2].astype(F32)).T
        lent[...] = (held[1, :half].astype(F32) + held[3, :half].astype(F32)).astype(BF)
        second[...] = held[1, half:].astype(F32) + held[3, half:].astype(F32)

    columns = width // 4
    for i in range(2):
        value = mode_ref[i].astype(F32)
        value = value[0:3] + value[3:6]
        for j in range(4):
            modes[4 * i + j] = value[:, j * columns : (j + 1) * columns]


def finish(info, pairs, width):
    ins = [(info, smem())] + [(value, anywhere()) for pair in pairs for value in pair]
    outs = [
        (shape((width, width), F32), vmem()),
        (shape((width // 2, width), BF), vmem()),
        (shape((width // 2, width), F32), vmem()),
        (shape((8, 3, width // 4), F32), vmem()),
    ]
    scratch = [
        pltpu.VMEM((4, width, width), BF),
        pltpu.VMEM((2, MODE_ROWS, width), BF),
        DMA((6,)),
    ]
    return call(finish_kernel, ins, outs, scratch, {}, cost(10_000_000, 10_000_000))


def collect_kernel(sizes, sums_at, rows_at, *refs):
    info = refs[0]
    groups = []
    begin = 1
    for size in sizes:
        groups.append(refs[begin : begin + size])
        begin += size
    out, held, sems = refs[begin:]
    block = held.shape[1]
    for s in range(4):

        @pl.when(info[0] == s)
        def _():
            copies = [
                pltpu.make_async_copy(pack.at[pl.ds(row, block)], held.at[i], sems.at[i])
                for i, (pack, row) in enumerate(find_rows(groups[s], sums_at[s], rows_at[s]))
            ]
            start_all(copies)
            wait_all(copies)

    for i in range(4):
        out[slot_part(info, i)] = held[i].astype(F32)


def collect(info, groups, sums_at, rows_at, block):
    width = groups[0][0].shape[1]
    ins = [(info, smem())] + [(value, anywhere()) for group in groups for value in group]
    outs = [(shape((4, block, width), F32), vmem())]
    scratch = [pltpu.VMEM((4, block, width), BF), DMA((4,))]
    sizes = [len(group) for group in groups]
    kernel = functools.partial(collect_kernel, sizes, sums_at, rows_at)
    return call(kernel, ins, outs, scratch, {}, cost(1_000_000, 2_000_000))[0]


def flip(bits):
    return lambda i, n: i ^ bits


def later(value, *ended):
    return lax.optimization_barrier((value, ended))[0]


def my_half(chunk, dp_part):
    half = chunk.shape[0] // 2
    return lax.dynamic_slice_in_dim(chunk, dp_part % 2 * half, half, 0)


def trade(packs, which):
    others = [
        within(pack, "tensor", which, flip(bits)) for pack, bits in zip(packs[1:], FLIPS[1:])
    ]
    return (packs[0], *others)


def two_steps(s, info, sums, passed, rows):
    joined = add_passed(s, info, sums[2], passed, rows)
    near = within(sums[1], "tensor", (s,), flip(1))
    mirror = within(joined, "tensor", (s,), flip(3))
    return (sums[0], near, mirror)


def rope_tables(length):
    halfdim = HEAD_DIM // 2
    power = np.float32(-math.log(10000.0) * 2.0) * np.arange(halfdim, dtype=np.float32)
    inverse = np.exp(power / np.float32(HEAD_DIM))
    turn = np.arange(length, dtype=np.float32)[:, None] * inverse[None, :]
    cosine, sine = np.cos(turn), np.sin(turn)
    return np.tile(cosine, (1, 4)), np.tile(np.concatenate([-sine, sine], axis=1), (1, 2))


def body(clean, noise, times, flags, cotangent, w_main, w_half, w_mod):
    section = lax.axis_index("section")
    part = lax.axis_index("tensor")
    dp_part = lax.axis_index("dp")
    local_seqs, length, width = clean.shape
    columns = w_main.shape[3]
    halfdim = HEAD_DIM // 2

    def mine(values):
        return lax.dynamic_index_in_dim(values, part, 0, keepdims=False)

    theta = math.pi / 2 * (mine(times).astype(F32) + 1.0) / (TSTEPS + 1.0)
    noisy = jnp.cos(theta) * mine(clean).astype(F32) + jnp.sin(theta) * mine(noise).astype(F32)
    target = mine(cotangent)
    info = jnp.stack([section, part, dp_part % 2, mine(flags)]).astype(jnp.int32)

    halfwidth = width // 2
    freqs = jnp.exp(-math.log(10000.0) * jnp.arange(halfwidth, dtype=F32) / halfwidth)
    angles = times.astype(F32)[:, None] * freqs[None, :]
    temb = jnp.concatenate([jnp.sin(angles), jnp.cos(angles)], axis=1)
    mode_part = jnp.einsum("nd,dpc->pnc", temb, w_mod[0].astype(F32), precision=HIGHEST)
    mode_part = mode_part.reshape(3, 4 * columns)
    mode_high = lax.reduce_precision(mode_part, 8, 7)
    own_modes = jnp.concatenate(
        [mode_high, mode_part - mode_high, jnp.zeros((MODE_ROWS - 6, 4 * columns), F32)], axis=0
    ).astype(BF)

    main_local = w_main[0].reshape(width, 4 * columns)
    half_local = w_half[0]
    half_other = swap(half_local, "section", 1)
    second_local = jnp.concatenate([half_other, half_local], axis=0)
    odd = (1, 3)

    def odd_flip(value, axis, bits):
        return within(value, axis, odd, flip(bits))

    one = jnp.concatenate([my_half(main_local, dp_part), own_modes], axis=0)
    one_near = swap(one, "tensor", 1)
    one_mirror = swap(one, "tensor", 3)
    temb_turn = jnp.stack(
        [lax.dynamic_index_in_dim(temb, part ^ i, 0, keepdims=False) for i in FLIPS]
    )
    cosine, sine = (jnp.asarray(table) for table in rope_tables(length))
    one_near, (noisy, temb_turn, info, second_local) = lax.optimization_barrier(
        (one_near, (noisy, temb_turn, info, second_local))
    )
    one_near_x = swap(one_near, "dp", 1)
    one_far = swap(one_mirror, "tensor", 1)
    one_mirror_x = swap(one_mirror, "dp", 1)
    two_mirror = odd_flip(later(second_local, one_mirror), "tensor", 3)
    one_far_x = swap(one_far, "dp", 1)
    two_near = odd_flip(later(second_local, one_far), "tensor", 1)
    two_far = odd_flip(two_mirror, "tensor", 1)
    first = place(info, None, 0, [main_local], False)
    first = place(info, first, 1, [one_near, one_near_x], False)
    first = place(info, first, 2, [one_mirror, one_mirror_x], False)
    first = place(info, first, 3, [one_far, one_far_x], False)
    second = place(info, None, 0, [second_local], True)
    second = place(info, second, 1, [two_near], True)
    second = place(info, second, 2, [two_mirror], True)
    second = place(info, second, 3, [two_far], True)
    modes = pick_modes(info, [own_modes, one_near, one_mirror, one_far])
    temb_other = swap(temb_turn, "dp", 1)
    temb_pair = jnp.where(
        dp_part % 2 == 0,
        jnp.concatenate([temb_turn, temb_other]),
        jnp.concatenate([temb_other, temb_turn]),
    )

    def attend(s, base, arrived, keep):
        return attention_forward(s, info, base, arrived, modes, cosine, sine, first, keep)

    def feed(s, arrived, keep):
        return mlp_forward(s, info, arrived, modes, first, second, keep)

    def feed_back(s, grad, kept, keep):
        return mlp_back(s, info, grad, modes, kept, first, second, keep)

    def attend_back(s, grad, kept):
        return attention_back(s, info, grad, modes, cosine, sine, kept, first)

    def after(value, earlier):
        return lax.optimization_barrier((value, earlier))

    def across(value, s):
        return within(value, "dp", (s,), lambda i, n: i ^ 1)

    value = attend(0, noisy, None, False)[0]
    value = feed(1, section_hop(value, 0, 1), None)[0]
    value = attend(2, None, section_hop(value, 1, 1), False)[0]
    value = feed(3, section_hop(value, 2, 1), None)[0]
    guess = cyclic(value, "section", 1)

    kept_0 = attend(0, noisy, guess, True)
    kept_1 = feed(1, section_hop(kept_0[0], 0, 1), "packs")
    stream_2 = section_hop(kept_1[0], 1, 1)
    pack_1, stream_2 = after(kept_1[4:], stream_2)
    early_1 = trade(pack_1, (1,))
    kept_2 = attend(2, None, stream_2, True)
    kept_3 = feed(3, section_hop(kept_2[0], 2, 1), "message")

    back_3 = feed_back(3, target, kept_3, "message")
    grad_2 = section_hop(back_3[0], 3, -1)
    message_3, grad_2 = after(back_3[2], grad_2)
    other_3 = across(message_3, 3)
    back_2 = attend_back(2, grad_2, kept_2)
    grad_1 = lax.ppermute(back_2[0], "section", [(2, 1)])
    back_1 = feed_back(1, grad_1, kept_1, "packs")
    (message_2, hop_0), early_1 = after((back_2[2], back_1[0]), early_1)
    other_2 = across(message_2, 2)
    grad_0 = section_hop(hop_0, 1, -1)
    pack_1, grad_0 = after(back_1[2:], grad_0)
    late_1 = trade(pack_1, (1,))
    back_0 = attend_back(0, grad_0, kept_0)
    message_0, other_3 = after(back_0[2], other_3)
    other_0 = across(message_0, 0)
    other_2, message_0 = after(other_2, message_0)

    sums_3 = mlp_sums(3, info, kept_3, back_3, other_3)
    sums_3, late_1 = after(sums_3, late_1)
    part_3 = within(sums_3[3], "tensor", (3,), flip(1))
    sums_2 = attention_sums(2, info, kept_2, back_2, other_2)
    part_2 = within(sums_2[3], "tensor", (2,), flip(1))
    sums_0 = attention_sums(0, info, kept_0, back_0, other_0)
    group_0 = trade(sums_0, (0,))
    own_1 = mlp_grads(1, info, early_1, late_1, length)
    sums_3, part_3 = after(sums_3, part_3)
    group_3 = two_steps(3, info, sums_3, part_3, width)
    own_0 = total_parts(0, info, group_0, width // 2)
    sums_2, part_2, own_0 = lax.optimization_barrier((sums_2, part_2, own_0))
    group_2 = two_steps(2, info, sums_2, part_2, width // 2)
    own_3 = total_parts(3, info, group_3, width)
    own_2 = total_parts(2, info, group_2, width // 2)

    def other_pairs(value, s):
        size = lax.axis_size("dp")
        bit = 2
        while bit < size:
            partner = within(value, "dp", (s,), lambda i, n: i ^ bit)
            value = (value.astype(F32) + partner.astype(F32)).astype(BF)
            bit *= 2
        return value

    pairs = []
    for s, own in enumerate((own_0, own_1, own_2, own_3)):
        own = other_pairs(own, s)
        pairs.append((own, across(own, s)))
    block = length // 4
    sums_at = (width // 2, 2 * length, width // 2, width)
    groups = (group_0, early_1, group_2, group_3)
    outputs = collect(info, groups, sums_at, (0, 0, 0, 0), block)
    groups = (group_0, late_1, group_2, group_3)
    in_grads = collect(info, groups, sums_at, (block, 0, block, block), block)
    pairs, outputs, in_grads = lax.optimization_barrier((pairs, outputs, in_grads))
    main_total, lent, second_total, mode_grads = finish(info, pairs, width)
    returned = swap(lent, "section", 1)
    mode_total = jnp.einsum("nd,npc->dpc", temb_pair, mode_grads, precision=HIGHEST)
    bit = 2
    while bit < lax.axis_size("dp"):
        mode_total = mode_total + swap(mode_total, "dp", bit)
        bit *= 2
    main_total = main_total.reshape(1, width, 4, columns)
    returned, main_total, mode_total = lax.optimization_barrier(
        (returned, main_total, mode_total)
    )
    half_total = jnp.where(section % 2 == 0, returned.astype(F32), second_total)
    return (
        outputs[None],
        in_grads[None],
        main_total,
        half_total[None],
        mode_total[None],
    )


def solution(mesh):
    in_specs = (
        P("dp", None, None),
        P("dp", None, None),
        P("dp"),
        P("dp"),
        P("dp", None, None),
        P("section", None, None, "tensor"),
        P("section", "tensor", None),
        P("section", None, None, "tensor"),
    )
    out_specs = (
        P("section", "dp", "tensor", None),
        P("section", "dp", "tensor", None),
        P("section", None, None, "tensor"),
        P("section", "tensor", None),
        P("section", None, None, "tensor"),
    )
    return jax.shard_map(body, mesh=mesh, in_specs=in_specs, out_specs=out_specs, check_vma=False)
```

```python
import functools
import math

import jax
import jax.numpy as jnp
import numpy as np
from jax import lax
from jax.experimental import pallas as pl
from jax.experimental.pallas import tpu as pltpu
from jax.sharding import PartitionSpec as P

HEAD_DIM = 64
TSTEPS = 1000
EPSILON = 1e-05
HIGHEST = lax.Precision.HIGHEST
BF = jnp.bfloat16
F32 = jnp.float32
VMEM_BYTES = 32 * 1024 * 1024
WEIGHT_SIZE = 4 * 768 * 768
FLIPS = (0, 1, 3, 2)
GELU_C = math.sqrt(2.0 / math.pi)
GELU_A = 0.044715


def cyclic(value, axis, by):
    size = lax.axis_size(axis)
    return lax.ppermute(value, axis, [(i, (i + by) % size) for i in range(size)])


def swap(value, axis, bit):
    size = lax.axis_size(axis)
    return lax.ppermute(value, axis, [(i, i ^ bit) for i in range(size)])


def within(value, axis, which, route):
    size = lax.axis_size(axis)
    pairs = [(s * size + i, s * size + route(i, size)) for s in which for i in range(size)]
    return lax.ppermute(value, ("section", axis), pairs)


def section_hop(value, source, by):
    target = source + by
    if source // 2 == target // 2:
        return swap(value, "section", 1)
    return cyclic(value, "section", by)


def dot(left, right):
    return lax.dot_general(left, right, (((1,), (0,)), ((), ())), preferred_element_type=F32)


def dot_nt(left, right):
    return lax.dot_general(left, right, (((1,), (1,)), ((), ())), preferred_element_type=F32)


def dot_tn(left, right):
    return lax.dot_general(left, right, (((0,), (0,)), ((), ())), preferred_element_type=F32)


def standardize(stream):
    centred = stream - jnp.mean(stream, axis=-1, keepdims=True)
    variance = jnp.mean(centred * centred, axis=-1, keepdims=True)
    inverse = lax.rsqrt(variance + EPSILON)
    return centred * inverse, inverse


def swap_halves(block, first):
    return jnp.where(first, pltpu.roll(block, 96, 1), pltpu.roll(block, 32, 1))


def first_mask(rows):
    lane = lax.broadcasted_iota(jnp.int32, (rows, 128), 1)
    return (lane % HEAD_DIM) < HEAD_DIM // 2


def norm_back(normed_grad, stream, scale, grad):
    hat, inverse = standardize(stream)
    shift_grad = jnp.sum(normed_grad, axis=0, keepdims=True)
    scale_grad = jnp.sum(normed_grad * hat, axis=0, keepdims=True)
    hat_grad = normed_grad * (1.0 + scale)
    mean_one = jnp.mean(hat_grad, axis=-1, keepdims=True)
    mean_two = jnp.mean(hat_grad * hat, axis=-1, keepdims=True)
    in_grad = grad + inverse * (hat_grad - mean_one - hat * mean_two)
    return in_grad, shift_grad, scale_grad


def start_all(copies):
    for copy in copies:
        copy.start()


def wait_all(copies):
    for copy in copies:
        copy.wait()


def slot_rows(info, slot, block):
    return pl.ds(pl.multiple_of(slot_part(info, slot) * block, block), block)


def send_halves(send, source, target, at):
    for k in range(2):
        send(source.at[k], target.at[at + k])


def put_halves(ref, value):
    half = ref.shape[2]
    ref[0] = value[:, :half]
    ref[1] = value[:, half:]


MODE_ROWS = 16


def put_mode_grads(ref, values):
    joined = jnp.concatenate(values, axis=0)
    high = joined.astype(BF)
    rest = (joined - high.astype(F32)).astype(BF)
    filler = jnp.zeros((MODE_ROWS - 6, joined.shape[1]), BF)
    both = jnp.concatenate([high, rest, filler], axis=0)
    columns = both.shape[1] // 4
    ref[...] = jnp.zeros_like(ref)
    for part in range(4):
        ref[part, :, :columns] = both[:, part * columns : (part + 1) * columns]


def slot_part(info, slot):
    return info[1] ^ FLIPS[slot]


def send_rows(send, source, info, outs, second):
    block = source.shape[0] // 4
    for slot, out in enumerate(outs):
        target = out.at[pl.ds(block if second else 0, block)]
        send(source.at[slot_rows(info, slot, block)], target)


def row_outs(rows, width):
    return [(shape((rows // 2, width), BF), hbm())] * 4


def vmem():
    return pl.BlockSpec(memory_space=pltpu.VMEM)


def smem():
    return pl.BlockSpec(memory_space=pltpu.SMEM)


def hbm():
    return pl.BlockSpec(memory_space=pltpu.HBM)


def anywhere():
    return pl.BlockSpec(memory_space=pl.ANY)


def params(limit):
    return pltpu.CompilerParams(vmem_limit_bytes=limit)


def cost(flops, nbytes):
    return pl.CostEstimate(flops=flops, bytes_accessed=nbytes, transcendentals=0)


def call(kernel, ins, outs, scratch, aliases, estimate, limit=VMEM_BYTES):
    def placed(value, spec):
        if spec.memory_space is pltpu.HBM:
            return pltpu.with_memory_space_constraint(value, pltpu.HBM)
        if value.size >= WEIGHT_SIZE:
            return pltpu.with_memory_space_constraint(value, pltpu.VMEM)
        return value

    def result(value, spec):
        if spec.memory_space is pltpu.HBM:
            return pltpu.HBM(value.shape, value.dtype)
        if math.prod(value.shape) >= WEIGHT_SIZE:
            return pltpu.VMEM(value.shape, value.dtype)
        return value

    return pl.pallas_call(
        kernel,
        out_shape=[result(*pair) for pair in outs],
        in_specs=[spec for _, spec in ins],
        out_specs=[spec for _, spec in outs],
        scratch_shapes=scratch,
        input_output_aliases=aliases,
        compiler_params=params(limit),
        cost_estimate=estimate,
    )(*[placed(*pair) for pair in ins])


def shape(dims, dtype):
    return jax.ShapeDtypeStruct(dims, dtype)


DMA = pltpu.SemaphoreType.DMA


def place_kernel(slot, odd_only, *refs):
    info, pieces, (out, sems) = refs[0], refs[1:-3], refs[-2:]
    rows = out.shape[1] // len(pieces)

    def copy_all():
        copies = []
        for i, piece in enumerate(pieces):
            begin = 0
            if len(pieces) == 2:
                begin = pl.multiple_of((info[2] if i == 0 else 1 - info[2]) * rows, rows)
            target = out.at[slot, pl.ds(begin, rows)]
            copies.append(pltpu.make_async_copy(piece.at[pl.ds(0, rows)], target, sems.at[i]))
        start_all(copies)
        wait_all(copies)

    if odd_only:
        pl.when(info[0] % 2 == 1)(copy_all)
    else:
        copy_all()


def first_kernel(odd_only, info, piece, out, sems):
    place_kernel(0, odd_only, info, piece, None, out, sems)


def place(info, weight, slot, pieces, odd_only):
    ins = [(info, smem())] + [(piece, anywhere()) for piece in pieces]
    width = pieces[0].shape[1]
    aliases = {}
    if weight is None:
        kernel = functools.partial(first_kernel, odd_only)
    else:
        kernel = functools.partial(place_kernel, slot, odd_only)
        aliases = {len(ins): 0}
        ins.append((weight, vmem()))
    outs = [(shape((4, width, width), BF), vmem())]
    estimate = cost(1_000_000, 2_000_000)
    return call(kernel, ins, outs, [DMA((2,))], aliases, estimate, 1024 * 1024)[0]


def modes_kernel(*refs):
    info, pieces, (modes, mode_ref, sems) = refs[0], refs[1:5], refs[5:]
    copies = [
        pltpu.make_async_copy(
            piece.at[pl.ds(piece.shape[0] - MODE_ROWS, MODE_ROWS)], mode_ref.at[i], sems.at[i]
        )
        for i, piece in enumerate(pieces)
    ]
    start_all(copies)
    wait_all(copies)
    columns = modes.shape[1] // 4
    for part in range(4):
        bits = info[1] ^ part
        block = mode_ref[bits ^ (bits >> 1)].astype(F32)
        value = block[0:3] + block[3:6]
        chosen = jnp.zeros((3, columns), F32)
        for sequence in range(4):
            here = value[:, sequence * columns : (sequence + 1) * columns]
            chosen = jnp.where(info[1] == sequence, here, chosen)
        modes[:, part * columns : (part + 1) * columns] = chosen


def pick_modes(info, pieces):
    width = pieces[0].shape[1]
    ins = [(info, smem())] + [(piece, anywhere()) for piece in pieces]
    outs = [(shape((3, width), F32), vmem())]
    scratch = [pltpu.VMEM((4, MODE_ROWS, width), BF), DMA((4,))]
    estimate = cost(1_000_000, 1_000_000)
    return call(modes_kernel, ins, outs, scratch, {}, estimate, 2 * 1024 * 1024)[0]


def head_parts(heads, head):
    j, at = head // 3, head % 3 * HEAD_DIM
    return tuple(heads[j, :, at + 192 * i : at + 192 * i + HEAD_DIM] for i in range(3))


def attention_forward_kernel(s, has_base, has_arrived, keep, *refs):
    refs = list(refs)
    info = refs.pop(0)
    base = refs.pop(0) if has_base else None
    arrived = refs.pop(0) if has_arrived else None
    modes, cosine, sine, w = refs[:4]
    refs = refs[4:]
    result = refs.pop(0)
    if keep:
        heads_out, lse_out, attended_out, branch_out, stream_out = refs[:5]
        normed_out = refs[5]
        row_out = refs[6:10]
        refs = refs[10:]
    normed, branch, heads, attended_ref, scores_ref = refs[:5]
    if keep:
        stream_ref, lse, halves, osems = refs[5:]

    def load_stream():
        if not has_base:
            return arrived[...].astype(F32)
        if not has_arrived:
            return base[...]
        return base[...] + info[3].astype(F32) * arrived[...].astype(F32)

    @pl.when(info[0] == s)
    def _():
        outs = []

        def send(source, target):
            copy = pltpu.make_async_copy(source, target, osems.at[len(outs)])
            copy.start()
            outs.append(copy)

        stream = load_stream()
        hat, _ = standardize(stream)
        normed[...] = (hat * (1.0 + modes[1:2, :]) + modes[0:1, :]).astype(BF)
        rows = normed.shape[0]
        if keep:
            stream_ref[...] = stream
            send(stream_ref, stream_out)
            put_halves(halves, normed[...])
            send_halves(send, halves, normed_out, 0)
        first = first_mask(rows)
        low = lax.broadcasted_iota(jnp.int32, (rows, 128), 1) < HEAD_DIM
        for j in range(4):
            raw = dot(normed[...], w[j, :, :576])
            turned = []
            for unit in range(3):
                block = raw[:, unit * 128 : (unit + 1) * 128]
                block = block * cosine[...] + swap_halves(block, first) * sine[...]
                if unit == 0:
                    block = block * 0.125
                if unit == 1:
                    block = jnp.where(low, block * 0.125, block)
                turned.append(block)
            heads[j] = jnp.concatenate(turned + [raw[:, 384:576]], axis=1).astype(BF)
            if keep:
                send(heads.at[j], heads_out.at[j])
        for head in range(12):
            q, k, _ = head_parts(heads, head)
            scores_ref[head] = dot_nt(k, q)
        for j in range(4):
            pieces_t = [jnp.zeros((HEAD_DIM, rows), BF)]
            for head in range(3 * j, 3 * j + 3):
                _, _, v = head_parts(heads, head)
                scores = scores_ref[head]
                top = jnp.max(scores, axis=0, keepdims=True)
                raised = jnp.exp(scores - top)
                total = jnp.sum(raised, axis=0, keepdims=True)
                if keep:
                    lse[head : head + 1, :] = top + jnp.log(total)
                mixed = dot_tn(v, raised.astype(BF)) * (1.0 / total)
                pieces_t.append(mixed.astype(BF))
            attended_ref[j] = jnp.concatenate(pieces_t, axis=0).T
            if keep:
                send(attended_ref.at[j], attended_out.at[j])
        for j in range(4):
            part = dot_nt(attended_ref[j], w[j, :, 512:768])
            branch[...] = part if j == 0 else branch[...] + part
        result[...] = (load_stream() + modes[2:3, :] * branch[...]).astype(BF)
        if keep:
            send(lse, lse_out)
            send(branch, branch_out)
            send_rows(send, result, info, row_out, False)
            wait_all(outs)


def attention_forward(s, info, base, arrived, modes, cosine, sine, weights, keep):
    width = modes.shape[1]
    rows = cosine.shape[0]
    ins = [(info, smem())]
    for value in (base, arrived):
        if value is not None:
            ins.append((value, vmem()))
    ins += [(modes, vmem()), (cosine, vmem()), (sine, vmem()), (weights, vmem())]
    outs = [(shape((rows, width), BF), vmem())]
    scratch = [
        pltpu.VMEM((rows, width), BF),
        pltpu.VMEM((rows, width), F32),
        pltpu.VMEM((4, rows, 576), BF),
        pltpu.VMEM((4, rows, 256), BF),
        pltpu.VMEM((12, rows, rows), F32),
    ]
    if keep:
        outs += [
            (shape((4, rows, 576), BF), hbm()),
            (shape((12, rows), F32), hbm()),
            (shape((4, rows, 256), BF), hbm()),
            (shape((rows, width), F32), hbm()),
            (shape((rows, width), F32), hbm()),
            (shape((2, rows, width // 2), BF), hbm()),
        ]
        outs += row_outs(rows, width)
        scratch += [
            pltpu.VMEM((rows, width), F32),
            pltpu.VMEM((12, rows), F32),
            pltpu.VMEM((2, rows, width // 2), BF),
            DMA((19,)),
        ]
    kernel = functools.partial(
        attention_forward_kernel, s, base is not None, arrived is not None, keep
    )
    return call(kernel, ins, outs, scratch, {}, cost(2_000_000_000, 6_000_000))


def attention_back_kernel(s, *refs):
    info, grad, modes, cosine, sine, w = refs[:6]
    heads_in, lse_in, attended_in, branch_in, stream_in = refs[6:11]
    refs = refs[15:]
    in_grad, mode_out, message, pack_out, bg_out = refs[:5]
    row_out = refs[5:9]
    heads, lse, attended_ref, branch, stream, bg, ng, halves, pack_ref = refs[9:18]
    att_grad, scores_ref, prob_grads, probs_ref, ds_ref, raw_ref = refs[18:24]
    mode_ref, isems, osems = refs[24:]

    @pl.when(info[0] == s)
    def _():
        loads = []
        for source, target in (
            (heads_in, heads),
            (lse_in, lse),
            (attended_in, attended_ref),
            (stream_in, stream),
            (branch_in, branch),
        ):
            copy = pltpu.make_async_copy(source, target, isems.at[len(loads)])
            loads.append(copy)
        start_all(loads)
        outs = []

        def send(source, target):
            copy = pltpu.make_async_copy(source, target, osems.at[len(outs)])
            copy.start()
            outs.append(copy)

        g = grad[...].astype(F32)
        rows = g.shape[0]
        bg[...] = (modes[2:3, :] * g).astype(BF)
        put_halves(halves, bg[...])
        send_halves(send, halves, bg_out, 0)
        send_halves(send, halves, message, 0)
        first = first_mask(rows)
        for j in range(4):
            att_grad[j] = dot(bg[...], w[j, :, 512:768]).astype(BF)
        wait_all(loads[:2])
        for head in range(12):
            q, k, _ = head_parts(heads, head)
            scores_ref[head] = dot_nt(k, q)
        for head in range(12):
            _, _, v = head_parts(heads, head)
            at = 64 + head % 3 * HEAD_DIM
            prob_grads[head] = dot_nt(v, att_grad[head // 3, :, at : at + HEAD_DIM])
        for head in range(12):
            probs = jnp.exp(scores_ref[head] - lse[head : head + 1, :])
            inner = jnp.sum(prob_grads[head] * probs, axis=0, keepdims=True)
            probs_ref[head] = probs.astype(BF)
            ds_ref[head] = (probs * (prob_grads[head] - inner)).astype(BF)
        wait_all(loads[2:])
        for j in range(4):
            dq, dk, dv = [], [], []
            for head in range(3 * j, 3 * j + 3):
                q, k, _ = head_parts(heads, head)
                at = 64 + head % 3 * HEAD_DIM
                dv.append(dot(probs_ref[head], att_grad[j, :, at : at + HEAD_DIM]))
                dk.append(dot(ds_ref[head], q))
                dq.append(dot_tn(k, ds_ref[head]))
            dq_all = (jnp.concatenate(dq, axis=0) * 0.125).T
            both = jnp.concatenate([dq_all] + dk, axis=1)
            turned = []
            for unit in range(3):
                block = both[:, unit * 128 : (unit + 1) * 128]
                turned.append(block * cosine[...] - swap_halves(block, first) * sine[...])
            raw = jnp.concatenate(turned + dv, axis=1).astype(BF)
            raw_ref[j] = raw
            pack_ref[j, 0] = raw[:, :384]
            pack_ref[j, 1] = jnp.concatenate([raw[:, 384:576], attended_ref[j, :, 64:256]], axis=1)
            send(pack_ref.at[j, info[2]], pack_out.at[j])
            send(pack_ref.at[j, 1 - info[2]], message.at[2 + j])
        for j in range(4):
            part = dot_nt(raw_ref[j], w[j, :, :576])
            ng[...] = part if j == 0 else ng[...] + part
        total, shift_grad, scale_grad = norm_back(
            ng[...], stream[...], modes[1:2, :], grad[...].astype(F32)
        )
        in_grad[...] = total.astype(BF)
        send_rows(send, in_grad, info, row_out, True)
        gate_grad = jnp.sum(grad[...].astype(F32) * branch[...], axis=0, keepdims=True)
        put_mode_grads(mode_ref, (shift_grad, scale_grad, gate_grad))
        send(mode_ref, mode_out)
        wait_all(outs)


def attention_back(s, info, grad, modes, cosine, sine, kept, weights, chain):
    rows, width = grad.shape
    ins = [(info, smem()), (grad, vmem()), (modes, vmem()), (cosine, vmem()), (sine, vmem())]
    ins += [(weights, vmem())]
    ins += [(value, hbm()) for value in kept[1:6]]
    outs = [
        (shape((rows, width), BF), vmem()),
        (shape((4, MODE_ROWS, 256), BF), hbm()),
        (shape((6, rows, width // 2), BF), hbm()),
        (shape((4, rows, width // 2), BF), hbm()),
        (shape((2, rows, width // 2), BF), hbm()),
    ]
    outs += row_outs(rows, width)
    aliases = {len(ins) + i: len(outs) - 4 + i for i in range(4)}
    ins += [(value, hbm()) for value in chain]
    scratch = [
        pltpu.VMEM((4, rows, 576), BF),
        pltpu.VMEM((12, rows), F32),
        pltpu.VMEM((4, rows, 256), BF),
        pltpu.VMEM((rows, width), F32),
        pltpu.VMEM((rows, width), F32),
        pltpu.VMEM((rows, width), BF),
        pltpu.VMEM((rows, width), F32),
        pltpu.VMEM((2, rows, width // 2), BF),
        pltpu.VMEM((4, 2, rows, width // 2), BF),
        pltpu.VMEM((4, rows, 256), BF),
        pltpu.VMEM((12, rows, rows), F32),
        pltpu.VMEM((12, rows, rows), F32),
        pltpu.VMEM((12, rows, rows), BF),
        pltpu.VMEM((12, rows, rows), BF),
        pltpu.VMEM((4, rows, 576), BF),
        pltpu.VMEM((4, MODE_ROWS, 256), BF),
        DMA((5,)),
        DMA((17,)),
    ]
    kernel = functools.partial(attention_back_kernel, s)
    return call(kernel, ins, outs, scratch, aliases, cost(3_000_000_000, 10_000_000))


def mlp_forward_kernel(s, keep, *refs):
    info, arrived, modes, w1, w2 = refs[:5]
    refs = refs[5 + (4 if keep == "message" else 0) :]
    result = refs[0]
    refs = refs[1:]
    if keep:
        slope_out, branch_out, stream_out = refs[:3]
        refs = refs[3:]
    if keep == "packs":
        packs = refs[:4]
        refs = refs[4:]
    if keep == "message":
        act_out, normed_out, message = refs[:3]
        row_out = refs[3:7]
        refs = refs[7:]
    normed, branch = refs[:2]
    if keep:
        act_ref, slope_ref, halves, osems = refs[2:]

    @pl.when(info[0] == s)
    def _():
        outs = []

        def send(source, target):
            copy = pltpu.make_async_copy(source, target, osems.at[len(outs)])
            copy.start()
            outs.append(copy)

        hat, _ = standardize(arrived[...].astype(F32))
        normed[...] = (hat * (1.0 + modes[1:2, :]) + modes[0:1, :]).astype(BF)
        rows = normed.shape[0]
        if keep:
            send(arrived, stream_out)
        if keep == "packs":
            for pack in packs[:3]:
                send(normed, pack.at[pl.ds(0, rows)])
        if keep == "message":
            put_halves(halves, normed[...])
            send_halves(send, halves, normed_out, 0)
            send_halves(send, halves, message, 0)
        hidden_next = dot(normed[...], w1[0])
        for j in range(4):
            hidden = hidden_next
            if j < 3:
                hidden_next = dot(normed[...], w1[j + 1])
            square = hidden * hidden
            bend = jnp.tanh(GELU_C * hidden * (1.0 + GELU_A * square))
            act = (0.5 * hidden * (1.0 + bend)).astype(BF)
            if keep:
                slope = 0.5 * (1.0 + bend) + (0.5 * GELU_C) * hidden * (1.0 - bend * bend) * (
                    1.0 + (3.0 * GELU_A) * square
                )
                slope_ref[j] = slope.astype(BF)
                send(slope_ref.at[j], slope_out.at[j])
            if keep == "packs":
                act_ref[j] = act
                send(act_ref.at[j], packs[j].at[pl.ds(rows if j < 3 else 0, rows)])
            if keep == "message":
                put_halves(act_ref.at[j], act)
                send(act_ref.at[j, info[2]], act_out.at[j])
                send(act_ref.at[j, 1 - info[2]], message.at[8 + j])
            part = dot(act, w2[j])
            branch[...] = part if j == 0 else branch[...] + part
        result[...] = (arrived[...].astype(F32) + modes[2:3, :] * branch[...]).astype(BF)
        if keep:
            send(branch, branch_out)
            block = rows // 4
            if keep == "packs":
                for slot, pack in enumerate(packs):
                    target = pack.at[pl.ds(pack.shape[0] - block, block)]
                    send(result.at[slot_rows(info, slot, block)], target)
            else:
                send_rows(send, result, info, row_out, False)
            wait_all(outs)


def mlp_forward(s, info, arrived, modes, first, second, keep, chain=None):
    rows, width = arrived.shape
    ins = [(info, smem()), (arrived, vmem()), (modes, vmem())]
    ins += [(first, vmem()), (second, vmem())]
    outs = [(shape((rows, width), BF), vmem())]
    scratch = [
        pltpu.VMEM((rows, width), BF),
        pltpu.VMEM((rows, width), F32),
    ]
    if keep:
        outs += [
            (shape((4, rows, width), BF), hbm()),
            (shape((rows, width), F32), hbm()),
            (shape((rows, width), BF), hbm()),
        ]
        if keep == "packs":
            outs += [(shape((2 * rows + rows // 4, width), BF), hbm())] * 3
            outs += [(shape((rows + rows // 4, width), BF), hbm())]
        else:
            outs += [
                (shape((4, rows, width // 2), BF), hbm()),
                (shape((2, rows, width // 2), BF), hbm()),
                (shape((12, rows, width // 2), BF), hbm()),
            ]
            outs += row_outs(rows, width)
        wide = (4, rows, width) if keep == "packs" else (4, 2, rows, width // 2)
        scratch += [
            pltpu.VMEM(wide, BF),
            pltpu.VMEM((4, rows, width), BF),
            pltpu.VMEM((2, rows, width // 2), BF),
            DMA((24,)),
        ]
    aliases = {}
    if keep == "message":
        aliases = {len(ins) + i: len(outs) - 4 + i for i in range(4)}
        ins += [(value, hbm()) for value in chain]
    kernel = functools.partial(mlp_forward_kernel, s, keep)
    return call(kernel, ins, outs, scratch, aliases, cost(2_400_000_000, 10_000_000))


def mlp_back_kernel(s, keep, *refs):
    info, grad, modes, slope_in, branch_in, stream_in, w1, w2 = refs[:8]
    if keep == "packs":
        in_grad, mode_out = refs[8:10]
        packs = refs[10:14]
        refs = refs[14:]
    else:
        in_grad, mode_out, message, hidden_out, bg_out = refs[13:18]
        row_out = refs[18:22]
        refs = refs[22:]
    slope, branch, stream, bg, ng, halves, hidden_ref = refs[:7]
    mode_ref, isems, osems = refs[7:]

    @pl.when(info[0] == s)
    def _():
        loads = [
            pltpu.make_async_copy(source, target, isems.at[i])
            for i, (source, target) in enumerate(
                ((slope_in, slope), (stream_in, stream), (branch_in, branch))
            )
        ]
        start_all(loads)
        outs = []

        def send(source, target):
            copy = pltpu.make_async_copy(source, target, osems.at[len(outs)])
            copy.start()
            outs.append(copy)

        g = grad[...].astype(F32)
        rows = g.shape[0]
        bg[...] = (modes[2:3, :] * g).astype(BF)
        if keep == "packs":
            for pack in packs[:3]:
                send(bg, pack.at[pl.ds(0, rows)])
        else:
            put_halves(halves, bg[...])
            send_halves(send, halves, bg_out, 0)
            send_halves(send, halves, message, 2)
        act_grad_next = dot_nt(bg[...], w2[0])
        for j in range(4):
            act_grad = act_grad_next
            if j < 3:
                act_grad_next = dot_nt(bg[...], w2[j + 1])
            if j == 0:
                loads[0].wait()
            hidden_grad = (act_grad * slope[j].astype(F32)).astype(BF)
            if keep == "packs":
                hidden_ref[j] = hidden_grad
                send(hidden_ref.at[j], packs[j].at[pl.ds(rows if j < 3 else 0, rows)])
            else:
                put_halves(hidden_ref.at[j], hidden_grad)
                send(hidden_ref.at[j, info[2]], hidden_out.at[j])
                send(hidden_ref.at[j, 1 - info[2]], message.at[4 + j])
            part = dot_nt(hidden_grad, w1[j])
            ng[...] = part if j == 0 else ng[...] + part
        wait_all(loads[1:])
        total, shift_grad, scale_grad = norm_back(
            ng[...], stream[...].astype(F32), modes[1:2, :], grad[...].astype(F32)
        )
        in_grad[...] = total.astype(BF)
        block = rows // 4
        if keep == "packs":
            for slot, pack in enumerate(packs):
                at = pack.shape[0] - MODE_ROWS - block
                send(in_grad.at[slot_rows(info, slot, block)], pack.at[pl.ds(at, block)])
        else:
            send_rows(send, in_grad, info, row_out, True)
        gate_grad = jnp.sum(grad[...].astype(F32) * branch[...], axis=0, keepdims=True)
        put_mode_grads(mode_ref, (shift_grad, scale_grad, gate_grad))
        send(mode_ref, mode_out)
        if keep == "packs":
            for slot, pack in enumerate(packs):
                send(
                    mode_ref.at[slot_part(info, slot)],
                    pack.at[pl.ds(pack.shape[0] - MODE_ROWS, MODE_ROWS), pl.ds(0, 256)],
                )
        wait_all(outs)


def mlp_back(s, info, grad, modes, kept, first, second, keep, chain=None):
    rows, width = grad.shape
    ins = [(info, smem()), (grad, vmem()), (modes, vmem())]
    ins += [(value, hbm()) for value in kept[1:4]]
    ins += [(first, vmem()), (second, vmem())]
    outs = [
        (shape((rows, width), BF), vmem()),
        (shape((4, MODE_ROWS, 256), BF), hbm()),
    ]
    aliases = {}
    if keep == "packs":
        rest = rows // 4 + MODE_ROWS
        outs += [(shape((2 * rows + rest, width), BF), hbm())] * 3
        outs += [(shape((rows + rest, width), BF), hbm())]
    else:
        aliases = {len(ins): 2}
        ins += [(kept[6], hbm())]
        outs += [
            (shape(kept[6].shape, BF), hbm()),
            (shape((4, rows, width // 2), BF), hbm()),
            (shape((2, rows, width // 2), BF), hbm()),
        ]
        outs += row_outs(rows, width)
        aliases.update({len(ins) + i: len(outs) - 4 + i for i in range(4)})
        ins += [(value, hbm()) for value in chain]
    wide = (4, rows, width) if keep == "packs" else (4, 2, rows, width // 2)
    scratch = [
        pltpu.VMEM((4, rows, width), BF),
        pltpu.VMEM((rows, width), F32),
        pltpu.VMEM((rows, width), BF),
        pltpu.VMEM((rows, width), BF),
        pltpu.VMEM((rows, width), F32),
        pltpu.VMEM((2, rows, width // 2), BF),
        pltpu.VMEM(wide, BF),
        pltpu.VMEM((4, MODE_ROWS, 256), BF),
        DMA((3,)),
        DMA((18,)),
    ]
    kernel = functools.partial(mlp_back_kernel, s, keep)
    return call(kernel, ins, outs, scratch, aliases, cost(2_400_000_000, 12_000_000))


def row_copies(group, row, target, sems):
    rows = target.shape[0] // 4
    return [
        pltpu.make_async_copy(
            pack.at[pl.ds(row, rows)], target.at[pl.ds(i * rows, rows)], sems.at[i]
        )
        for i, pack in enumerate(group)
    ]


def rest_to_slots(slots, row_ref, mode_ref, outs, at, info, sems):
    copies = []
    for slot, out in zip(slots, outs):
        row = at
        if row_ref is not None:
            block = row_ref.shape[1]
            target = out.at[pl.ds(row, block)]
            copies.append(pltpu.make_async_copy(row_ref.at[slot], target, sems.at[0, slot]))
            row += block
        target = out.at[pl.ds(row, MODE_ROWS), pl.ds(0, 256)]
        copies.append(
            pltpu.make_async_copy(mode_ref.at[slot_part(info, slot)], target, sems.at[1, slot])
        )
    return copies


def two_sequences(own, other, at, target, sems, which):
    rows = own.shape[1]
    copies = []
    for j in which:
        copies += [
            pltpu.make_async_copy(own.at[j], target.at[j, pl.ds(0, rows)], sems.at[j, 0]),
            pltpu.make_async_copy(
                other.at[at + j], target.at[j, pl.ds(rows, rows)], sems.at[j, 1]
            ),
        ]
    return copies


def attention_sums_kernel(s, slots, with_rows, *refs):
    info, normed_in, bg_in, pack_in, other_normed, other, mode_in = refs[:7]
    row_in = refs[7 : 7 + with_rows]
    refs = refs[7 + with_rows :]
    outs = refs[: len(slots)]
    refs = refs[len(slots) :]
    n_ref, b_ref, p_ref, held, row_ref, mode_ref = refs[:6]
    nsems, bsems, psems, osems, lsems, rsems = refs[6:]
    half = held.shape[1]

    @pl.when(info[0] == s)
    def _():
        loads = [pltpu.make_async_copy(mode_in, mode_ref, lsems.at[4])]
        for i, value in enumerate(row_in):
            loads.append(pltpu.make_async_copy(value, row_ref.at[i], lsems.at[i]))
        rows = row_ref if with_rows else None
        moves = rest_to_slots(slots, rows, mode_ref, outs, half, info, rsems)
        copies = (
            two_sequences(normed_in, other_normed, 0, n_ref, nsems, range(2))
            + two_sequences(pack_in, other, 2, p_ref, psems, slots)
            + two_sequences(bg_in, other, 0, b_ref, bsems, range(2))
        )
        start_all(copies + loads)
        wait_all(copies + loads)
        start_all(moves)
        tokens = jnp.concatenate([n_ref[0], n_ref[1]], axis=1)
        branch = jnp.concatenate([b_ref[0], b_ref[1]], axis=1)
        for j, out in zip(slots, outs):
            held[j] = dot_tn(p_ref[j], tokens).astype(BF)

            @pl.when(info[2] == 1)
            def _():
                outward = dot_tn(p_ref[j, :, 128:], branch)
                held[j, half // 2 :, :] = outward[half // 2 - 128 :].astype(BF)

            copy = pltpu.make_async_copy(held.at[j], out.at[pl.ds(0, half)], osems.at[j])
            copy.start()
            moves.append(copy)
        wait_all(moves)


def attention_sums(s, info, kept, back, other, slots, with_rows):
    rows = kept[6].shape[1]
    half = kept[6].shape[2]
    width = 2 * half
    ins = [(info, smem())]
    ins += [
        (kept[6], hbm()),
        (back[4], hbm()),
        (back[3], hbm()),
        (other[0], anywhere()),
        (other[1], anywhere()),
        (back[1], hbm()),
    ]
    rest = MODE_ROWS
    if with_rows:
        ins += [(value, hbm()) for value in back[5:9]]
        rest += rows // 2
    outs = [(shape((half + rest, width), BF), hbm())] * len(slots)
    scratch = [
        pltpu.VMEM((2, 2 * rows, half), BF),
        pltpu.VMEM((2, 2 * rows, half), BF),
        pltpu.VMEM((4, 2 * rows, half), BF),
        pltpu.VMEM((4, half, width), BF),
        pltpu.VMEM((4, rows // 2, width), BF),
        pltpu.VMEM((4, MODE_ROWS, 256), BF),
        DMA((2, 2)),
        DMA((2, 2)),
        DMA((4, 2)),
        DMA((4,)),
        DMA((5,)),
        DMA((2, 4)),
    ]
    kernel = functools.partial(attention_sums_kernel, s, slots, 4 if with_rows else 0)
    return call(kernel, ins, outs, scratch, {}, cost(1_300_000_000, 8_000_000))


def mlp_sums_kernel(s, slots, *refs):
    info, normed_in, bg_in, hidden_in, act_in, other, mode_in = refs[:7]
    outs = refs[7 : 7 + len(slots)]
    refs = refs[7 + len(slots) :]
    n_ref, b_ref, h_ref, a_ref, held, mode_ref = refs[:6]
    nsems, bsems, hsems, asems, osems, lsems, rsems = refs[6:]
    half = held.shape[1] // 2

    @pl.when(info[0] == s)
    def _():
        loads = [pltpu.make_async_copy(mode_in, mode_ref, lsems.at[4])]
        moves = rest_to_slots(slots, None, mode_ref, outs, 2 * half, info, rsems)
        left = two_sequences(normed_in, other, 0, n_ref, nsems, range(2))
        left += two_sequences(hidden_in, other, 4, h_ref, hsems, slots)
        right = two_sequences(bg_in, other, 2, b_ref, bsems, range(2))
        right += two_sequences(act_in, other, 8, a_ref, asems, slots)
        start_all(left + right + loads)
        wait_all(left)
        tokens = jnp.concatenate([n_ref[0], n_ref[1]], axis=1)
        for j in slots:
            held[j, :half] = dot_tn(h_ref[j], tokens).astype(BF)
        wait_all(right + loads)
        start_all(moves)
        branch = jnp.concatenate([b_ref[0], b_ref[1]], axis=1)
        for j, out in zip(slots, outs):
            held[j, half:] = dot_tn(a_ref[j], branch).astype(BF)
            copy = pltpu.make_async_copy(held.at[j], out.at[pl.ds(0, 2 * half)], osems.at[j])
            copy.start()
            moves.append(copy)
        wait_all(moves)


def mlp_sums(s, info, kept, back, other, slots):
    rows = kept[5].shape[1]
    half = kept[5].shape[2]
    width = 2 * half
    ins = [(info, smem())]
    ins += [
        (kept[5], hbm()),
        (back[4], hbm()),
        (back[3], hbm()),
        (kept[4], hbm()),
        (other, anywhere()),
        (back[1], hbm()),
    ]
    outs = [(shape((width + MODE_ROWS, width), BF), hbm())] * len(slots)
    scratch = [
        pltpu.VMEM((2, 2 * rows, half), BF),
        pltpu.VMEM((2, 2 * rows, half), BF),
        pltpu.VMEM((4, 2 * rows, half), BF),
        pltpu.VMEM((4, 2 * rows, half), BF),
        pltpu.VMEM((4, width, width), BF),
        pltpu.VMEM((4, MODE_ROWS, 256), BF),
        DMA((2, 2)),
        DMA((2, 2)),
        DMA((4, 2)),
        DMA((4, 2)),
        DMA((4,)),
        DMA((5,)),
        DMA((2, 4)),
    ]
    kernel = functools.partial(mlp_sums_kernel, s, slots)
    return call(kernel, ins, outs, scratch, {}, cost(2_600_000_000, 12_000_000))


def add_passed_kernel(s, *refs):
    info, own, passed, out, held, total, sems = refs
    rows = total.shape[0]
    rest = own.shape[0] - rows

    @pl.when(info[0] == s)
    def _():
        copies = [
            pltpu.make_async_copy(value, held.at[i], sems.at[i])
            for i, value in enumerate((own, passed))
        ]
        start_all(copies)
        wait_all(copies)
        moves = [
            pltpu.make_async_copy(
                held.at[i, pl.ds(rows, rest)], out.at[pl.ds(rows + i * rest, rest)], sems.at[2 + i]
            )
            for i in range(2)
        ]
        start_all(moves)
        total[...] = (held[0, :rows].astype(F32) + held[1, :rows].astype(F32)).astype(BF)
        moves.append(pltpu.make_async_copy(total, out.at[pl.ds(0, rows)], sems.at[4]))
        moves[2].start()
        wait_all(moves)


def add_passed(s, info, own, passed, rows):
    length, width = own.shape
    ins = [(info, smem()), (own, hbm()), (passed, anywhere())]
    outs = [(shape((2 * length - rows, width), BF), hbm())]
    scratch = [pltpu.VMEM((2, length, width), BF), pltpu.VMEM((rows, width), BF), DMA((5,))]
    kernel = functools.partial(add_passed_kernel, s)
    return call(kernel, ins, outs, scratch, {}, cost(10_000_000, 5_000_000))[0]


def rest_at(group, rows, at):
    rest = group[0].shape[0] - rows
    own, near, mirror = group
    return [(own, rows + at), (near, rows + at), (mirror, rows + at), (mirror, rows + rest + at)]


def join_modes(held, columns):
    return jnp.concatenate([held[i, :, :columns] for i in range(4)], axis=1)


def total_kernel(s, at, *refs):
    info = refs[0]
    parts = refs[1:-4]
    out, held, mode_ref, sems = refs[-4:]
    rows = held.shape[1]

    @pl.when(info[0] == s)
    def _():
        copies = []
        for i, part in enumerate(parts):
            copies.append(
                pltpu.make_async_copy(part.at[pl.ds(0, rows)], held.at[i], sems.at[0, i])
            )
        for i, (part, row) in enumerate(rest_at(parts, rows, at)):
            modes = part.at[pl.ds(row, MODE_ROWS), pl.ds(0, 256)]
            copies.append(pltpu.make_async_copy(modes, mode_ref.at[i], sems.at[1, i]))
        start_all(copies)
        wait_all(copies)
        total = held[0].astype(F32)
        for i in range(1, len(parts)):
            total = total + held[i].astype(F32)
        out[:rows] = total.astype(BF)
        out[rows:] = join_modes(mode_ref, out.shape[1] // 4)


def total_parts(s, info, group, rows):
    width = group[0].shape[1]
    at = group[0].shape[0] - MODE_ROWS - rows
    ins = [(info, smem())] + [(value, anywhere()) for value in group]
    outs = [(shape((rows + MODE_ROWS, width), BF), vmem())]
    scratch = [
        pltpu.VMEM((len(group), rows, width), BF),
        pltpu.VMEM((4, MODE_ROWS, 256), BF),
        DMA((2, 4)),
    ]
    kernel = functools.partial(total_kernel, s, at)
    return call(kernel, ins, outs, scratch, {}, cost(10_000_000, 5_000_000))[0]


def mlp_grads_kernel(s, *refs):
    info = refs[0]
    early, late = refs[1:6], refs[6:11]
    out = refs[11]
    a_ref, n_ref, h_ref, b_ref, mode_ref, sems = refs[12:]
    rows = n_ref.shape[0] // 4

    def places(group):
        shared = [(pack, 0) for pack in (*group[:3], group[4])]
        columns = [(pack, rows) for pack in group[:3]] + [(group[3], 0)]
        return shared, columns

    @pl.when(info[0] == s)
    def _():
        copies = []
        for k, (target, wanted) in enumerate(
            zip((n_ref, a_ref, b_ref, h_ref), places(early) + places(late))
        ):
            for i, (pack, row) in enumerate(wanted):
                copies.append(
                    pltpu.make_async_copy(
                        pack.at[pl.ds(row, rows)], target.at[pl.ds(i * rows, rows)], sems.at[k, i]
                    )
                )
        for i, pack in enumerate(late[:4]):
            modes = pack.at[pl.ds(pack.shape[0] - MODE_ROWS, MODE_ROWS), pl.ds(0, 256)]
            copies.append(pltpu.make_async_copy(modes, mode_ref.at[i], sems.at[4, i]))
        start_all(copies)
        wait_all(copies)
        width = n_ref.shape[1]
        out[pl.ds(2 * width, MODE_ROWS), :] = join_modes(mode_ref, width // 4)
        for c in range(width // 256):
            part = pl.ds(c * 256, 256)
            out[part, :] = dot_tn(h_ref[:, part], n_ref[...]).astype(BF)
            out[pl.ds(width + c * 256, 256), :] = dot_tn(a_ref[:, part], b_ref[...]).astype(BF)


def mlp_grads(s, info, early, late, rows):
    width = late[0].shape[1]
    ins = [(info, smem())]
    ins += [(value, anywhere()) for value in (*early, *late)]
    outs = [(shape((2 * width + MODE_ROWS, width), BF), vmem())]
    scratch = [pltpu.VMEM((4 * rows, width), BF)] * 4
    scratch += [pltpu.VMEM((4, MODE_ROWS, 256), BF), DMA((5, 4))]
    kernel = functools.partial(mlp_grads_kernel, s)
    return call(kernel, ins, outs, scratch, {}, cost(2_600_000_000, 10_000_000))[0]


def finish_kernel(*refs):
    info = refs[0]
    pairs = [refs[1 + 2 * s : 3 + 2 * s] for s in range(4)]
    main, lent, second_out, modes, held, mode_ref, second, sems = refs[9:]
    width = main.shape[0]
    half = width // 2
    here = pl.ds(pl.multiple_of(info[2] * half, half), half)
    there = pl.ds(pl.multiple_of((1 - info[2]) * half, half), half)

    def mode_copies(s):
        copies = []
        for i, value in enumerate(pairs[s]):
            rows = value.at[pl.ds(value.shape[0] - MODE_ROWS, MODE_ROWS)]
            which = info[2] if i == 0 else 1 - info[2]
            copies.append(pltpu.make_async_copy(rows, mode_ref.at[which], sems.at[4 + i]))
        return copies

    def halves(s):
        own, other = pairs[s]
        copies = mode_copies(s)
        for k in range(own.shape[0] // half):
            part = pl.ds(k * half, half)
            copies += [
                pltpu.make_async_copy(own.at[part], held.at[k, here], sems.at[2 * k]),
                pltpu.make_async_copy(other.at[part], held.at[k, there], sems.at[2 * k + 1]),
            ]
        start_all(copies)
        wait_all(copies)
        main[...] = held[0].astype(F32).T
        if own.shape[0] > width:
            lent[...] = held[1, :half]
            second[...] = held[1, half:].astype(F32)
            copy = pltpu.make_async_copy(second, second_out, sems.at[6])
            copy.start()
            copy.wait()

    for s in (0, 2, 3):

        @pl.when(info[0] == s)
        def _():
            halves(s)

    @pl.when(info[0] == 1)
    def _():
        copies = mode_copies(1)
        for i, value in enumerate(pairs[1]):
            for k in range(2):
                part = value.at[pl.ds(k * width, width)]
                copies.append(
                    pltpu.make_async_copy(part, held.at[2 * i + k], sems.at[2 * i + k])
                )
        start_all(copies)
        wait_all(copies)
        main[...] = (held[0].astype(F32) + held[2].astype(F32)).T
        lent[...] = (held[1, :half].astype(F32) + held[3, :half].astype(F32)).astype(BF)
        second[...] = held[1, half:].astype(F32) + held[3, half:].astype(F32)
        copy = pltpu.make_async_copy(second, second_out, sems.at[6])
        copy.start()
        copy.wait()

    columns = width // 4
    for i in range(2):
        value = mode_ref[i].astype(F32)
        value = value[0:3] + value[3:6]
        for j in range(4):
            modes[4 * i + j] = value[:, j * columns : (j + 1) * columns]


def finish(info, pairs, width):
    ins = [(info, smem())] + [(value, anywhere()) for pair in pairs for value in pair]
    outs = [
        (shape((width, width), F32), vmem()),
        (shape((width // 2, width), BF), vmem()),
        (shape((width // 2, width), F32), hbm()),
        (shape((8, 3, width // 4), F32), vmem()),
    ]
    scratch = [
        pltpu.VMEM((4, width, width), BF),
        pltpu.VMEM((2, MODE_ROWS, width), BF),
        pltpu.VMEM((width // 2, width), F32),
        DMA((7,)),
    ]
    return call(finish_kernel, ins, outs, scratch, {}, cost(10_000_000, 10_000_000))


def collect_kernel(rows_at, *refs):
    info = refs[0]
    outs = refs[-6:-4]
    held, wide, sems, osems = refs[-4:]
    block = held.shape[2]
    begin = 1
    for sections, rows in rows_at:
        group = refs[begin : begin + 8]
        begin += 8
        chosen = info[0] == sections[0]
        for s in sections[1:]:
            chosen = jnp.logical_or(chosen, info[0] == s)

        @pl.when(chosen)
        def _():
            copies = []
            for i, (pack, row) in enumerate(zip(group, rows)):
                copies.append(
                    pltpu.make_async_copy(
                        pack.at[pl.ds(row, block)], held.at[i // 4, i % 4], sems.at[i]
                    )
                )
            start_all(copies)
            wait_all(copies)
            moves = []
            for k in range(2):
                for i in range(4):
                    wide[k, slot_part(info, i)] = held[k, i].astype(F32)
                moves.append(pltpu.make_async_copy(wide.at[k], outs[k], osems.at[k]))
                moves[k].start()
            wait_all(moves)


def collect(info, groups, block, older):
    ins = [(info, smem())]
    rows_at = []
    for sections, places in groups:
        ins += [(value, anywhere()) for value, _ in places]
        rows_at.append((sections, tuple(row for _, row in places)))
    width = groups[0][1][0][0].shape[1]
    outs = [(shape((4, block, width), F32), hbm())] * 2
    aliases = {}
    if older is not None:
        aliases = {len(ins) + i: i for i in range(2)}
        ins += [(value, hbm()) for value in older]
    scratch = [
        pltpu.VMEM((2, 4, block, width), BF),
        pltpu.VMEM((2, 4, block, width), F32),
        DMA((8,)),
        DMA((2,)),
    ]
    kernel = functools.partial(collect_kernel, tuple(rows_at))
    return call(kernel, ins, outs, scratch, aliases, cost(1_000_000, 2_000_000))


def half_kernel(info, returned, second, out, wide, sem):
    @pl.when(info[0] % 2 == 0)
    def _():
        wide[...] = returned[...].astype(F32)
        copy = pltpu.make_async_copy(wide, out, sem)
        copy.start()
        copy.wait()


def choose_half(info, returned, second):
    ins = [(info, smem()), (returned, vmem()), (second, hbm())]
    outs = [(shape(second.shape, F32), hbm())]
    scratch = [pltpu.VMEM(second.shape, F32), DMA]
    return call(half_kernel, ins, outs, scratch, {2: 0}, cost(1_000_000, 2_000_000))[0]


def flip(bits):
    return lambda i, n: i ^ bits


def later(value, *ended):
    return lax.optimization_barrier((value, ended))[0]


def my_half(chunk, dp_part):
    half = chunk.shape[0] // 2
    return lax.dynamic_slice_in_dim(chunk, dp_part % 2 * half, half, 0)


def trade(packs, which):
    others = [
        within(pack, "tensor", which, flip(bits)) for pack, bits in zip(packs[1:], FLIPS[1:])
    ]
    return (packs[0], *others)


def trade_shared(packs, s, rows):
    group = trade(packs, (s,))
    passed = within(group[2][:rows], "tensor", (s,), flip(1))
    return (*group, passed)


def two_steps(s, info, sums, passed, rows):
    joined = add_passed(s, info, sums[2], passed, rows)
    near = within(sums[1], "tensor", (s,), flip(1))
    mirror = within(joined, "tensor", (s,), flip(3))
    return (later(sums[0], joined), near, mirror)


def rope_tables(length):
    halfdim = HEAD_DIM // 2
    power = np.float32(-math.log(10000.0) * 2.0) * np.arange(halfdim, dtype=np.float32)
    inverse = np.exp(power / np.float32(HEAD_DIM))
    turn = np.arange(length, dtype=np.float32)[:, None] * inverse[None, :]
    cosine, sine = np.cos(turn), np.sin(turn)
    return np.tile(cosine, (1, 4)), np.tile(np.concatenate([-sine, sine], axis=1), (1, 2))


def body(clean, noise, times, flags, cotangent, w_main, w_half, w_mod):
    section = lax.axis_index("section")
    part = lax.axis_index("tensor")
    dp_part = lax.axis_index("dp")
    local_seqs, length, width = clean.shape
    columns = w_main.shape[3]
    halfdim = HEAD_DIM // 2

    def mine(values):
        return lax.dynamic_index_in_dim(values, part, 0, keepdims=False)

    theta = math.pi / 2 * (mine(times).astype(F32) + 1.0) / (TSTEPS + 1.0)
    noisy = jnp.cos(theta) * mine(clean).astype(F32) + jnp.sin(theta) * mine(noise).astype(F32)
    target = mine(cotangent)
    info = jnp.stack([section, part, dp_part % 2, mine(flags)]).astype(jnp.int32)

    halfwidth = width // 2
    freqs = jnp.exp(-math.log(10000.0) * jnp.arange(halfwidth, dtype=F32) / halfwidth)
    angles = times.astype(F32)[:, None] * freqs[None, :]
    temb = jnp.concatenate([jnp.sin(angles), jnp.cos(angles)], axis=1)
    mode_part = jnp.einsum("nd,dpc->pnc", temb, w_mod[0].astype(F32), precision=HIGHEST)
    mode_part = mode_part.reshape(3, 4 * columns)
    mode_high = lax.reduce_precision(mode_part, 8, 7)
    own_modes = jnp.concatenate(
        [mode_high, mode_part - mode_high, jnp.zeros((MODE_ROWS - 6, 4 * columns), F32)], axis=0
    ).astype(BF)

    main_local = w_main[0].reshape(width, 4 * columns)
    half_local = w_half[0]
    half_other = swap(half_local, "section", 1)
    second_local = jnp.concatenate([half_other, half_local], axis=0)
    odd = (1, 3)

    def odd_flip(value, axis, bits):
        return within(value, axis, odd, flip(bits))

    one = jnp.concatenate([my_half(main_local, dp_part), own_modes], axis=0)
    one_near = swap(one, "tensor", 1)
    one_mirror = swap(one, "tensor", 3)
    temb_turn = jnp.stack(
        [lax.dynamic_index_in_dim(temb, part ^ i, 0, keepdims=False) for i in FLIPS]
    )
    cosine, sine = (jnp.asarray(table) for table in rope_tables(length))
    one_near, (noisy, temb_turn, info, second_local) = lax.optimization_barrier(
        (one_near, (noisy, temb_turn, info, second_local))
    )
    one_near_x = swap(one_near, "dp", 1)
    one_far = swap(one_mirror, "tensor", 1)
    one_mirror_x = swap(one_mirror, "dp", 1)
    two_mirror = odd_flip(later(second_local, one_mirror), "tensor", 3)
    one_far_x = swap(one_far, "dp", 1)
    two_near = odd_flip(later(second_local, one_far), "tensor", 1)
    two_far = odd_flip(two_mirror, "tensor", 1)
    first = place(info, None, 0, [main_local], False)
    first = place(info, first, 1, [one_near, one_near_x], False)
    first = place(info, first, 2, [one_mirror, one_mirror_x], False)
    first = place(info, first, 3, [one_far, one_far_x], False)
    second = place(info, None, 0, [second_local], True)
    second = place(info, second, 1, [two_near], True)
    second = place(info, second, 2, [two_mirror], True)
    second = place(info, second, 3, [two_far], True)
    modes = pick_modes(info, [own_modes, one_near, one_mirror, one_far])
    temb_other = swap(temb_turn, "dp", 1)
    temb_pair = jnp.where(
        dp_part % 2 == 0,
        jnp.concatenate([temb_turn, temb_other]),
        jnp.concatenate([temb_other, temb_turn]),
    )

    def attend(s, base, arrived, keep):
        return attention_forward(s, info, base, arrived, modes, cosine, sine, first, keep)

    def feed(s, arrived, keep, chain=None):
        return mlp_forward(s, info, arrived, modes, first, second, keep, chain)

    def feed_back(s, grad, kept, keep, chain=None):
        return mlp_back(s, info, grad, modes, kept, first, second, keep, chain)

    def attend_back(s, grad, kept, chain):
        return attention_back(s, info, grad, modes, cosine, sine, kept, first, chain)

    def after(value, earlier):
        return lax.optimization_barrier((value, earlier))

    def across(value, s):
        return within(value, "dp", (s,), lambda i, n: i ^ 1)

    value = attend(0, noisy, None, False)[0]
    value = feed(1, section_hop(value, 0, 1), None)[0]
    value = attend(2, None, section_hop(value, 1, 1), False)[0]
    value = feed(3, section_hop(value, 2, 1), None)[0]
    guess = cyclic(value, "section", 1)

    noisy, temb_pair = after(noisy, temb_pair)
    kept_0 = attend(0, noisy, guess, True)
    stream_1 = section_hop(kept_0[0], 0, 1)
    normed_0 = across(kept_0[6], 0)
    kept_1 = feed(1, later(stream_1, normed_0), "packs")
    stream_2 = section_hop(kept_1[0], 1, 1)
    pack_1, stream_2 = after(kept_1[4:8], stream_2)
    early_1 = trade_shared(pack_1, 1, length)
    kept_2 = attend(2, None, stream_2, True)
    stream_3 = section_hop(kept_2[0], 2, 1)
    normed_2 = across(kept_2[6], 2)
    kept_3 = feed(3, later(stream_3, normed_2), "message", kept_2[7:])

    back_3 = feed_back(3, later(target, early_1[1:3]), kept_3, "message", kept_3[7:])
    grad_2 = section_hop(back_3[0], 3, -1)
    message_3, grad_2 = after(back_3[2], grad_2)
    other_3 = across(message_3, 3)
    back_2 = attend_back(2, grad_2, kept_2, back_3[5:])
    grad_1 = lax.ppermute(back_2[0], "section", [(2, 1)])
    back_1 = feed_back(1, grad_1, kept_1, "packs")
    message_2, hop_0 = after(back_2[2], back_1[0])
    other_2 = (normed_2, across(message_2, 2))
    grad_0 = section_hop(later(hop_0, early_1[3:]), 1, -1)
    rows_high = trade(back_2[5:], (2, 3))
    back_0 = attend_back(0, later(grad_0, other_3, rows_high), kept_0, kept_0[7:])
    other_0 = (normed_0, across(back_0[2], 0))

    def pass_on(far, s):
        return within(far, "tensor", (s,), flip(1))

    def other_pairs(value, s):
        size = lax.axis_size("dp")
        bit = 2
        while bit < size:
            partner = within(value, "dp", (s,), lambda i, n: i ^ bit)
            value = (value.astype(F32) + partner.astype(F32)).astype(BF)
            bit *= 2
        return value

    def finished(s, own):
        own = other_pairs(own, s)
        return (own, across(own, s))

    (far_3,) = mlp_sums(3, info, kept_3, back_3, later(other_3, back_0[0]), (3,))
    passed_3 = pass_on(far_3, 3)
    sums_3 = mlp_sums(3, info, kept_3, back_3, later(other_3, far_3), (0, 1, 2))
    late_1 = trade_shared(later(back_1[2:], back_0[0]), 1, length)
    group_3 = two_steps(3, info, sums_3, passed_3, width)
    own_3 = total_parts(3, info, group_3, width)
    other_0, other_2 = later((other_0, other_2), late_1[:4], own_3)
    block = length // 4
    places = [(pack, pack.shape[0] - block) for pack in early_1[:4]]
    places += [(pack, pack.shape[0] - MODE_ROWS - block) for pack in late_1[:4]]
    places_high = [(rows, 0) for rows in rows_high] + [(rows, block) for rows in rows_high]
    groups = [((1,), places), ((2, 3), places_high)]
    results = collect(info, groups, block, None)
    other_0, results = after(other_0, results)
    (far_0,) = attention_sums(0, info, kept_0, back_0, other_0, (3,), True)
    passed_0 = pass_on(far_0, 0)
    sums_0 = attention_sums(0, info, kept_0, back_0, later(other_0, far_0), (0, 1, 2), True)
    pair_3 = finished(3, own_3)
    group_0 = two_steps(0, info, sums_0, later(passed_0, pair_3), width // 2)
    (far_2,) = attention_sums(2, info, kept_2, back_2, other_2, (3,), False)
    passed_2 = pass_on(far_2, 2)
    sums_2 = attention_sums(2, info, kept_2, back_2, later(other_2, far_2), (0, 1, 2), False)
    group_2 = two_steps(2, info, sums_2, later(passed_2, group_0[0]), width // 2)
    own_1 = mlp_grads(1, info, early_1, late_1, length)
    own_0 = total_parts(0, info, group_0, width // 2)
    places = rest_at(group_0, width // 2, 0) + rest_at(group_0, width // 2, block)
    outputs, in_grads = collect(info, [((0,), places)], block, results)
    own_2 = total_parts(2, info, group_2, width // 2)
    pair_0, pair_1, pair_2 = finished(0, own_0), finished(1, own_1), finished(2, own_2)
    pairs = [pair_0, pair_1, pair_2, pair_3]
    pairs, outputs, in_grads = lax.optimization_barrier((pairs, outputs, in_grads))
    main_total, lent, second_total, mode_grads = finish(info, pairs, width)
    returned = swap(lent, "section", 1)
    mode_total = jnp.einsum("nd,npc->dpc", temb_pair, mode_grads, precision=HIGHEST)
    bit = 2
    while bit < lax.axis_size("dp"):
        mode_total = mode_total + swap(mode_total, "dp", bit)
        bit *= 2
    main_total = main_total.reshape(1, width, 4, columns)
    returned, main_total, mode_total = lax.optimization_barrier(
        (returned, main_total, mode_total)
    )
    half_total = choose_half(info, returned, second_total)
    return (
        outputs[None],
        in_grads[None],
        main_total,
        half_total[None],
        mode_total[None],
    )


def solution(mesh):
    in_specs = (
        P("dp", None, None),
        P("dp", None, None),
        P("dp"),
        P("dp"),
        P("dp", None, None),
        P("section", None, None, "tensor"),
        P("section", "tensor", None),
        P("section", None, None, "tensor"),
    )
    out_specs = (
        P("section", "dp", "tensor", None),
        P("section", "dp", "tensor", None),
        P("section", None, None, "tensor"),
        P("section", "tensor", None),
        P("section", None, None, "tensor"),
    )
    return jax.shard_map(body, mesh=mesh, in_specs=in_specs, out_specs=out_specs, check_vma=False)
```

```python
import functools
import math

import jax
import jax.numpy as jnp
import numpy as np
from jax import lax
from jax.experimental import pallas as pl
from jax.experimental.pallas import tpu as pltpu
from jax.sharding import PartitionSpec as P

HEAD_DIM = 64
TSTEPS = 1000
EPSILON = 1e-05
HIGHEST = lax.Precision.HIGHEST
BF = jnp.bfloat16
F32 = jnp.float32
VMEM_BYTES = 32 * 1024 * 1024
WEIGHT_SIZE = 4 * 768 * 768
FLIPS = (0, 1, 3, 2)
GELU_C = math.sqrt(2.0 / math.pi)
GELU_A = 0.044715


def cyclic(value, axis, by):
    size = lax.axis_size(axis)
    return lax.ppermute(value, axis, [(i, (i + by) % size) for i in range(size)])


def swap(value, axis, bit):
    size = lax.axis_size(axis)
    return lax.ppermute(value, axis, [(i, i ^ bit) for i in range(size)])


def within(value, axis, which, route):
    size = lax.axis_size(axis)
    pairs = [(s * size + i, s * size + route(i, size)) for s in which for i in range(size)]
    return lax.ppermute(value, ("section", axis), pairs)


def section_hop(value, source, by):
    target = source + by
    if source // 2 == target // 2:
        return swap(value, "section", 1)
    return cyclic(value, "section", by)


def dot(left, right):
    return lax.dot_general(left, right, (((1,), (0,)), ((), ())), preferred_element_type=F32)


def dot_nt(left, right):
    return lax.dot_general(left, right, (((1,), (1,)), ((), ())), preferred_element_type=F32)


def dot_tn(left, right):
    return lax.dot_general(left, right, (((0,), (0,)), ((), ())), preferred_element_type=F32)


def standardize(stream):
    centred = stream - jnp.mean(stream, axis=-1, keepdims=True)
    variance = jnp.mean(centred * centred, axis=-1, keepdims=True)
    inverse = lax.rsqrt(variance + EPSILON)
    return centred * inverse, inverse


def swap_halves(block, first):
    return jnp.where(first, pltpu.roll(block, 96, 1), pltpu.roll(block, 32, 1))


def first_mask(rows):
    lane = lax.broadcasted_iota(jnp.int32, (rows, 128), 1)
    return (lane % HEAD_DIM) < HEAD_DIM // 2


def norm_back(normed_grad, stream, scale, grad):
    hat, inverse = standardize(stream)
    shift_grad = jnp.sum(normed_grad, axis=0, keepdims=True)
    scale_grad = jnp.sum(normed_grad * hat, axis=0, keepdims=True)
    hat_grad = normed_grad * (1.0 + scale)
    mean_one = jnp.mean(hat_grad, axis=-1, keepdims=True)
    mean_two = jnp.mean(hat_grad * hat, axis=-1, keepdims=True)
    in_grad = grad + inverse * (hat_grad - mean_one - hat * mean_two)
    return in_grad, shift_grad, scale_grad


def start_all(copies):
    for copy in copies:
        copy.start()


def wait_all(copies):
    for copy in copies:
        copy.wait()


def slot_rows(info, slot, block):
    return pl.ds(pl.multiple_of(slot_part(info, slot) * block, block), block)


def send_halves(send, source, target, at):
    for k in range(2):
        send(source.at[k], target.at[at + k])


def put_halves(ref, value):
    half = ref.shape[2]
    ref[0] = value[:, :half]
    ref[1] = value[:, half:]


MODE_ROWS = 16


def put_mode_grads(ref, values):
    joined = jnp.concatenate(values, axis=0)
    high = joined.astype(BF)
    rest = (joined - high.astype(F32)).astype(BF)
    filler = jnp.zeros((MODE_ROWS - 6, joined.shape[1]), BF)
    both = jnp.concatenate([high, rest, filler], axis=0)
    columns = both.shape[1] // 4
    ref[...] = jnp.zeros_like(ref)
    for part in range(4):
        ref[part, :, :columns] = both[:, part * columns : (part + 1) * columns]


def slot_part(info, slot):
    return info[1] ^ FLIPS[slot]


def send_rows(send, source, info, outs, second):
    block = source.shape[0] // 4
    for slot, out in enumerate(outs):
        target = out.at[pl.ds(block if second else 0, block)]
        send(source.at[slot_rows(info, slot, block)], target)


def row_outs(rows, width):
    return [(shape((rows // 2, width), BF), hbm())] * 4


def vmem():
    return pl.BlockSpec(memory_space=pltpu.VMEM)


def smem():
    return pl.BlockSpec(memory_space=pltpu.SMEM)


def hbm():
    return pl.BlockSpec(memory_space=pltpu.HBM)


def anywhere():
    return pl.BlockSpec(memory_space=pl.ANY)


def params(limit):
    return pltpu.CompilerParams(vmem_limit_bytes=limit)


def cost(flops, nbytes):
    return pl.CostEstimate(flops=flops, bytes_accessed=nbytes, transcendentals=0)


def call(kernel, ins, outs, scratch, aliases, estimate, limit=VMEM_BYTES):
    def placed(value, spec):
        if spec.memory_space is pltpu.HBM:
            return pltpu.with_memory_space_constraint(value, pltpu.HBM)
        if value.size >= WEIGHT_SIZE:
            return pltpu.with_memory_space_constraint(value, pltpu.VMEM)
        return value

    def result(value, spec):
        if spec.memory_space is pltpu.HBM:
            return pltpu.HBM(value.shape, value.dtype)
        if math.prod(value.shape) >= WEIGHT_SIZE:
            return pltpu.VMEM(value.shape, value.dtype)
        return value

    return pl.pallas_call(
        kernel,
        out_shape=[result(*pair) for pair in outs],
        in_specs=[spec for _, spec in ins],
        out_specs=[spec for _, spec in outs],
        scratch_shapes=scratch,
        input_output_aliases=aliases,
        compiler_params=params(limit),
        cost_estimate=estimate,
    )(*[placed(*pair) for pair in ins])


def shape(dims, dtype):
    return jax.ShapeDtypeStruct(dims, dtype)


DMA = pltpu.SemaphoreType.DMA


def place_kernel(slot, odd_only, *refs):
    info, pieces, (out, sems) = refs[0], refs[1:-3], refs[-2:]
    rows = out.shape[1] // len(pieces)

    def copy_all():
        copies = []
        for i, piece in enumerate(pieces):
            begin = 0
            if len(pieces) == 2:
                begin = pl.multiple_of((info[2] if i == 0 else 1 - info[2]) * rows, rows)
            target = out.at[slot, pl.ds(begin, rows)]
            copies.append(pltpu.make_async_copy(piece.at[pl.ds(0, rows)], target, sems.at[i]))
        start_all(copies)
        wait_all(copies)

    if odd_only:
        pl.when(info[0] % 2 == 1)(copy_all)
    else:
        copy_all()


def first_kernel(odd_only, info, piece, out, sems):
    place_kernel(0, odd_only, info, piece, None, out, sems)


def place(info, weight, slot, pieces, odd_only):
    ins = [(info, smem())] + [(piece, anywhere()) for piece in pieces]
    width = pieces[0].shape[1]
    aliases = {}
    if weight is None:
        kernel = functools.partial(first_kernel, odd_only)
    else:
        kernel = functools.partial(place_kernel, slot, odd_only)
        aliases = {len(ins): 0}
        ins.append((weight, vmem()))
    outs = [(shape((4, width, width), BF), vmem())]
    estimate = cost(1_000_000, 2_000_000)
    return call(kernel, ins, outs, [DMA((2,))], aliases, estimate, 1024 * 1024)[0]


def modes_kernel(*refs):
    info, pieces, (modes, mode_ref, sems) = refs[0], refs[1:5], refs[5:]
    copies = [
        pltpu.make_async_copy(
            piece.at[pl.ds(piece.shape[0] - MODE_ROWS, MODE_ROWS)], mode_ref.at[i], sems.at[i]
        )
        for i, piece in enumerate(pieces)
    ]
    start_all(copies)
    wait_all(copies)
    columns = modes.shape[1] // 4
    for part in range(4):
        bits = info[1] ^ part
        block = mode_ref[bits ^ (bits >> 1)].astype(F32)
        value = block[0:3] + block[3:6]
        chosen = jnp.zeros((3, columns), F32)
        for sequence in range(4):
            here = value[:, sequence * columns : (sequence + 1) * columns]
            chosen = jnp.where(info[1] == sequence, here, chosen)
        modes[:, part * columns : (part + 1) * columns] = chosen


def pick_modes(info, pieces):
    width = pieces[0].shape[1]
    ins = [(info, smem())] + [(piece, anywhere()) for piece in pieces]
    outs = [(shape((3, width), F32), vmem())]
    scratch = [pltpu.VMEM((4, MODE_ROWS, width), BF), DMA((4,))]
    estimate = cost(1_000_000, 1_000_000)
    return call(modes_kernel, ins, outs, scratch, {}, estimate, 2 * 1024 * 1024)[0]


def head_parts(heads, head):
    j, at = head // 3, head % 3 * HEAD_DIM
    return tuple(heads[j, :, at + 192 * i : at + 192 * i + HEAD_DIM] for i in range(3))


def attention_forward_kernel(s, has_base, has_arrived, keep, *refs):
    refs = list(refs)
    info = refs.pop(0)
    base = refs.pop(0) if has_base else None
    arrived = refs.pop(0) if has_arrived else None
    modes, cosine, sine, w = refs[:4]
    refs = refs[4:]
    result = refs.pop(0)
    if keep:
        heads_out, lse_out, attended_out, branch_out, stream_out = refs[:5]
        normed_out = refs[5]
        row_out = refs[6:10]
        refs = refs[10:]
    normed, branch, heads, attended_ref, scores_ref = refs[:5]
    if keep:
        stream_ref, lse, halves, osems = refs[5:]

    def load_stream():
        if not has_base:
            return arrived[...].astype(F32)
        if not has_arrived:
            return base[...]
        return base[...] + info[3].astype(F32) * arrived[...].astype(F32)

    @pl.when(info[0] == s)
    def _():
        outs = []

        def send(source, target):
            copy = pltpu.make_async_copy(source, target, osems.at[len(outs)])
            copy.start()
            outs.append(copy)

        stream = load_stream()
        hat, _ = standardize(stream)
        normed[...] = (hat * (1.0 + modes[1:2, :]) + modes[0:1, :]).astype(BF)
        rows = normed.shape[0]
        if keep:
            stream_ref[...] = stream
            send(stream_ref, stream_out)
            put_halves(halves, normed[...])
            send_halves(send, halves, normed_out, 0)
        first = first_mask(rows)
        low = lax.broadcasted_iota(jnp.int32, (rows, 128), 1) < HEAD_DIM
        for j in range(4):
            raw = dot(normed[...], w[j, :, :576])
            turned = []
            for unit in range(3):
                block = raw[:, unit * 128 : (unit + 1) * 128]
                block = block * cosine[...] + swap_halves(block, first) * sine[...]
                if unit == 0:
                    block = block * 0.125
                if unit == 1:
                    block = jnp.where(low, block * 0.125, block)
                turned.append(block)
            heads[j] = jnp.concatenate(turned + [raw[:, 384:576]], axis=1).astype(BF)
            if keep:
                send(heads.at[j], heads_out.at[j])
        for head in range(12):
            q, k, _ = head_parts(heads, head)
            scores_ref[head] = dot_nt(k, q)
        for j in range(4):
            pieces_t = [jnp.zeros((HEAD_DIM, rows), BF)]
            for head in range(3 * j, 3 * j + 3):
                _, _, v = head_parts(heads, head)
                scores = scores_ref[head]
                top = jnp.max(scores, axis=0, keepdims=True)
                raised = jnp.exp(scores - top)
                total = jnp.sum(raised, axis=0, keepdims=True)
                if keep:
                    lse[head : head + 1, :] = top + jnp.log(total)
                mixed = dot_tn(v, raised.astype(BF)) * (1.0 / total)
                pieces_t.append(mixed.astype(BF))
            attended_ref[j] = jnp.concatenate(pieces_t, axis=0).T
            if keep:
                send(attended_ref.at[j], attended_out.at[j])
        for j in range(4):
            part = dot_nt(attended_ref[j], w[j, :, 512:768])
            branch[...] = part if j == 0 else branch[...] + part
        result[...] = (load_stream() + modes[2:3, :] * branch[...]).astype(BF)
        if keep:
            send(lse, lse_out)
            send(branch, branch_out)
            send_rows(send, result, info, row_out, False)
            wait_all(outs)


def attention_forward(s, info, base, arrived, modes, cosine, sine, weights, keep):
    width = modes.shape[1]
    rows = cosine.shape[0]
    ins = [(info, smem())]
    for value in (base, arrived):
        if value is not None:
            ins.append((value, vmem()))
    ins += [(modes, vmem()), (cosine, vmem()), (sine, vmem()), (weights, vmem())]
    outs = [(shape((rows, width), BF), vmem())]
    scratch = [
        pltpu.VMEM((rows, width), BF),
        pltpu.VMEM((rows, width), F32),
        pltpu.VMEM((4, rows, 576), BF),
        pltpu.VMEM((4, rows, 256), BF),
        pltpu.VMEM((12, rows, rows), F32),
    ]
    if keep:
        outs += [
            (shape((4, rows, 576), BF), hbm()),
            (shape((12, rows), F32), hbm()),
            (shape((4, rows, 256), BF), hbm()),
            (shape((rows, width), F32), hbm()),
            (shape((rows, width), F32), hbm()),
            (shape((2, rows, width // 2), BF), hbm()),
        ]
        outs += row_outs(rows, width)
        scratch += [
            pltpu.VMEM((rows, width), F32),
            pltpu.VMEM((12, rows), F32),
            pltpu.VMEM((2, rows, width // 2), BF),
            DMA((19,)),
        ]
    kernel = functools.partial(
        attention_forward_kernel, s, base is not None, arrived is not None, keep
    )
    return call(kernel, ins, outs, scratch, {}, cost(2_000_000_000, 6_000_000))


def attention_back_kernel(s, shared, *refs):
    info, grad, modes, cosine, sine, w = refs[:6]
    heads_in, lse_in, attended_in, branch_in, stream_in = refs[6:11]
    refs = refs[15 + shared :]
    in_grad, mode_out, message, pack_out, bg_out = refs[:5]
    row_out = refs[5:9]
    heads, lse, attended_ref, branch, stream, bg, ng, halves, pack_ref = refs[9:18]
    att_grad, scores_ref, prob_grads, probs_ref, ds_ref, raw_ref = refs[18:24]
    mode_ref, isems, osems = refs[24:]

    @pl.when(info[0] == s)
    def _():
        loads = []
        for source, target in (
            (heads_in, heads),
            (lse_in, lse),
            (attended_in, attended_ref),
            (stream_in, stream),
            (branch_in, branch),
        ):
            copy = pltpu.make_async_copy(source, target, isems.at[len(loads)])
            loads.append(copy)
        start_all(loads)
        outs = []

        def send(source, target):
            copy = pltpu.make_async_copy(source, target, osems.at[len(outs)])
            copy.start()
            outs.append(copy)

        g = grad[...].astype(F32)
        rows = g.shape[0]
        bg[...] = (modes[2:3, :] * g).astype(BF)
        put_halves(halves, bg[...])
        send_halves(send, halves, bg_out, 0)
        send_halves(send, halves, message, 0)
        first = first_mask(rows)
        for j in range(4):
            att_grad[j] = dot(bg[...], w[j, :, 512:768]).astype(BF)
        wait_all(loads[:2])
        for head in range(12):
            q, k, _ = head_parts(heads, head)
            scores_ref[head] = dot_nt(k, q)
        for head in range(12):
            _, _, v = head_parts(heads, head)
            at = 64 + head % 3 * HEAD_DIM
            prob_grads[head] = dot_nt(v, att_grad[head // 3, :, at : at + HEAD_DIM])
        for head in range(12):
            probs = jnp.exp(scores_ref[head] - lse[head : head + 1, :])
            inner = jnp.sum(prob_grads[head] * probs, axis=0, keepdims=True)
            probs_ref[head] = probs.astype(BF)
            ds_ref[head] = (probs * (prob_grads[head] - inner)).astype(BF)
        wait_all(loads[2:])
        for j in range(4):
            dq, dk, dv = [], [], []
            for head in range(3 * j, 3 * j + 3):
                q, k, _ = head_parts(heads, head)
                at = 64 + head % 3 * HEAD_DIM
                dv.append(dot(probs_ref[head], att_grad[j, :, at : at + HEAD_DIM]))
                dk.append(dot(ds_ref[head], q))
                dq.append(dot_tn(k, ds_ref[head]))
            dq_all = (jnp.concatenate(dq, axis=0) * 0.125).T
            both = jnp.concatenate([dq_all] + dk, axis=1)
            turned = []
            for unit in range(3):
                block = both[:, unit * 128 : (unit + 1) * 128]
                turned.append(block * cosine[...] - swap_halves(block, first) * sine[...])
            raw = jnp.concatenate(turned + dv, axis=1).astype(BF)
            raw_ref[j] = raw
            pack_ref[j, 0] = raw[:, :384]
            pack_ref[j, 1] = jnp.concatenate([raw[:, 384:576], attended_ref[j, :, 64:256]], axis=1)
            send(pack_ref.at[j, info[2]], pack_out.at[j])
            send(pack_ref.at[j, 1 - info[2]], message.at[2 + j])
        for j in range(4):
            part = dot_nt(raw_ref[j], w[j, :, :576])
            ng[...] = part if j == 0 else ng[...] + part
        total, shift_grad, scale_grad = norm_back(
            ng[...], stream[...], modes[1:2, :], grad[...].astype(F32)
        )
        in_grad[...] = total.astype(BF)
        send_rows(send, in_grad, info, row_out, True)
        gate_grad = jnp.sum(grad[...].astype(F32) * branch[...], axis=0, keepdims=True)
        put_mode_grads(mode_ref, (shift_grad, scale_grad, gate_grad))
        send(mode_ref, mode_out)
        wait_all(outs)


def attention_back(s, info, grad, modes, cosine, sine, kept, weights, chain, message):
    rows, width = grad.shape
    ins = [(info, smem()), (grad, vmem()), (modes, vmem()), (cosine, vmem()), (sine, vmem())]
    ins += [(weights, vmem())]
    ins += [(value, hbm()) for value in kept[1:6]]
    outs = [
        (shape((rows, width), BF), vmem()),
        (shape((4, MODE_ROWS, 256), BF), hbm()),
        (shape((6, rows, width // 2), BF), hbm()),
        (shape((4, rows, width // 2), BF), hbm()),
        (shape((2, rows, width // 2), BF), hbm()),
    ]
    outs += row_outs(rows, width)
    aliases = {len(ins) + i: len(outs) - 4 + i for i in range(4)}
    ins += [(value, hbm()) for value in chain]
    if message is not None:
        aliases[len(ins)] = 2
        ins.append((message, hbm()))
    scratch = [
        pltpu.VMEM((4, rows, 576), BF),
        pltpu.VMEM((12, rows), F32),
        pltpu.VMEM((4, rows, 256), BF),
        pltpu.VMEM((rows, width), F32),
        pltpu.VMEM((rows, width), F32),
        pltpu.VMEM((rows, width), BF),
        pltpu.VMEM((rows, width), F32),
        pltpu.VMEM((2, rows, width // 2), BF),
        pltpu.VMEM((4, 2, rows, width // 2), BF),
        pltpu.VMEM((4, rows, 256), BF),
        pltpu.VMEM((12, rows, rows), F32),
        pltpu.VMEM((12, rows, rows), F32),
        pltpu.VMEM((12, rows, rows), BF),
        pltpu.VMEM((12, rows, rows), BF),
        pltpu.VMEM((4, rows, 576), BF),
        pltpu.VMEM((4, MODE_ROWS, 256), BF),
        DMA((5,)),
        DMA((17,)),
    ]
    kernel = functools.partial(attention_back_kernel, s, 0 if message is None else 1)
    return call(kernel, ins, outs, scratch, aliases, cost(3_000_000_000, 10_000_000))


def mlp_forward_kernel(s, keep, *refs):
    info, arrived, modes, w1, w2 = refs[:5]
    refs = refs[5 + (4 if keep == "message" else 0) :]
    result = refs[0]
    refs = refs[1:]
    if keep:
        slope_out, branch_out, stream_out = refs[:3]
        refs = refs[3:]
    if keep == "packs":
        packs = refs[:4]
        refs = refs[4:]
    if keep == "message":
        act_out, normed_out, message = refs[:3]
        row_out = refs[3:7]
        refs = refs[7:]
    normed, branch = refs[:2]
    if keep:
        act_ref, slope_ref, halves, osems = refs[2:]

    @pl.when(info[0] == s)
    def _():
        outs = []

        def send(source, target):
            copy = pltpu.make_async_copy(source, target, osems.at[len(outs)])
            copy.start()
            outs.append(copy)

        hat, _ = standardize(arrived[...].astype(F32))
        normed[...] = (hat * (1.0 + modes[1:2, :]) + modes[0:1, :]).astype(BF)
        rows = normed.shape[0]
        if keep:
            send(arrived, stream_out)
        if keep == "packs":
            for pack in packs[:3]:
                send(normed, pack.at[pl.ds(0, rows)])
        if keep == "message":
            put_halves(halves, normed[...])
            send_halves(send, halves, normed_out, 0)
            send_halves(send, halves, message, 0)
        hidden_next = dot(normed[...], w1[0])
        for j in range(4):
            hidden = hidden_next
            if j < 3:
                hidden_next = dot(normed[...], w1[j + 1])
            square = hidden * hidden
            bend = jnp.tanh(GELU_C * hidden * (1.0 + GELU_A * square))
            act = (0.5 * hidden * (1.0 + bend)).astype(BF)
            if keep:
                slope = 0.5 * (1.0 + bend) + (0.5 * GELU_C) * hidden * (1.0 - bend * bend) * (
                    1.0 + (3.0 * GELU_A) * square
                )
                slope_ref[j] = slope.astype(BF)
                send(slope_ref.at[j], slope_out.at[j])
            if keep == "packs":
                act_ref[j] = act
                send(act_ref.at[j], packs[j].at[pl.ds(rows if j < 3 else 0, rows)])
            if keep == "message":
                put_halves(act_ref.at[j], act)
                send(act_ref.at[j, info[2]], act_out.at[j])
                send(act_ref.at[j, 1 - info[2]], message.at[8 + j])
            part = dot(act, w2[j])
            branch[...] = part if j == 0 else branch[...] + part
        result[...] = (arrived[...].astype(F32) + modes[2:3, :] * branch[...]).astype(BF)
        if keep:
            send(branch, branch_out)
            block = rows // 4
            if keep == "packs":
                for slot, pack in enumerate(packs):
                    target = pack.at[pl.ds(pack.shape[0] - block, block)]
                    send(result.at[slot_rows(info, slot, block)], target)
            else:
                send_rows(send, result, info, row_out, False)
            wait_all(outs)


def mlp_forward(s, info, arrived, modes, first, second, keep, chain=None):
    rows, width = arrived.shape
    ins = [(info, smem()), (arrived, vmem()), (modes, vmem())]
    ins += [(first, vmem()), (second, vmem())]
    outs = [(shape((rows, width), BF), vmem())]
    scratch = [
        pltpu.VMEM((rows, width), BF),
        pltpu.VMEM((rows, width), F32),
    ]
    if keep:
        outs += [
            (shape((4, rows, width), BF), hbm()),
            (shape((rows, width), F32), hbm()),
            (shape((rows, width), BF), hbm()),
        ]
        if keep == "packs":
            outs += [(shape((2 * rows + rows // 4, width), BF), hbm())] * 3
            outs += [(shape((rows + rows // 4, width), BF), hbm())]
        else:
            outs += [
                (shape((4, rows, width // 2), BF), hbm()),
                (shape((2, rows, width // 2), BF), hbm()),
                (shape((12, rows, width // 2), BF), hbm()),
            ]
            outs += row_outs(rows, width)
        wide = (4, rows, width) if keep == "packs" else (4, 2, rows, width // 2)
        scratch += [
            pltpu.VMEM(wide, BF),
            pltpu.VMEM((4, rows, width), BF),
            pltpu.VMEM((2, rows, width // 2), BF),
            DMA((24,)),
        ]
    aliases = {}
    if keep == "message":
        aliases = {len(ins) + i: len(outs) - 4 + i for i in range(4)}
        ins += [(value, hbm()) for value in chain]
    kernel = functools.partial(mlp_forward_kernel, s, keep)
    return call(kernel, ins, outs, scratch, aliases, cost(2_400_000_000, 10_000_000))


def mlp_back_kernel(s, keep, *refs):
    info, grad, modes, slope_in, branch_in, stream_in, w1, w2 = refs[:8]
    if keep == "packs":
        in_grad, mode_out = refs[8:10]
        packs = refs[10:14]
        refs = refs[14:]
    else:
        in_grad, mode_out, message, hidden_out, bg_out = refs[13:18]
        row_out = refs[18:22]
        refs = refs[22:]
    slope, branch, stream, bg, ng, halves, hidden_ref = refs[:7]
    mode_ref, isems, osems = refs[7:]

    @pl.when(info[0] == s)
    def _():
        loads = [
            pltpu.make_async_copy(source, target, isems.at[i])
            for i, (source, target) in enumerate(
                ((slope_in, slope), (stream_in, stream), (branch_in, branch))
            )
        ]
        start_all(loads)
        outs = []

        def send(source, target):
            copy = pltpu.make_async_copy(source, target, osems.at[len(outs)])
            copy.start()
            outs.append(copy)

        g = grad[...].astype(F32)
        rows = g.shape[0]
        bg[...] = (modes[2:3, :] * g).astype(BF)
        if keep == "packs":
            for pack in packs[:3]:
                send(bg, pack.at[pl.ds(0, rows)])
        else:
            put_halves(halves, bg[...])
            send_halves(send, halves, bg_out, 0)
            send_halves(send, halves, message, 2)
        act_grad_next = dot_nt(bg[...], w2[0])
        for j in range(4):
            act_grad = act_grad_next
            if j < 3:
                act_grad_next = dot_nt(bg[...], w2[j + 1])
            if j == 0:
                loads[0].wait()
            hidden_grad = (act_grad * slope[j].astype(F32)).astype(BF)
            if keep == "packs":
                hidden_ref[j] = hidden_grad
                send(hidden_ref.at[j], packs[j].at[pl.ds(rows if j < 3 else 0, rows)])
            else:
                put_halves(hidden_ref.at[j], hidden_grad)
                send(hidden_ref.at[j, info[2]], hidden_out.at[j])
                send(hidden_ref.at[j, 1 - info[2]], message.at[4 + j])
            part = dot_nt(hidden_grad, w1[j])
            ng[...] = part if j == 0 else ng[...] + part
        wait_all(loads[1:])
        total, shift_grad, scale_grad = norm_back(
            ng[...], stream[...].astype(F32), modes[1:2, :], grad[...].astype(F32)
        )
        in_grad[...] = total.astype(BF)
        block = rows // 4
        if keep == "packs":
            for slot, pack in enumerate(packs):
                at = pack.shape[0] - MODE_ROWS - block
                send(in_grad.at[slot_rows(info, slot, block)], pack.at[pl.ds(at, block)])
        else:
            send_rows(send, in_grad, info, row_out, True)
        gate_grad = jnp.sum(grad[...].astype(F32) * branch[...], axis=0, keepdims=True)
        put_mode_grads(mode_ref, (shift_grad, scale_grad, gate_grad))
        send(mode_ref, mode_out)
        if keep == "packs":
            for slot, pack in enumerate(packs):
                send(
                    mode_ref.at[slot_part(info, slot)],
                    pack.at[pl.ds(pack.shape[0] - MODE_ROWS, MODE_ROWS), pl.ds(0, 256)],
                )
        wait_all(outs)


def mlp_back(s, info, grad, modes, kept, first, second, keep, chain=None):
    rows, width = grad.shape
    ins = [(info, smem()), (grad, vmem()), (modes, vmem())]
    ins += [(value, hbm()) for value in kept[1:4]]
    ins += [(first, vmem()), (second, vmem())]
    outs = [
        (shape((rows, width), BF), vmem()),
        (shape((4, MODE_ROWS, 256), BF), hbm()),
    ]
    aliases = {}
    if keep == "packs":
        rest = rows // 4 + MODE_ROWS
        outs += [(shape((2 * rows + rest, width), BF), hbm())] * 3
        outs += [(shape((rows + rest, width), BF), hbm())]
    else:
        aliases = {len(ins): 2}
        ins += [(kept[6], hbm())]
        outs += [
            (shape(kept[6].shape, BF), hbm()),
            (shape((4, rows, width // 2), BF), hbm()),
            (shape((2, rows, width // 2), BF), hbm()),
        ]
        outs += row_outs(rows, width)
        aliases.update({len(ins) + i: len(outs) - 4 + i for i in range(4)})
        ins += [(value, hbm()) for value in chain]
    wide = (4, rows, width) if keep == "packs" else (4, 2, rows, width // 2)
    scratch = [
        pltpu.VMEM((4, rows, width), BF),
        pltpu.VMEM((rows, width), F32),
        pltpu.VMEM((rows, width), BF),
        pltpu.VMEM((rows, width), BF),
        pltpu.VMEM((rows, width), F32),
        pltpu.VMEM((2, rows, width // 2), BF),
        pltpu.VMEM(wide, BF),
        pltpu.VMEM((4, MODE_ROWS, 256), BF),
        DMA((3,)),
        DMA((18,)),
    ]
    kernel = functools.partial(mlp_back_kernel, s, keep)
    return call(kernel, ins, outs, scratch, aliases, cost(2_400_000_000, 12_000_000))


def row_copies(group, row, target, sems):
    rows = target.shape[0] // 4
    return [
        pltpu.make_async_copy(
            pack.at[pl.ds(row, rows)], target.at[pl.ds(i * rows, rows)], sems.at[i]
        )
        for i, pack in enumerate(group)
    ]


def rest_to_slots(slots, row_ref, mode_ref, outs, at, info, sems):
    copies = []
    for slot, out in zip(slots, outs):
        row = at
        if row_ref is not None:
            block = row_ref.shape[1]
            target = out.at[pl.ds(row, block)]
            copies.append(pltpu.make_async_copy(row_ref.at[slot], target, sems.at[0, slot]))
            row += block
        target = out.at[pl.ds(row, MODE_ROWS), pl.ds(0, 256)]
        copies.append(
            pltpu.make_async_copy(mode_ref.at[slot_part(info, slot)], target, sems.at[1, slot])
        )
    return copies


def two_sequences(own, other, at, target, sems, which):
    rows = own.shape[1]
    copies = []
    for j in which:
        copies += [
            pltpu.make_async_copy(own.at[j], target.at[j, pl.ds(0, rows)], sems.at[j, 0]),
            pltpu.make_async_copy(
                other.at[at + j], target.at[j, pl.ds(rows, rows)], sems.at[j, 1]
            ),
        ]
    return copies


def attention_sums_kernel(s, slots, with_rows, *refs):
    info, normed_in, bg_in, pack_in, other_normed, other, mode_in = refs[:7]
    row_in = refs[7 : 7 + with_rows]
    refs = refs[7 + with_rows :]
    outs = refs[: len(slots)]
    refs = refs[len(slots) :]
    n_ref, b_ref, p_ref, held, row_ref, mode_ref = refs[:6]
    nsems, bsems, psems, osems, lsems, rsems = refs[6:]
    half = held.shape[1]

    @pl.when(info[0] == s)
    def _():
        loads = [pltpu.make_async_copy(mode_in, mode_ref, lsems.at[4])]
        for i, value in enumerate(row_in):
            loads.append(pltpu.make_async_copy(value, row_ref.at[i], lsems.at[i]))
        rows = row_ref if with_rows else None
        moves = rest_to_slots(slots, rows, mode_ref, outs, half, info, rsems)
        copies = (
            two_sequences(normed_in, other_normed, 0, n_ref, nsems, range(2))
            + two_sequences(pack_in, other, 2, p_ref, psems, slots)
            + two_sequences(bg_in, other, 0, b_ref, bsems, range(2))
        )
        start_all(copies + loads)
        wait_all(copies + loads)
        start_all(moves)
        tokens = jnp.concatenate([n_ref[0], n_ref[1]], axis=1)
        branch = jnp.concatenate([b_ref[0], b_ref[1]], axis=1)
        for j, out in zip(slots, outs):
            held[j] = dot_tn(p_ref[j], tokens).astype(BF)

            @pl.when(info[2] == 1)
            def _():
                outward = dot_tn(p_ref[j, :, 128:], branch)
                held[j, half // 2 :, :] = outward[half // 2 - 128 :].astype(BF)

            copy = pltpu.make_async_copy(held.at[j], out.at[pl.ds(0, half)], osems.at[j])
            copy.start()
            moves.append(copy)
        wait_all(moves)


def attention_sums(s, info, kept, back, other, slots, with_rows):
    rows = kept[6].shape[1]
    half = kept[6].shape[2]
    width = 2 * half
    ins = [(info, smem())]
    ins += [
        (kept[6], hbm()),
        (back[4], hbm()),
        (back[3], hbm()),
        (other[0], anywhere()),
        (other[1], anywhere()),
        (back[1], hbm()),
    ]
    rest = MODE_ROWS
    if with_rows:
        ins += [(value, hbm()) for value in back[5:9]]
        rest += rows // 2
    outs = [(shape((half + rest, width), BF), hbm())] * len(slots)
    scratch = [
        pltpu.VMEM((2, 2 * rows, half), BF),
        pltpu.VMEM((2, 2 * rows, half), BF),
        pltpu.VMEM((4, 2 * rows, half), BF),
        pltpu.VMEM((4, half, width), BF),
        pltpu.VMEM((4, rows // 2, width), BF),
        pltpu.VMEM((4, MODE_ROWS, 256), BF),
        DMA((2, 2)),
        DMA((2, 2)),
        DMA((4, 2)),
        DMA((4,)),
        DMA((5,)),
        DMA((2, 4)),
    ]
    kernel = functools.partial(attention_sums_kernel, s, slots, 4 if with_rows else 0)
    return call(kernel, ins, outs, scratch, {}, cost(1_300_000_000, 8_000_000))


def mlp_sums_kernel(s, slots, *refs):
    info, normed_in, bg_in, hidden_in, act_in, other, mode_in = refs[:7]
    outs = refs[7 : 7 + len(slots)]
    refs = refs[7 + len(slots) :]
    n_ref, b_ref, h_ref, a_ref, held, mode_ref = refs[:6]
    nsems, bsems, hsems, asems, osems, lsems, rsems = refs[6:]
    half = held.shape[1] // 2

    @pl.when(info[0] == s)
    def _():
        loads = [pltpu.make_async_copy(mode_in, mode_ref, lsems.at[4])]
        moves = rest_to_slots(slots, None, mode_ref, outs, 2 * half, info, rsems)
        left = two_sequences(normed_in, other, 0, n_ref, nsems, range(2))
        left += two_sequences(hidden_in, other, 4, h_ref, hsems, slots)
        right = two_sequences(bg_in, other, 2, b_ref, bsems, range(2))
        right += two_sequences(act_in, other, 8, a_ref, asems, slots)
        start_all(left + right + loads)
        wait_all(left)
        tokens = jnp.concatenate([n_ref[0], n_ref[1]], axis=1)
        for j in slots:
            held[j, :half] = dot_tn(h_ref[j], tokens).astype(BF)
        wait_all(right + loads)
        start_all(moves)
        branch = jnp.concatenate([b_ref[0], b_ref[1]], axis=1)
        for j, out in zip(slots, outs):
            held[j, half:] = dot_tn(a_ref[j], branch).astype(BF)
            copy = pltpu.make_async_copy(held.at[j], out.at[pl.ds(0, 2 * half)], osems.at[j])
            copy.start()
            moves.append(copy)
        wait_all(moves)


def mlp_sums(s, info, kept, back, other, slots):
    rows = kept[5].shape[1]
    half = kept[5].shape[2]
    width = 2 * half
    ins = [(info, smem())]
    ins += [
        (kept[5], hbm()),
        (back[4], hbm()),
        (back[3], hbm()),
        (kept[4], hbm()),
        (other, anywhere()),
        (back[1], hbm()),
    ]
    outs = [(shape((width + MODE_ROWS, width), BF), hbm())] * len(slots)
    scratch = [
        pltpu.VMEM((2, 2 * rows, half), BF),
        pltpu.VMEM((2, 2 * rows, half), BF),
        pltpu.VMEM((4, 2 * rows, half), BF),
        pltpu.VMEM((4, 2 * rows, half), BF),
        pltpu.VMEM((4, width, width), BF),
        pltpu.VMEM((4, MODE_ROWS, 256), BF),
        DMA((2, 2)),
        DMA((2, 2)),
        DMA((4, 2)),
        DMA((4, 2)),
        DMA((4,)),
        DMA((5,)),
        DMA((2, 4)),
    ]
    kernel = functools.partial(mlp_sums_kernel, s, slots)
    return call(kernel, ins, outs, scratch, {}, cost(2_600_000_000, 12_000_000))


def add_passed_kernel(s, *refs):
    info, own, passed, out, held, total, sems = refs
    rows = total.shape[0]
    rest = own.shape[0] - rows

    @pl.when(info[0] == s)
    def _():
        copies = [
            pltpu.make_async_copy(value, held.at[i], sems.at[i])
            for i, value in enumerate((own, passed))
        ]
        start_all(copies)
        wait_all(copies)
        moves = [
            pltpu.make_async_copy(
                held.at[i, pl.ds(rows, rest)], out.at[pl.ds(rows + i * rest, rest)], sems.at[2 + i]
            )
            for i in range(2)
        ]
        start_all(moves)
        total[...] = (held[0, :rows].astype(F32) + held[1, :rows].astype(F32)).astype(BF)
        moves.append(pltpu.make_async_copy(total, out.at[pl.ds(0, rows)], sems.at[4]))
        moves[2].start()
        wait_all(moves)


def add_passed(s, info, own, passed, rows):
    length, width = own.shape
    ins = [(info, smem()), (own, hbm()), (passed, anywhere())]
    outs = [(shape((2 * length - rows, width), BF), hbm())]
    scratch = [pltpu.VMEM((2, length, width), BF), pltpu.VMEM((rows, width), BF), DMA((5,))]
    kernel = functools.partial(add_passed_kernel, s)
    return call(kernel, ins, outs, scratch, {}, cost(10_000_000, 5_000_000))[0]


def rest_at(group, rows, at):
    rest = group[0].shape[0] - rows
    own, near, mirror = group
    return [(own, rows + at), (near, rows + at), (mirror, rows + at), (mirror, rows + rest + at)]


def join_modes(held, columns):
    return jnp.concatenate([held[i, :, :columns] for i in range(4)], axis=1)


def total_kernel(s, at, *refs):
    info = refs[0]
    parts = refs[1:-4]
    out, held, mode_ref, sems = refs[-4:]
    rows = held.shape[1]

    @pl.when(info[0] == s)
    def _():
        copies = []
        for i, part in enumerate(parts):
            copies.append(
                pltpu.make_async_copy(part.at[pl.ds(0, rows)], held.at[i], sems.at[0, i])
            )
        for i, (part, row) in enumerate(rest_at(parts, rows, at)):
            modes = part.at[pl.ds(row, MODE_ROWS), pl.ds(0, 256)]
            copies.append(pltpu.make_async_copy(modes, mode_ref.at[i], sems.at[1, i]))
        start_all(copies)
        wait_all(copies)
        total = held[0].astype(F32)
        for i in range(1, len(parts)):
            total = total + held[i].astype(F32)
        out[:rows] = total.astype(BF)
        out[rows:] = join_modes(mode_ref, out.shape[1] // 4)


def total_parts(s, info, group, rows):
    width = group[0].shape[1]
    at = group[0].shape[0] - MODE_ROWS - rows
    ins = [(info, smem())] + [(value, anywhere()) for value in group]
    outs = [(shape((rows + MODE_ROWS, width), BF), vmem())]
    scratch = [
        pltpu.VMEM((len(group), rows, width), BF),
        pltpu.VMEM((4, MODE_ROWS, 256), BF),
        DMA((2, 4)),
    ]
    kernel = functools.partial(total_kernel, s, at)
    return call(kernel, ins, outs, scratch, {}, cost(10_000_000, 5_000_000))[0]


def mlp_grads_kernel(s, *refs):
    info = refs[0]
    early, late = refs[1:6], refs[6:11]
    out = refs[11]
    a_ref, n_ref, h_ref, b_ref, mode_ref, sems = refs[12:]
    rows = n_ref.shape[0] // 4

    def places(group):
        shared = [(pack, 0) for pack in (*group[:3], group[4])]
        columns = [(pack, rows) for pack in group[:3]] + [(group[3], 0)]
        return shared, columns

    @pl.when(info[0] == s)
    def _():
        copies = []
        for k, (target, wanted) in enumerate(
            zip((n_ref, a_ref, b_ref, h_ref), places(early) + places(late))
        ):
            for i, (pack, row) in enumerate(wanted):
                copies.append(
                    pltpu.make_async_copy(
                        pack.at[pl.ds(row, rows)], target.at[pl.ds(i * rows, rows)], sems.at[k, i]
                    )
                )
        for i, pack in enumerate(late[:4]):
            modes = pack.at[pl.ds(pack.shape[0] - MODE_ROWS, MODE_ROWS), pl.ds(0, 256)]
            copies.append(pltpu.make_async_copy(modes, mode_ref.at[i], sems.at[4, i]))
        start_all(copies)
        wait_all(copies)
        width = n_ref.shape[1]
        out[pl.ds(2 * width, MODE_ROWS), :] = join_modes(mode_ref, width // 4)
        for c in range(width // 256):
            part = pl.ds(c * 256, 256)
            out[part, :] = dot_tn(h_ref[:, part], n_ref[...]).astype(BF)
            out[pl.ds(width + c * 256, 256), :] = dot_tn(a_ref[:, part], b_ref[...]).astype(BF)


def mlp_grads(s, info, early, late, rows):
    width = late[0].shape[1]
    ins = [(info, smem())]
    ins += [(value, anywhere()) for value in (*early, *late)]
    outs = [(shape((2 * width + MODE_ROWS, width), BF), vmem())]
    scratch = [pltpu.VMEM((4 * rows, width), BF)] * 4
    scratch += [pltpu.VMEM((4, MODE_ROWS, 256), BF), DMA((5, 4))]
    kernel = functools.partial(mlp_grads_kernel, s)
    return call(kernel, ins, outs, scratch, {}, cost(2_600_000_000, 10_000_000))[0]


def finish_kernel(*refs):
    info = refs[0]
    pairs = [refs[1 + 2 * s : 3 + 2 * s] for s in range(4)]
    main, lent, second_out, modes, held, mode_ref, second, sems = refs[9:]
    width = main.shape[0]
    half = width // 2
    here = pl.ds(pl.multiple_of(info[2] * half, half), half)
    there = pl.ds(pl.multiple_of((1 - info[2]) * half, half), half)

    def mode_copies(s):
        copies = []
        for i, value in enumerate(pairs[s]):
            rows = value.at[pl.ds(value.shape[0] - MODE_ROWS, MODE_ROWS)]
            which = info[2] if i == 0 else 1 - info[2]
            copies.append(pltpu.make_async_copy(rows, mode_ref.at[which], sems.at[4 + i]))
        return copies

    def halves(s):
        own, other = pairs[s]
        copies = mode_copies(s)
        for k in range(own.shape[0] // half):
            part = pl.ds(k * half, half)
            copies += [
                pltpu.make_async_copy(own.at[part], held.at[k, here], sems.at[2 * k]),
                pltpu.make_async_copy(other.at[part], held.at[k, there], sems.at[2 * k + 1]),
            ]
        start_all(copies)
        wait_all(copies)
        main[...] = held[0].astype(F32).T
        if own.shape[0] > width:
            lent[...] = held[1, :half]
            second[...] = held[1, half:].astype(F32)
            copy = pltpu.make_async_copy(second, second_out, sems.at[6])
            copy.start()
            copy.wait()

    for s in (0, 2, 3):

        @pl.when(info[0] == s)
        def _():
            halves(s)

    @pl.when(info[0] == 1)
    def _():
        copies = mode_copies(1)
        for i, value in enumerate(pairs[1]):
            for k in range(2):
                part = value.at[pl.ds(k * width, width)]
                copies.append(
                    pltpu.make_async_copy(part, held.at[2 * i + k], sems.at[2 * i + k])
                )
        start_all(copies)
        wait_all(copies)
        main[...] = (held[0].astype(F32) + held[2].astype(F32)).T
        lent[...] = (held[1, :half].astype(F32) + held[3, :half].astype(F32)).astype(BF)
        second[...] = held[1, half:].astype(F32) + held[3, half:].astype(F32)
        copy = pltpu.make_async_copy(second, second_out, sems.at[6])
        copy.start()
        copy.wait()

    columns = width // 4
    for i in range(2):
        value = mode_ref[i].astype(F32)
        value = value[0:3] + value[3:6]
        for j in range(4):
            modes[4 * i + j] = value[:, j * columns : (j + 1) * columns]


def finish(info, pairs, width):
    ins = [(info, smem())] + [(value, anywhere()) for pair in pairs for value in pair]
    outs = [
        (shape((width, width), F32), vmem()),
        (shape((width // 2, width), BF), vmem()),
        (shape((width // 2, width), F32), hbm()),
        (shape((8, 3, width // 4), F32), vmem()),
    ]
    scratch = [
        pltpu.VMEM((4, width, width), BF),
        pltpu.VMEM((2, MODE_ROWS, width), BF),
        pltpu.VMEM((width // 2, width), F32),
        DMA((7,)),
    ]
    return call(finish_kernel, ins, outs, scratch, {}, cost(10_000_000, 10_000_000))


def collect_kernel(rows_at, *refs):
    info = refs[0]
    outs = refs[-6:-4]
    held, wide, sems, osems = refs[-4:]
    block = held.shape[2]
    begin = 1
    for sections, rows in rows_at:
        group = refs[begin : begin + 8]
        begin += 8
        chosen = info[0] == sections[0]
        for s in sections[1:]:
            chosen = jnp.logical_or(chosen, info[0] == s)

        @pl.when(chosen)
        def _():
            copies = []
            for i, (pack, row) in enumerate(zip(group, rows)):
                copies.append(
                    pltpu.make_async_copy(
                        pack.at[pl.ds(row, block)], held.at[i // 4, i % 4], sems.at[i]
                    )
                )
            start_all(copies)
            wait_all(copies)
            moves = []
            for k in range(2):
                for i in range(4):
                    wide[k, slot_part(info, i)] = held[k, i].astype(F32)
                moves.append(pltpu.make_async_copy(wide.at[k], outs[k], osems.at[k]))
                moves[k].start()
            wait_all(moves)


def collect(info, groups, block, older):
    ins = [(info, smem())]
    rows_at = []
    for sections, places in groups:
        ins += [(value, anywhere()) for value, _ in places]
        rows_at.append((sections, tuple(row for _, row in places)))
    width = groups[0][1][0][0].shape[1]
    outs = [(shape((4, block, width), F32), hbm())] * 2
    aliases = {}
    if older is not None:
        aliases = {len(ins) + i: i for i in range(2)}
        ins += [(value, hbm()) for value in older]
    scratch = [
        pltpu.VMEM((2, 4, block, width), BF),
        pltpu.VMEM((2, 4, block, width), F32),
        DMA((8,)),
        DMA((2,)),
    ]
    kernel = functools.partial(collect_kernel, tuple(rows_at))
    return call(kernel, ins, outs, scratch, aliases, cost(1_000_000, 2_000_000))


def half_kernel(info, returned, second, out, wide, sem):
    @pl.when(info[0] % 2 == 0)
    def _():
        wide[...] = returned[...].astype(F32)
        copy = pltpu.make_async_copy(wide, out, sem)
        copy.start()
        copy.wait()


def choose_half(info, returned, second):
    ins = [(info, smem()), (returned, vmem()), (second, hbm())]
    outs = [(shape(second.shape, F32), hbm())]
    scratch = [pltpu.VMEM(second.shape, F32), DMA]
    return call(half_kernel, ins, outs, scratch, {2: 0}, cost(1_000_000, 2_000_000))[0]


def flip(bits):
    return lambda i, n: i ^ bits


def later(value, *ended):
    return lax.optimization_barrier((value, ended))[0]


def my_half(chunk, dp_part):
    half = chunk.shape[0] // 2
    return lax.dynamic_slice_in_dim(chunk, dp_part % 2 * half, half, 0)


def trade(packs, which):
    others = [
        within(pack, "tensor", which, flip(bits)) for pack, bits in zip(packs[1:], FLIPS[1:])
    ]
    return (packs[0], *others)


def trade_shared(packs, s, rows):
    group = trade(packs, (s,))
    passed = within(group[2][:rows], "tensor", (s,), flip(1))
    return (*group, passed)


def two_steps(s, info, sums, passed, rows):
    joined = add_passed(s, info, sums[2], passed, rows)
    near = within(sums[1], "tensor", (s,), flip(1))
    mirror = within(joined, "tensor", (s,), flip(3))
    return (later(sums[0], joined), near, mirror)


def rope_tables(length):
    halfdim = HEAD_DIM // 2
    power = np.float32(-math.log(10000.0) * 2.0) * np.arange(halfdim, dtype=np.float32)
    inverse = np.exp(power / np.float32(HEAD_DIM))
    turn = np.arange(length, dtype=np.float32)[:, None] * inverse[None, :]
    cosine, sine = np.cos(turn), np.sin(turn)
    return np.tile(cosine, (1, 4)), np.tile(np.concatenate([-sine, sine], axis=1), (1, 2))


def body(clean, noise, times, flags, cotangent, w_main, w_half, w_mod):
    section = lax.axis_index("section")
    part = lax.axis_index("tensor")
    dp_part = lax.axis_index("dp")
    local_seqs, length, width = clean.shape
    columns = w_main.shape[3]
    halfdim = HEAD_DIM // 2

    def mine(values):
        return lax.dynamic_index_in_dim(values, part, 0, keepdims=False)

    theta = math.pi / 2 * (mine(times).astype(F32) + 1.0) / (TSTEPS + 1.0)
    noisy = jnp.cos(theta) * mine(clean).astype(F32) + jnp.sin(theta) * mine(noise).astype(F32)
    target = mine(cotangent)
    info = jnp.stack([section, part, dp_part % 2, mine(flags)]).astype(jnp.int32)

    halfwidth = width // 2
    freqs = jnp.exp(-math.log(10000.0) * jnp.arange(halfwidth, dtype=F32) / halfwidth)
    angles = times.astype(F32)[:, None] * freqs[None, :]
    temb = jnp.concatenate([jnp.sin(angles), jnp.cos(angles)], axis=1)
    mode_part = jnp.einsum("nd,dpc->pnc", temb, w_mod[0].astype(F32), precision=HIGHEST)
    mode_part = mode_part.reshape(3, 4 * columns)
    mode_high = lax.reduce_precision(mode_part, 8, 7)
    own_modes = jnp.concatenate(
        [mode_high, mode_part - mode_high, jnp.zeros((MODE_ROWS - 6, 4 * columns), F32)], axis=0
    ).astype(BF)

    main_local = w_main[0].reshape(width, 4 * columns)
    half_local = w_half[0]
    half_other = swap(half_local, "section", 1)
    second_local = jnp.concatenate([half_other, half_local], axis=0)
    odd = (1, 3)

    def odd_flip(value, axis, bits):
        return within(value, axis, odd, flip(bits))

    one = jnp.concatenate([my_half(main_local, dp_part), own_modes], axis=0)
    one_near = swap(one, "tensor", 1)
    one_mirror = swap(one, "tensor", 3)
    temb_turn = jnp.stack(
        [lax.dynamic_index_in_dim(temb, part ^ i, 0, keepdims=False) for i in FLIPS]
    )
    cosine, sine = (jnp.asarray(table) for table in rope_tables(length))
    one_near, (noisy, temb_turn, info, second_local) = lax.optimization_barrier(
        (one_near, (noisy, temb_turn, info, second_local))
    )
    one_near_x = swap(one_near, "dp", 1)
    one_far = swap(one_mirror, "tensor", 1)
    one_mirror_x = swap(one_mirror, "dp", 1)
    two_mirror = odd_flip(later(second_local, one_mirror), "tensor", 3)
    one_far_x = swap(one_far, "dp", 1)
    two_near = odd_flip(later(second_local, one_far), "tensor", 1)
    two_far = odd_flip(two_mirror, "tensor", 1)
    first = place(info, None, 0, [main_local], False)
    first = place(info, first, 1, [one_near, one_near_x], False)
    first = place(info, first, 2, [one_mirror, one_mirror_x], False)
    first = place(info, first, 3, [one_far, one_far_x], False)
    second = place(info, None, 0, [second_local], True)
    second = place(info, second, 1, [two_near], True)
    second = place(info, second, 2, [two_mirror], True)
    second = place(info, second, 3, [two_far], True)
    modes = pick_modes(info, [own_modes, one_near, one_mirror, one_far])
    temb_other = swap(temb_turn, "dp", 1)
    temb_pair = jnp.where(
        dp_part % 2 == 0,
        jnp.concatenate([temb_turn, temb_other]),
        jnp.concatenate([temb_other, temb_turn]),
    )

    def attend(s, base, arrived, keep):
        return attention_forward(s, info, base, arrived, modes, cosine, sine, first, keep)

    def feed(s, arrived, keep, chain=None):
        return mlp_forward(s, info, arrived, modes, first, second, keep, chain)

    def feed_back(s, grad, kept, keep, chain=None):
        return mlp_back(s, info, grad, modes, kept, first, second, keep, chain)

    def attend_back(s, grad, kept, chain, message):
        return attention_back(
            s, info, grad, modes, cosine, sine, kept, first, chain, message
        )

    def after(value, earlier):
        return lax.optimization_barrier((value, earlier))

    def across(value, *which):
        return within(value, "dp", which, flip(1))

    value = attend(0, noisy, None, False)[0]
    value = feed(1, section_hop(value, 0, 1), None)[0]
    value = attend(2, None, section_hop(value, 1, 1), False)[0]
    value = feed(3, section_hop(value, 2, 1), None)[0]
    guess = cyclic(value, "section", 1)

    noisy, temb_pair = after(noisy, temb_pair)
    kept_0 = attend(0, noisy, guess, True)
    stream_1 = section_hop(kept_0[0], 0, 1)
    normed_0 = across(kept_0[6], 0)
    kept_1 = feed(1, later(stream_1, normed_0), "packs")
    stream_2 = section_hop(kept_1[0], 1, 1)
    pack_1, stream_2 = after(kept_1[4:8], stream_2)
    early_1 = trade_shared(pack_1, 1, length)
    kept_2 = attend(2, None, stream_2, True)
    stream_3 = section_hop(kept_2[0], 2, 1)
    normed_2 = across(kept_2[6], 2)
    kept_3 = feed(3, later(stream_3, normed_2), "message", kept_2[7:])

    back_3 = feed_back(3, later(target, early_1[1:3]), kept_3, "message", kept_3[7:])
    grad_2 = section_hop(back_3[0], 3, -1)
    message_3, grad_2 = after(back_3[2], grad_2)
    other_3 = across(message_3, 3)
    back_2 = attend_back(2, grad_2, kept_2, back_3[5:], None)
    grad_1 = lax.ppermute(back_2[0], "section", [(2, 1)])
    rows_high = trade((back_2[5], later(back_2[6], grad_1), *back_2[7:]), (2, 3))
    back_1 = feed_back(1, later(grad_1, rows_high[2:]), kept_1, "packs")
    grad_0 = section_hop(later(back_1[0], early_1[3:]), 1, -1)
    grad_0 = later(grad_0, other_3)
    back_0 = attend_back(0, grad_0, kept_0, kept_0[7:], back_2[2])
    other_even = across(back_0[2], 0, 2)
    other_0, other_2 = (normed_0, other_even), (normed_2, other_even)

    def pass_on(far, s):
        return within(far, "tensor", (s,), flip(1))

    def other_pairs(value, s):
        size = lax.axis_size("dp")
        bit = 2
        while bit < size:
            partner = within(value, "dp", (s,), lambda i, n: i ^ bit)
            value = (value.astype(F32) + partner.astype(F32)).astype(BF)
            bit *= 2
        return value

    def finished(s, own):
        own = other_pairs(own, s)
        return (own, across(own, s))

    (far_3,) = mlp_sums(3, info, kept_3, back_3, later(other_3, back_0[0]), (3,))
    passed_3 = later(pass_on(far_3, 3), rows_high)
    sums_3 = mlp_sums(3, info, kept_3, back_3, later(other_3, far_3), (0, 1, 2))
    late_1 = trade_shared(later(back_1[2:], back_0[0]), 1, length)
    group_3 = two_steps(3, info, sums_3, passed_3, width)
    own_3 = total_parts(3, info, group_3, width)
    other_0, other_2 = later((other_0, other_2), late_1[:4], own_3)
    block = length // 4
    places = [(pack, pack.shape[0] - block) for pack in early_1[:4]]
    places += [(pack, pack.shape[0] - MODE_ROWS - block) for pack in late_1[:4]]
    places_high = [(rows, 0) for rows in rows_high] + [(rows, block) for rows in rows_high]
    groups = [((1,), places), ((2, 3), places_high)]
    results = collect(info, groups, block, None)
    other_0, results = after(other_0, results)
    (far_0,) = attention_sums(0, info, kept_0, back_0, other_0, (3,), True)
    passed_0 = pass_on(far_0, 0)
    sums_0 = attention_sums(0, info, kept_0, back_0, later(other_0, far_0), (0, 1, 2), True)
    pair_3 = finished(3, own_3)
    group_0 = two_steps(0, info, sums_0, later(passed_0, pair_3), width // 2)
    (far_2,) = attention_sums(2, info, kept_2, back_2, other_2, (3,), False)
    passed_2 = pass_on(far_2, 2)
    sums_2 = attention_sums(2, info, kept_2, back_2, later(other_2, far_2), (0, 1, 2), False)
    group_2 = two_steps(2, info, sums_2, later(passed_2, group_0[0]), width // 2)
    own_1 = mlp_grads(1, info, early_1, late_1, length)
    own_0 = total_parts(0, info, group_0, width // 2)
    places = rest_at(group_0, width // 2, 0) + rest_at(group_0, width // 2, block)
    outputs, in_grads = collect(info, [((0,), places)], block, results)
    own_2 = total_parts(2, info, group_2, width // 2)
    pair_0, pair_1, pair_2 = finished(0, own_0), finished(1, own_1), finished(2, own_2)
    pairs = [pair_0, pair_1, pair_2, pair_3]
    pairs, outputs, in_grads = lax.optimization_barrier((pairs, outputs, in_grads))
    main_total, lent, second_total, mode_grads = finish(info, pairs, width)
    returned = swap(lent, "section", 1)
    mode_total = jnp.einsum("nd,npc->dpc", temb_pair, mode_grads, precision=HIGHEST)
    bit = 2
    while bit < lax.axis_size("dp"):
        mode_total = mode_total + swap(mode_total, "dp", bit)
        bit *= 2
    main_total = main_total.reshape(1, width, 4, columns)
    returned, main_total, mode_total = lax.optimization_barrier(
        (returned, main_total, mode_total)
    )
    half_total = choose_half(info, returned, second_total)
    return (
        outputs[None],
        in_grads[None],
        main_total,
        half_total[None],
        mode_total[None],
    )


def solution(mesh):
    in_specs = (
        P("dp", None, None),
        P("dp", None, None),
        P("dp"),
        P("dp"),
        P("dp", None, None),
        P("section", None, None, "tensor"),
        P("section", "tensor", None),
        P("section", None, None, "tensor"),
    )
    out_specs = (
        P("section", "dp", "tensor", None),
        P("section", "dp", "tensor", None),
        P("section", None, None, "tensor"),
        P("section", "tensor", None),
        P("section", None, None, "tensor"),
    )
    return jax.shard_map(body, mesh=mesh, in_specs=in_specs, out_specs=out_specs, check_vma=False)
```

```python
import functools
import math

import jax
import jax.numpy as jnp
import numpy as np
from jax import lax
from jax.experimental import pallas as pl
from jax.experimental.pallas import tpu as pltpu
from jax.sharding import PartitionSpec as P

HEAD_DIM = 64
TSTEPS = 1000
EPSILON = 1e-05
HIGHEST = lax.Precision.HIGHEST
BF = jnp.bfloat16
F32 = jnp.float32
VMEM_BYTES = 32 * 1024 * 1024
WEIGHT_SIZE = 4 * 768 * 768
FLIPS = (0, 1, 3, 2)
GELU_C = math.sqrt(2.0 / math.pi)
GELU_A = 0.044715


def cyclic(value, axis, by):
    size = lax.axis_size(axis)
    return lax.ppermute(value, axis, [(i, (i + by) % size) for i in range(size)])


def swap(value, axis, bit):
    size = lax.axis_size(axis)
    return lax.ppermute(value, axis, [(i, i ^ bit) for i in range(size)])


def within(value, axis, which, route):
    size = lax.axis_size(axis)
    pairs = [(s * size + i, s * size + route(i, size)) for s in which for i in range(size)]
    return lax.ppermute(value, ("section", axis), pairs)


def section_hop(value, source, by):
    target = source + by
    if source // 2 == target // 2:
        return swap(value, "section", 1)
    return cyclic(value, "section", by)


def dot(left, right):
    return lax.dot_general(left, right, (((1,), (0,)), ((), ())), preferred_element_type=F32)


def dot_nt(left, right):
    return lax.dot_general(left, right, (((1,), (1,)), ((), ())), preferred_element_type=F32)


def dot_tn(left, right):
    return lax.dot_general(left, right, (((0,), (0,)), ((), ())), preferred_element_type=F32)


def standardize(stream):
    centred = stream - jnp.mean(stream, axis=-1, keepdims=True)
    variance = jnp.mean(centred * centred, axis=-1, keepdims=True)
    inverse = lax.rsqrt(variance + EPSILON)
    return centred * inverse, inverse


def swap_halves(block, first):
    return jnp.where(first, pltpu.roll(block, 96, 1), pltpu.roll(block, 32, 1))


def first_mask(rows):
    lane = lax.broadcasted_iota(jnp.int32, (rows, 128), 1)
    return (lane % HEAD_DIM) < HEAD_DIM // 2


def norm_back(normed_grad, stream, scale, grad):
    hat, inverse = standardize(stream)
    shift_grad = jnp.sum(normed_grad, axis=0, keepdims=True)
    scale_grad = jnp.sum(normed_grad * hat, axis=0, keepdims=True)
    hat_grad = normed_grad * (1.0 + scale)
    mean_one = jnp.mean(hat_grad, axis=-1, keepdims=True)
    mean_two = jnp.mean(hat_grad * hat, axis=-1, keepdims=True)
    in_grad = grad + inverse * (hat_grad - mean_one - hat * mean_two)
    return in_grad, shift_grad, scale_grad


def start_all(copies):
    for copy in copies:
        copy.start()


def wait_all(copies):
    for copy in copies:
        copy.wait()


def slot_rows(info, slot, block):
    return pl.ds(pl.multiple_of(slot_part(info, slot) * block, block), block)


def send_halves(send, source, target, at):
    for k in range(2):
        send(source.at[k], target.at[at + k])


def put_halves(ref, value):
    half = ref.shape[2]
    ref[0] = value[:, :half]
    ref[1] = value[:, half:]


MODE_ROWS = 16


def put_mode_grads(ref, values):
    joined = jnp.concatenate(values, axis=0)
    high = joined.astype(BF)
    rest = (joined - high.astype(F32)).astype(BF)
    filler = jnp.zeros((MODE_ROWS - 6, joined.shape[1]), BF)
    both = jnp.concatenate([high, rest, filler], axis=0)
    columns = both.shape[1] // 4
    ref[...] = jnp.zeros_like(ref)
    for part in range(4):
        ref[part, :, :columns] = both[:, part * columns : (part + 1) * columns]


def slot_part(info, slot):
    return info[1] ^ FLIPS[slot]


def send_rows(send, source, info, outs, second):
    block = source.shape[0] // 4
    for slot, out in enumerate(outs):
        target = out.at[pl.ds(block if second else 0, block)]
        send(source.at[slot_rows(info, slot, block)], target)


def row_outs(rows, width):
    return [(shape((rows // 2, width), BF), hbm())] * 4


def vmem():
    return pl.BlockSpec(memory_space=pltpu.VMEM)


def smem():
    return pl.BlockSpec(memory_space=pltpu.SMEM)


def hbm():
    return pl.BlockSpec(memory_space=pltpu.HBM)


def anywhere():
    return pl.BlockSpec(memory_space=pl.ANY)


def params(limit):
    return pltpu.CompilerParams(vmem_limit_bytes=limit)


def cost(flops, nbytes):
    return pl.CostEstimate(flops=flops, bytes_accessed=nbytes, transcendentals=0)


def call(kernel, ins, outs, scratch, aliases, estimate, limit=VMEM_BYTES):
    def placed(value, spec):
        if spec.memory_space is pltpu.HBM:
            return pltpu.with_memory_space_constraint(value, pltpu.HBM)
        if value.size >= WEIGHT_SIZE:
            return pltpu.with_memory_space_constraint(value, pltpu.VMEM)
        return value

    def result(value, spec):
        if spec.memory_space is pltpu.HBM:
            return pltpu.HBM(value.shape, value.dtype)
        if math.prod(value.shape) >= WEIGHT_SIZE:
            return pltpu.VMEM(value.shape, value.dtype)
        return value

    return pl.pallas_call(
        kernel,
        out_shape=[result(*pair) for pair in outs],
        in_specs=[spec for _, spec in ins],
        out_specs=[spec for _, spec in outs],
        scratch_shapes=scratch,
        input_output_aliases=aliases,
        compiler_params=params(limit),
        cost_estimate=estimate,
    )(*[placed(*pair) for pair in ins])


def shape(dims, dtype):
    return jax.ShapeDtypeStruct(dims, dtype)


DMA = pltpu.SemaphoreType.DMA


def place_kernel(slot, odd_only, *refs):
    info, pieces, (out, sems) = refs[0], refs[1:-3], refs[-2:]
    rows = out.shape[1] // len(pieces)

    def copy_all():
        copies = []
        for i, piece in enumerate(pieces):
            begin = 0
            if len(pieces) == 2:
                begin = pl.multiple_of((info[2] if i == 0 else 1 - info[2]) * rows, rows)
            target = out.at[slot, pl.ds(begin, rows)]
            copies.append(pltpu.make_async_copy(piece.at[pl.ds(0, rows)], target, sems.at[i]))
        start_all(copies)
        wait_all(copies)

    if odd_only:
        pl.when(info[0] % 2 == 1)(copy_all)
    else:
        copy_all()


def first_kernel(odd_only, info, piece, out, sems):
    place_kernel(0, odd_only, info, piece, None, out, sems)


def place(info, weight, slot, pieces, odd_only):
    ins = [(info, smem())] + [(piece, anywhere()) for piece in pieces]
    width = pieces[0].shape[1]
    aliases = {}
    if weight is None:
        kernel = functools.partial(first_kernel, odd_only)
    else:
        kernel = functools.partial(place_kernel, slot, odd_only)
        aliases = {len(ins): 0}
        ins.append((weight, vmem()))
    outs = [(shape((4, width, width), BF), vmem())]
    estimate = cost(1_000_000, 2_000_000)
    return call(kernel, ins, outs, [DMA((2,))], aliases, estimate, 1024 * 1024)[0]


def modes_kernel(*refs):
    info, pieces, (modes, mode_ref, sems) = refs[0], refs[1:5], refs[5:]
    copies = [
        pltpu.make_async_copy(
            piece.at[pl.ds(piece.shape[0] - MODE_ROWS, MODE_ROWS)], mode_ref.at[i], sems.at[i]
        )
        for i, piece in enumerate(pieces)
    ]
    start_all(copies)
    wait_all(copies)
    columns = modes.shape[1] // 4
    for part in range(4):
        bits = info[1] ^ part
        block = mode_ref[bits ^ (bits >> 1)].astype(F32)
        value = block[0:3] + block[3:6]
        chosen = jnp.zeros((3, columns), F32)
        for sequence in range(4):
            here = value[:, sequence * columns : (sequence + 1) * columns]
            chosen = jnp.where(info[1] == sequence, here, chosen)
        modes[:, part * columns : (part + 1) * columns] = chosen


def pick_modes(info, pieces):
    width = pieces[0].shape[1]
    ins = [(info, smem())] + [(piece, anywhere()) for piece in pieces]
    outs = [(shape((3, width), F32), vmem())]
    scratch = [pltpu.VMEM((4, MODE_ROWS, width), BF), DMA((4,))]
    estimate = cost(1_000_000, 1_000_000)
    return call(modes_kernel, ins, outs, scratch, {}, estimate, 2 * 1024 * 1024)[0]


def head_parts(heads, head):
    j, at = head // 3, head % 3 * HEAD_DIM
    return tuple(heads[j, :, at + 192 * i : at + 192 * i + HEAD_DIM] for i in range(3))


def attention_forward_kernel(s, has_base, has_arrived, keep, *refs):
    refs = list(refs)
    info = refs.pop(0)
    base = refs.pop(0) if has_base else None
    arrived = refs.pop(0) if has_arrived else None
    modes, cosine, sine, w = refs[:4]
    refs = refs[4:]
    result = refs.pop(0)
    if keep:
        heads_out, lse_out, attended_out, branch_out, stream_out = refs[:5]
        normed_out = refs[5]
        row_out = refs[6:10]
        refs = refs[10:]
    normed, branch, heads, attended_ref, scores_ref = refs[:5]
    if keep:
        stream_ref, lse, halves, osems = refs[5:]

    def load_stream():
        if not has_base:
            return arrived[...].astype(F32)
        if not has_arrived:
            return base[...]
        return base[...] + info[3].astype(F32) * arrived[...].astype(F32)

    @pl.when(info[0] == s)
    def _():
        outs = []

        def send(source, target):
            copy = pltpu.make_async_copy(source, target, osems.at[len(outs)])
            copy.start()
            outs.append(copy)

        stream = load_stream()
        hat, _ = standardize(stream)
        normed[...] = (hat * (1.0 + modes[1:2, :]) + modes[0:1, :]).astype(BF)
        rows = normed.shape[0]
        if keep:
            stream_ref[...] = stream
            send(stream_ref, stream_out)
            put_halves(halves, normed[...])
            send_halves(send, halves, normed_out, 0)
        first = first_mask(rows)
        low = lax.broadcasted_iota(jnp.int32, (rows, 128), 1) < HEAD_DIM
        for j in range(4):
            raw = dot(normed[...], w[j, :, :576])
            turned = []
            for unit in range(3):
                block = raw[:, unit * 128 : (unit + 1) * 128]
                block = block * cosine[...] + swap_halves(block, first) * sine[...]
                if unit == 0:
                    block = block * 0.125
                if unit == 1:
                    block = jnp.where(low, block * 0.125, block)
                turned.append(block)
            heads[j] = jnp.concatenate(turned + [raw[:, 384:576]], axis=1).astype(BF)
            if keep:
                send(heads.at[j], heads_out.at[j])
        for head in range(12):
            q, k, _ = head_parts(heads, head)
            scores_ref[head] = dot_nt(k, q)
        for j in range(4):
            pieces_t = [jnp.zeros((HEAD_DIM, rows), BF)]
            for head in range(3 * j, 3 * j + 3):
                _, _, v = head_parts(heads, head)
                scores = scores_ref[head]
                top = jnp.max(scores, axis=0, keepdims=True)
                raised = jnp.exp(scores - top)
                total = jnp.sum(raised, axis=0, keepdims=True)
                if keep:
                    lse[head : head + 1, :] = top + jnp.log(total)
                mixed = dot_tn(v, raised.astype(BF)) * (1.0 / total)
                pieces_t.append(mixed.astype(BF))
            attended_ref[j] = jnp.concatenate(pieces_t, axis=0).T
            if keep:
                send(attended_ref.at[j], attended_out.at[j])
        for j in range(4):
            part = dot_nt(attended_ref[j], w[j, :, 512:768])
            branch[...] = part if j == 0 else branch[...] + part
        result[...] = (load_stream() + modes[2:3, :] * branch[...]).astype(BF)
        if keep:
            send(lse, lse_out)
            send(branch, branch_out)
            send_rows(send, result, info, row_out, False)
            wait_all(outs)


def attention_forward(s, info, base, arrived, modes, cosine, sine, weights, keep):
    width = modes.shape[1]
    rows = cosine.shape[0]
    ins = [(info, smem())]
    for value in (base, arrived):
        if value is not None:
            ins.append((value, vmem()))
    ins += [(modes, vmem()), (cosine, vmem()), (sine, vmem()), (weights, vmem())]
    outs = [(shape((rows, width), BF), vmem())]
    scratch = [
        pltpu.VMEM((rows, width), BF),
        pltpu.VMEM((rows, width), F32),
        pltpu.VMEM((4, rows, 576), BF),
        pltpu.VMEM((4, rows, 256), BF),
        pltpu.VMEM((12, rows, rows), F32),
    ]
    if keep:
        outs += [
            (shape((4, rows, 576), BF), hbm()),
            (shape((12, rows), F32), hbm()),
            (shape((4, rows, 256), BF), hbm()),
            (shape((rows, width), F32), hbm()),
            (shape((rows, width), F32), hbm()),
            (shape((2, rows, width // 2), BF), hbm()),
        ]
        outs += row_outs(rows, width)
        scratch += [
            pltpu.VMEM((rows, width), F32),
            pltpu.VMEM((12, rows), F32),
            pltpu.VMEM((2, rows, width // 2), BF),
            DMA((19,)),
        ]
    kernel = functools.partial(
        attention_forward_kernel, s, base is not None, arrived is not None, keep
    )
    return call(kernel, ins, outs, scratch, {}, cost(2_000_000_000, 6_000_000))


def attention_back_kernel(s, shared, *refs):
    info, grad, modes, cosine, sine, w = refs[:6]
    heads_in, lse_in, attended_in, branch_in, stream_in = refs[6:11]
    refs = refs[15 + shared :]
    in_grad, mode_out, message, pack_out, bg_out = refs[:5]
    row_out = refs[5:9]
    heads, lse, attended_ref, branch, stream, bg, ng, halves, pack_ref = refs[9:18]
    att_grad, scores_ref, prob_grads, probs_ref, ds_ref, raw_ref = refs[18:24]
    mode_ref, isems, osems = refs[24:]

    @pl.when(info[0] == s)
    def _():
        loads = []
        for source, target in (
            (heads_in, heads),
            (lse_in, lse),
            (attended_in, attended_ref),
            (stream_in, stream),
            (branch_in, branch),
        ):
            copy = pltpu.make_async_copy(source, target, isems.at[len(loads)])
            loads.append(copy)
        start_all(loads)
        outs = []

        def send(source, target):
            copy = pltpu.make_async_copy(source, target, osems.at[len(outs)])
            copy.start()
            outs.append(copy)

        g = grad[...].astype(F32)
        rows = g.shape[0]
        bg[...] = (modes[2:3, :] * g).astype(BF)
        put_halves(halves, bg[...])
        send_halves(send, halves, bg_out, 0)
        send_halves(send, halves, message, 0)
        first = first_mask(rows)
        for j in range(4):
            att_grad[j] = dot(bg[...], w[j, :, 512:768]).astype(BF)
        wait_all(loads[:2])
        for head in range(12):
            q, k, _ = head_parts(heads, head)
            scores_ref[head] = dot_nt(k, q)
        for head in range(12):
            _, _, v = head_parts(heads, head)
            at = 64 + head % 3 * HEAD_DIM
            prob_grads[head] = dot_nt(v, att_grad[head // 3, :, at : at + HEAD_DIM])
        for head in range(12):
            probs = jnp.exp(scores_ref[head] - lse[head : head + 1, :])
            inner = jnp.sum(prob_grads[head] * probs, axis=0, keepdims=True)
            probs_ref[head] = probs.astype(BF)
            ds_ref[head] = (probs * (prob_grads[head] - inner)).astype(BF)
        wait_all(loads[2:])
        for j in range(4):
            dq, dk, dv = [], [], []
            for head in range(3 * j, 3 * j + 3):
                q, k, _ = head_parts(heads, head)
                at = 64 + head % 3 * HEAD_DIM
                dv.append(dot(probs_ref[head], att_grad[j, :, at : at + HEAD_DIM]))
                dk.append(dot(ds_ref[head], q))
                dq.append(dot_tn(k, ds_ref[head]))
            dq_all = (jnp.concatenate(dq, axis=0) * 0.125).T
            both = jnp.concatenate([dq_all] + dk, axis=1)
            turned = []
            for unit in range(3):
                block = both[:, unit * 128 : (unit + 1) * 128]
                turned.append(block * cosine[...] - swap_halves(block, first) * sine[...])
            raw = jnp.concatenate(turned + dv, axis=1).astype(BF)
            raw_ref[j] = raw
            pack_ref[j, 0] = raw[:, :384]
            pack_ref[j, 1] = jnp.concatenate([raw[:, 384:576], attended_ref[j, :, 64:256]], axis=1)
            send(pack_ref.at[j, info[2]], pack_out.at[j])
            send(pack_ref.at[j, 1 - info[2]], message.at[2 + j])
        for j in range(4):
            part = dot_nt(raw_ref[j], w[j, :, :576])
            ng[...] = part if j == 0 else ng[...] + part
        total, shift_grad, scale_grad = norm_back(
            ng[...], stream[...], modes[1:2, :], grad[...].astype(F32)
        )
        in_grad[...] = total.astype(BF)
        send_rows(send, in_grad, info, row_out, True)
        gate_grad = jnp.sum(grad[...].astype(F32) * branch[...], axis=0, keepdims=True)
        put_mode_grads(mode_ref, (shift_grad, scale_grad, gate_grad))
        send(mode_ref, mode_out)
        wait_all(outs)


def attention_back(s, info, grad, modes, cosine, sine, kept, weights, chain, message):
    rows, width = grad.shape
    ins = [(info, smem()), (grad, vmem()), (modes, vmem()), (cosine, vmem()), (sine, vmem())]
    ins += [(weights, vmem())]
    ins += [(value, hbm()) for value in kept[1:6]]
    outs = [
        (shape((rows, width), BF), vmem()),
        (shape((4, MODE_ROWS, 256), BF), hbm()),
        (shape((6, rows, width // 2), BF), hbm()),
        (shape((4, rows, width // 2), BF), hbm()),
        (shape((2, rows, width // 2), BF), hbm()),
    ]
    outs += row_outs(rows, width)
    aliases = {len(ins) + i: len(outs) - 4 + i for i in range(4)}
    ins += [(value, hbm()) for value in chain]
    if message is not None:
        aliases[len(ins)] = 2
        ins.append((message, hbm()))
    scratch = [
        pltpu.VMEM((4, rows, 576), BF),
        pltpu.VMEM((12, rows), F32),
        pltpu.VMEM((4, rows, 256), BF),
        pltpu.VMEM((rows, width), F32),
        pltpu.VMEM((rows, width), F32),
        pltpu.VMEM((rows, width), BF),
        pltpu.VMEM((rows, width), F32),
        pltpu.VMEM((2, rows, width // 2), BF),
        pltpu.VMEM((4, 2, rows, width // 2), BF),
        pltpu.VMEM((4, rows, 256), BF),
        pltpu.VMEM((12, rows, rows), F32),
        pltpu.VMEM((12, rows, rows), F32),
        pltpu.VMEM((12, rows, rows), BF),
        pltpu.VMEM((12, rows, rows), BF),
        pltpu.VMEM((4, rows, 576), BF),
        pltpu.VMEM((4, MODE_ROWS, 256), BF),
        DMA((5,)),
        DMA((17,)),
    ]
    kernel = functools.partial(attention_back_kernel, s, 0 if message is None else 1)
    return call(kernel, ins, outs, scratch, aliases, cost(3_000_000_000, 10_000_000))


def mlp_forward_kernel(s, keep, *refs):
    info, arrived, modes, w1, w2 = refs[:5]
    refs = refs[5 + (4 if keep == "message" else 0) :]
    result = refs[0]
    refs = refs[1:]
    if keep:
        slope_out, branch_out, stream_out = refs[:3]
        refs = refs[3:]
    if keep == "packs":
        packs = refs[:4]
        refs = refs[4:]
    if keep == "message":
        act_out, normed_out, message = refs[:3]
        row_out = refs[3:7]
        refs = refs[7:]
    normed, branch = refs[:2]
    if keep:
        act_ref, slope_ref, halves, osems = refs[2:]

    @pl.when(info[0] == s)
    def _():
        outs = []

        def send(source, target):
            copy = pltpu.make_async_copy(source, target, osems.at[len(outs)])
            copy.start()
            outs.append(copy)

        hat, _ = standardize(arrived[...].astype(F32))
        normed[...] = (hat * (1.0 + modes[1:2, :]) + modes[0:1, :]).astype(BF)
        rows = normed.shape[0]
        if keep:
            send(arrived, stream_out)
        if keep == "packs":
            for pack in packs[:3]:
                send(normed, pack.at[pl.ds(0, rows)])
        if keep == "message":
            put_halves(halves, normed[...])
            send_halves(send, halves, normed_out, 0)
            send_halves(send, halves, message, 0)
        hidden_next = dot(normed[...], w1[0])
        for j in range(4):
            hidden = hidden_next
            if j < 3:
                hidden_next = dot(normed[...], w1[j + 1])
            square = hidden * hidden
            bend = jnp.tanh(GELU_C * hidden * (1.0 + GELU_A * square))
            act = (0.5 * hidden * (1.0 + bend)).astype(BF)
            if keep:
                slope = 0.5 * (1.0 + bend) + (0.5 * GELU_C) * hidden * (1.0 - bend * bend) * (
                    1.0 + (3.0 * GELU_A) * square
                )
                slope_ref[j] = slope.astype(BF)
                send(slope_ref.at[j], slope_out.at[j])
            if keep == "packs":
                act_ref[j] = act
                send(act_ref.at[j], packs[j].at[pl.ds(rows if j < 3 else 0, rows)])
            if keep == "message":
                put_halves(act_ref.at[j], act)
                send(act_ref.at[j, info[2]], act_out.at[j])
                send(act_ref.at[j, 1 - info[2]], message.at[8 + j])
            part = dot(act, w2[j])
            branch[...] = part if j == 0 else branch[...] + part
        result[...] = (arrived[...].astype(F32) + modes[2:3, :] * branch[...]).astype(BF)
        if keep:
            send(branch, branch_out)
            block = rows // 4
            if keep == "packs":
                for slot, pack in enumerate(packs):
                    target = pack.at[pl.ds(pack.shape[0] - block, block)]
                    send(result.at[slot_rows(info, slot, block)], target)
            else:
                send_rows(send, result, info, row_out, False)
            wait_all(outs)


def mlp_forward(s, info, arrived, modes, first, second, keep, chain=None):
    rows, width = arrived.shape
    ins = [(info, smem()), (arrived, vmem()), (modes, vmem())]
    ins += [(first, vmem()), (second, vmem())]
    outs = [(shape((rows, width), BF), vmem())]
    scratch = [
        pltpu.VMEM((rows, width), BF),
        pltpu.VMEM((rows, width), F32),
    ]
    if keep:
        outs += [
            (shape((4, rows, width), BF), hbm()),
            (shape((rows, width), F32), hbm()),
            (shape((rows, width), BF), hbm()),
        ]
        if keep == "packs":
            outs += [(shape((2 * rows + rows // 4, width), BF), hbm())] * 3
            outs += [(shape((rows + rows // 4, width), BF), hbm())]
        else:
            outs += [
                (shape((4, rows, width // 2), BF), hbm()),
                (shape((2, rows, width // 2), BF), hbm()),
                (shape((12, rows, width // 2), BF), hbm()),
            ]
            outs += row_outs(rows, width)
        wide = (4, rows, width) if keep == "packs" else (4, 2, rows, width // 2)
        scratch += [
            pltpu.VMEM(wide, BF),
            pltpu.VMEM((4, rows, width), BF),
            pltpu.VMEM((2, rows, width // 2), BF),
            DMA((24,)),
        ]
    aliases = {}
    if keep == "message":
        aliases = {len(ins) + i: len(outs) - 4 + i for i in range(4)}
        ins += [(value, hbm()) for value in chain]
    kernel = functools.partial(mlp_forward_kernel, s, keep)
    return call(kernel, ins, outs, scratch, aliases, cost(2_400_000_000, 10_000_000))


def mlp_back_kernel(s, keep, *refs):
    info, grad, modes, slope_in, branch_in, stream_in, w1, w2 = refs[:8]
    if keep == "packs":
        in_grad, mode_out = refs[8:10]
        packs = refs[10:14]
        refs = refs[14:]
    else:
        in_grad, mode_out, message, hidden_out, bg_out = refs[13:18]
        row_out = refs[18:22]
        refs = refs[22:]
    slope, branch, stream, bg, ng, halves, hidden_ref = refs[:7]
    mode_ref, isems, osems = refs[7:]

    @pl.when(info[0] == s)
    def _():
        loads = [
            pltpu.make_async_copy(source, target, isems.at[i])
            for i, (source, target) in enumerate(
                ((slope_in, slope), (stream_in, stream), (branch_in, branch))
            )
        ]
        start_all(loads)
        outs = []

        def send(source, target):
            copy = pltpu.make_async_copy(source, target, osems.at[len(outs)])
            copy.start()
            outs.append(copy)

        g = grad[...].astype(F32)
        rows = g.shape[0]
        bg[...] = (modes[2:3, :] * g).astype(BF)
        if keep == "packs":
            for pack in packs[:3]:
                send(bg, pack.at[pl.ds(0, rows)])
        else:
            put_halves(halves, bg[...])
            send_halves(send, halves, bg_out, 0)
            send_halves(send, halves, message, 2)
        act_grad_next = dot_nt(bg[...], w2[0])
        for j in range(4):
            act_grad = act_grad_next
            if j < 3:
                act_grad_next = dot_nt(bg[...], w2[j + 1])
            if j == 0:
                loads[0].wait()
            hidden_grad = (act_grad * slope[j].astype(F32)).astype(BF)
            if keep == "packs":
                hidden_ref[j] = hidden_grad
                send(hidden_ref.at[j], packs[j].at[pl.ds(rows if j < 3 else 0, rows)])
            else:
                put_halves(hidden_ref.at[j], hidden_grad)
                send(hidden_ref.at[j, info[2]], hidden_out.at[j])
                send(hidden_ref.at[j, 1 - info[2]], message.at[4 + j])
            part = dot_nt(hidden_grad, w1[j])
            ng[...] = part if j == 0 else ng[...] + part
        wait_all(loads[1:])
        total, shift_grad, scale_grad = norm_back(
            ng[...], stream[...].astype(F32), modes[1:2, :], grad[...].astype(F32)
        )
        in_grad[...] = total.astype(BF)
        block = rows // 4
        if keep == "packs":
            for slot, pack in enumerate(packs):
                at = pack.shape[0] - MODE_ROWS - block
                send(in_grad.at[slot_rows(info, slot, block)], pack.at[pl.ds(at, block)])
        else:
            send_rows(send, in_grad, info, row_out, True)
        gate_grad = jnp.sum(grad[...].astype(F32) * branch[...], axis=0, keepdims=True)
        put_mode_grads(mode_ref, (shift_grad, scale_grad, gate_grad))
        send(mode_ref, mode_out)
        if keep == "packs":
            for slot, pack in enumerate(packs):
                send(
                    mode_ref.at[slot_part(info, slot)],
                    pack.at[pl.ds(pack.shape[0] - MODE_ROWS, MODE_ROWS), pl.ds(0, 256)],
                )
        wait_all(outs)


def mlp_back(s, info, grad, modes, kept, first, second, keep, chain=None):
    rows, width = grad.shape
    ins = [(info, smem()), (grad, vmem()), (modes, vmem())]
    ins += [(value, hbm()) for value in kept[1:4]]
    ins += [(first, vmem()), (second, vmem())]
    outs = [
        (shape((rows, width), BF), vmem()),
        (shape((4, MODE_ROWS, 256), BF), hbm()),
    ]
    aliases = {}
    if keep == "packs":
        rest = rows // 4 + MODE_ROWS
        outs += [(shape((2 * rows + rest, width), BF), hbm())] * 3
        outs += [(shape((rows + rest, width), BF), hbm())]
    else:
        aliases = {len(ins): 2}
        ins += [(kept[6], hbm())]
        outs += [
            (shape(kept[6].shape, BF), hbm()),
            (shape((4, rows, width // 2), BF), hbm()),
            (shape((2, rows, width // 2), BF), hbm()),
        ]
        outs += row_outs(rows, width)
        aliases.update({len(ins) + i: len(outs) - 4 + i for i in range(4)})
        ins += [(value, hbm()) for value in chain]
    wide = (4, rows, width) if keep == "packs" else (4, 2, rows, width // 2)
    scratch = [
        pltpu.VMEM((4, rows, width), BF),
        pltpu.VMEM((rows, width), F32),
        pltpu.VMEM((rows, width), BF),
        pltpu.VMEM((rows, width), BF),
        pltpu.VMEM((rows, width), F32),
        pltpu.VMEM((2, rows, width // 2), BF),
        pltpu.VMEM(wide, BF),
        pltpu.VMEM((4, MODE_ROWS, 256), BF),
        DMA((3,)),
        DMA((18,)),
    ]
    kernel = functools.partial(mlp_back_kernel, s, keep)
    return call(kernel, ins, outs, scratch, aliases, cost(2_400_000_000, 12_000_000))


def row_copies(group, row, target, sems):
    rows = target.shape[0] // 4
    return [
        pltpu.make_async_copy(
            pack.at[pl.ds(row, rows)], target.at[pl.ds(i * rows, rows)], sems.at[i]
        )
        for i, pack in enumerate(group)
    ]


def rest_to_slots(slots, row_ref, mode_ref, outs, at, info, sems):
    copies = []
    for slot, out in zip(slots, outs):
        row = at
        if row_ref is not None:
            block = row_ref.shape[1]
            target = out.at[pl.ds(row, block)]
            copies.append(pltpu.make_async_copy(row_ref.at[slot], target, sems.at[0, slot]))
            row += block
        target = out.at[pl.ds(row, MODE_ROWS), pl.ds(0, 256)]
        copies.append(
            pltpu.make_async_copy(mode_ref.at[slot_part(info, slot)], target, sems.at[1, slot])
        )
    return copies


def two_sequences(own, other, at, target, sems, which):
    rows = own.shape[1]
    copies = []
    for j in which:
        copies += [
            pltpu.make_async_copy(own.at[j], target.at[j, pl.ds(0, rows)], sems.at[j, 0]),
            pltpu.make_async_copy(
                other.at[at + j], target.at[j, pl.ds(rows, rows)], sems.at[j, 1]
            ),
        ]
    return copies


def attention_sums_kernel(s, slots, with_rows, *refs):
    info, normed_in, bg_in, pack_in, other_normed, other, mode_in = refs[:7]
    row_in = refs[7 : 7 + with_rows]
    refs = refs[7 + with_rows :]
    outs = refs[: len(slots)]
    refs = refs[len(slots) :]
    n_ref, b_ref, p_ref, held, row_ref, mode_ref = refs[:6]
    nsems, bsems, psems, osems, lsems, rsems = refs[6:]
    half = held.shape[1]

    @pl.when(info[0] == s)
    def _():
        loads = [pltpu.make_async_copy(mode_in, mode_ref, lsems.at[4])]
        for i, value in enumerate(row_in):
            loads.append(pltpu.make_async_copy(value, row_ref.at[i], lsems.at[i]))
        rows = row_ref if with_rows else None
        moves = rest_to_slots(slots, rows, mode_ref, outs, half, info, rsems)
        copies = (
            two_sequences(normed_in, other_normed, 0, n_ref, nsems, range(2))
            + two_sequences(pack_in, other, 2, p_ref, psems, slots)
            + two_sequences(bg_in, other, 0, b_ref, bsems, range(2))
        )
        start_all(copies + loads)
        wait_all(copies + loads)
        start_all(moves)
        tokens = jnp.concatenate([n_ref[0], n_ref[1]], axis=1)
        branch = jnp.concatenate([b_ref[0], b_ref[1]], axis=1)
        for j, out in zip(slots, outs):
            held[j] = dot_tn(p_ref[j], tokens).astype(BF)

            @pl.when(info[2] == 1)
            def _():
                outward = dot_tn(p_ref[j, :, 128:], branch)
                held[j, half // 2 :, :] = outward[half // 2 - 128 :].astype(BF)

            copy = pltpu.make_async_copy(held.at[j], out.at[pl.ds(0, half)], osems.at[j])
            copy.start()
            moves.append(copy)
        wait_all(moves)


def attention_sums(s, info, kept, back, other, slots, with_rows):
    rows = kept[6].shape[1]
    half = kept[6].shape[2]
    width = 2 * half
    ins = [(info, smem())]
    ins += [
        (kept[6], hbm()),
        (back[4], hbm()),
        (back[3], hbm()),
        (other[0], anywhere()),
        (other[1], anywhere()),
        (back[1], hbm()),
    ]
    rest = MODE_ROWS
    if with_rows:
        ins += [(value, hbm()) for value in back[5:9]]
        rest += rows // 2
    outs = [(shape((half + rest, width), BF), hbm())] * len(slots)
    scratch = [
        pltpu.VMEM((2, 2 * rows, half), BF),
        pltpu.VMEM((2, 2 * rows, half), BF),
        pltpu.VMEM((4, 2 * rows, half), BF),
        pltpu.VMEM((4, half, width), BF),
        pltpu.VMEM((4, rows // 2, width), BF),
        pltpu.VMEM((4, MODE_ROWS, 256), BF),
        DMA((2, 2)),
        DMA((2, 2)),
        DMA((4, 2)),
        DMA((4,)),
        DMA((5,)),
        DMA((2, 4)),
    ]
    kernel = functools.partial(attention_sums_kernel, s, slots, 4 if with_rows else 0)
    return call(kernel, ins, outs, scratch, {}, cost(1_300_000_000, 8_000_000))


def mlp_sums_kernel(s, slots, *refs):
    info, normed_in, bg_in, hidden_in, act_in, other, mode_in = refs[:7]
    outs = refs[7 : 7 + len(slots)]
    refs = refs[7 + len(slots) :]
    n_ref, b_ref, h_ref, a_ref, held, mode_ref = refs[:6]
    nsems, bsems, hsems, asems, osems, lsems, rsems = refs[6:]
    half = held.shape[1] // 2

    @pl.when(info[0] == s)
    def _():
        loads = [pltpu.make_async_copy(mode_in, mode_ref, lsems.at[4])]
        moves = rest_to_slots(slots, None, mode_ref, outs, 2 * half, info, rsems)
        left = two_sequences(normed_in, other, 0, n_ref, nsems, range(2))
        left += two_sequences(hidden_in, other, 4, h_ref, hsems, slots)
        right = two_sequences(bg_in, other, 2, b_ref, bsems, range(2))
        right += two_sequences(act_in, other, 8, a_ref, asems, slots)
        start_all(left + right + loads)
        wait_all(left)
        tokens = jnp.concatenate([n_ref[0], n_ref[1]], axis=1)
        for j in slots:
            held[j, :half] = dot_tn(h_ref[j], tokens).astype(BF)
        wait_all(right + loads)
        start_all(moves)
        branch = jnp.concatenate([b_ref[0], b_ref[1]], axis=1)
        for j, out in zip(slots, outs):
            held[j, half:] = dot_tn(a_ref[j], branch).astype(BF)
            copy = pltpu.make_async_copy(held.at[j], out.at[pl.ds(0, 2 * half)], osems.at[j])
            copy.start()
            moves.append(copy)
        wait_all(moves)


def mlp_sums(s, info, kept, back, other, slots):
    rows = kept[5].shape[1]
    half = kept[5].shape[2]
    width = 2 * half
    ins = [(info, smem())]
    ins += [
        (kept[5], hbm()),
        (back[4], hbm()),
        (back[3], hbm()),
        (kept[4], hbm()),
        (other, anywhere()),
        (back[1], hbm()),
    ]
    outs = [(shape((width + MODE_ROWS, width), BF), hbm())] * len(slots)
    scratch = [
        pltpu.VMEM((2, 2 * rows, half), BF),
        pltpu.VMEM((2, 2 * rows, half), BF),
        pltpu.VMEM((4, 2 * rows, half), BF),
        pltpu.VMEM((4, 2 * rows, half), BF),
        pltpu.VMEM((4, width, width), BF),
        pltpu.VMEM((4, MODE_ROWS, 256), BF),
        DMA((2, 2)),
        DMA((2, 2)),
        DMA((4, 2)),
        DMA((4, 2)),
        DMA((4,)),
        DMA((5,)),
        DMA((2, 4)),
    ]
    kernel = functools.partial(mlp_sums_kernel, s, slots)
    return call(kernel, ins, outs, scratch, {}, cost(2_600_000_000, 12_000_000))


def add_passed_kernel(s, *refs):
    info, own, passed, out, held, total, sems = refs
    rows = total.shape[0]
    rest = own.shape[0] - rows

    @pl.when(info[0] == s)
    def _():
        copies = [
            pltpu.make_async_copy(value, held.at[i], sems.at[i])
            for i, value in enumerate((own, passed))
        ]
        start_all(copies)
        wait_all(copies)
        moves = [
            pltpu.make_async_copy(
                held.at[i, pl.ds(rows, rest)], out.at[pl.ds(rows + i * rest, rest)], sems.at[2 + i]
            )
            for i in range(2)
        ]
        start_all(moves)
        total[...] = (held[0, :rows].astype(F32) + held[1, :rows].astype(F32)).astype(BF)
        moves.append(pltpu.make_async_copy(total, out.at[pl.ds(0, rows)], sems.at[4]))
        moves[2].start()
        wait_all(moves)


def add_passed(s, info, own, passed, rows):
    length, width = own.shape
    ins = [(info, smem()), (own, hbm()), (passed, anywhere())]
    outs = [(shape((2 * length - rows, width), BF), hbm())]
    scratch = [pltpu.VMEM((2, length, width), BF), pltpu.VMEM((rows, width), BF), DMA((5,))]
    kernel = functools.partial(add_passed_kernel, s)
    return call(kernel, ins, outs, scratch, {}, cost(10_000_000, 5_000_000))[0]


def rest_at(group, rows, at):
    rest = group[0].shape[0] - rows
    own, near, mirror = group
    return [(own, rows + at), (near, rows + at), (mirror, rows + at), (mirror, rows + rest + at)]


def join_modes(held, columns):
    return jnp.concatenate([held[i, :, :columns] for i in range(4)], axis=1)


def total_kernel(s, at, *refs):
    info = refs[0]
    parts = refs[1:-4]
    out, held, mode_ref, sems = refs[-4:]
    rows = held.shape[1]

    @pl.when(info[0] == s)
    def _():
        copies = []
        for i, part in enumerate(parts):
            copies.append(
                pltpu.make_async_copy(part.at[pl.ds(0, rows)], held.at[i], sems.at[0, i])
            )
        for i, (part, row) in enumerate(rest_at(parts, rows, at)):
            modes = part.at[pl.ds(row, MODE_ROWS), pl.ds(0, 256)]
            copies.append(pltpu.make_async_copy(modes, mode_ref.at[i], sems.at[1, i]))
        start_all(copies)
        wait_all(copies)
        total = held[0].astype(F32)
        for i in range(1, len(parts)):
            total = total + held[i].astype(F32)
        out[:rows] = total.astype(BF)
        out[rows:] = join_modes(mode_ref, out.shape[1] // 4)


def total_parts(s, info, group, rows):
    width = group[0].shape[1]
    at = group[0].shape[0] - MODE_ROWS - rows
    ins = [(info, smem())] + [(value, anywhere()) for value in group]
    outs = [(shape((rows + MODE_ROWS, width), BF), vmem())]
    scratch = [
        pltpu.VMEM((len(group), rows, width), BF),
        pltpu.VMEM((4, MODE_ROWS, 256), BF),
        DMA((2, 4)),
    ]
    kernel = functools.partial(total_kernel, s, at)
    return call(kernel, ins, outs, scratch, {}, cost(10_000_000, 5_000_000))[0]


def mlp_grads_kernel(s, *refs):
    info = refs[0]
    early, late = refs[1:6], refs[6:11]
    out = refs[11]
    a_ref, n_ref, h_ref, b_ref, mode_ref, sems = refs[12:]
    rows = n_ref.shape[0] // 4

    def places(group):
        shared = [(pack, 0) for pack in (*group[:3], group[4])]
        columns = [(pack, rows) for pack in group[:3]] + [(group[3], 0)]
        return shared, columns

    @pl.when(info[0] == s)
    def _():
        copies = []
        for k, (target, wanted) in enumerate(
            zip((n_ref, a_ref, b_ref, h_ref), places(early) + places(late))
        ):
            for i, (pack, row) in enumerate(wanted):
                copies.append(
                    pltpu.make_async_copy(
                        pack.at[pl.ds(row, rows)], target.at[pl.ds(i * rows, rows)], sems.at[k, i]
                    )
                )
        for i, pack in enumerate(late[:4]):
            modes = pack.at[pl.ds(pack.shape[0] - MODE_ROWS, MODE_ROWS), pl.ds(0, 256)]
            copies.append(pltpu.make_async_copy(modes, mode_ref.at[i], sems.at[4, i]))
        start_all(copies)
        wait_all(copies)
        width = n_ref.shape[1]
        out[pl.ds(2 * width, MODE_ROWS), :] = join_modes(mode_ref, width // 4)
        for c in range(width // 256):
            part = pl.ds(c * 256, 256)
            out[part, :] = dot_tn(h_ref[:, part], n_ref[...]).astype(BF)
            out[pl.ds(width + c * 256, 256), :] = dot_tn(a_ref[:, part], b_ref[...]).astype(BF)


def mlp_grads(s, info, early, late, rows):
    width = late[0].shape[1]
    ins = [(info, smem())]
    ins += [(value, anywhere()) for value in (*early, *late)]
    outs = [(shape((2 * width + MODE_ROWS, width), BF), vmem())]
    scratch = [pltpu.VMEM((4 * rows, width), BF)] * 4
    scratch += [pltpu.VMEM((4, MODE_ROWS, 256), BF), DMA((5, 4))]
    kernel = functools.partial(mlp_grads_kernel, s)
    return call(kernel, ins, outs, scratch, {}, cost(2_600_000_000, 10_000_000))[0]


def finish_kernel(*refs):
    info = refs[0]
    pairs = [refs[1 + 2 * s : 3 + 2 * s] for s in range(4)]
    main, lent, second_out, modes, held, mode_ref, second, sems = refs[9:]
    width = main.shape[0]
    half = width // 2
    here = pl.ds(pl.multiple_of(info[2] * half, half), half)
    there = pl.ds(pl.multiple_of((1 - info[2]) * half, half), half)

    def mode_copies(s):
        copies = []
        for i, value in enumerate(pairs[s]):
            rows = value.at[pl.ds(value.shape[0] - MODE_ROWS, MODE_ROWS)]
            which = info[2] if i == 0 else 1 - info[2]
            copies.append(pltpu.make_async_copy(rows, mode_ref.at[which], sems.at[4 + i]))
        return copies

    def halves(s):
        own, other = pairs[s]
        copies = mode_copies(s)
        for k in range(own.shape[0] // half):
            part = pl.ds(k * half, half)
            copies += [
                pltpu.make_async_copy(own.at[part], held.at[k, here], sems.at[2 * k]),
                pltpu.make_async_copy(other.at[part], held.at[k, there], sems.at[2 * k + 1]),
            ]
        start_all(copies)
        wait_all(copies)
        main[...] = held[0].astype(F32).T
        if own.shape[0] > width:
            lent[...] = held[1, :half]
            second[...] = held[1, half:].astype(F32)
            copy = pltpu.make_async_copy(second, second_out, sems.at[6])
            copy.start()
            copy.wait()

    for s in (0, 2, 3):

        @pl.when(info[0] == s)
        def _():
            halves(s)

    @pl.when(info[0] == 1)
    def _():
        copies = mode_copies(1)
        for i, value in enumerate(pairs[1]):
            for k in range(2):
                part = value.at[pl.ds(k * width, width)]
                copies.append(
                    pltpu.make_async_copy(part, held.at[2 * i + k], sems.at[2 * i + k])
                )
        start_all(copies)
        wait_all(copies)
        main[...] = (held[0].astype(F32) + held[2].astype(F32)).T
        lent[...] = (held[1, :half].astype(F32) + held[3, :half].astype(F32)).astype(BF)
        second[...] = held[1, half:].astype(F32) + held[3, half:].astype(F32)
        copy = pltpu.make_async_copy(second, second_out, sems.at[6])
        copy.start()
        copy.wait()

    columns = width // 4
    for i in range(2):
        value = mode_ref[i].astype(F32)
        value = value[0:3] + value[3:6]
        for j in range(4):
            modes[4 * i + j] = value[:, j * columns : (j + 1) * columns]


def finish(info, pairs, width):
    ins = [(info, smem())] + [(value, anywhere()) for pair in pairs for value in pair]
    outs = [
        (shape((width, width), F32), vmem()),
        (shape((width // 2, width), BF), vmem()),
        (shape((width // 2, width), F32), hbm()),
        (shape((8, 3, width // 4), F32), vmem()),
    ]
    scratch = [
        pltpu.VMEM((4, width, width), BF),
        pltpu.VMEM((2, MODE_ROWS, width), BF),
        pltpu.VMEM((width // 2, width), F32),
        DMA((7,)),
    ]
    return call(finish_kernel, ins, outs, scratch, {}, cost(10_000_000, 10_000_000))


def collect_kernel(rows_at, *refs):
    info = refs[0]
    outs = refs[-6:-4]
    held, wide, sems, osems = refs[-4:]
    block = held.shape[2]
    begin = 1
    for sections, rows in rows_at:
        group = refs[begin : begin + 8]
        begin += 8
        chosen = info[0] == sections[0]
        for s in sections[1:]:
            chosen = jnp.logical_or(chosen, info[0] == s)

        @pl.when(chosen)
        def _():
            copies = []
            for i, (pack, row) in enumerate(zip(group, rows)):
                copies.append(
                    pltpu.make_async_copy(
                        pack.at[pl.ds(row, block)], held.at[i // 4, i % 4], sems.at[i]
                    )
                )
            start_all(copies)
            wait_all(copies)
            moves = []
            for k in range(2):
                for i in range(4):
                    wide[k, slot_part(info, i)] = held[k, i].astype(F32)
                moves.append(pltpu.make_async_copy(wide.at[k], outs[k], osems.at[k]))
                moves[k].start()
            wait_all(moves)


def collect(info, groups, block, older):
    ins = [(info, smem())]
    rows_at = []
    for sections, places in groups:
        ins += [(value, anywhere()) for value, _ in places]
        rows_at.append((sections, tuple(row for _, row in places)))
    width = groups[0][1][0][0].shape[1]
    outs = [(shape((4, block, width), F32), hbm())] * 2
    aliases = {}
    if older is not None:
        aliases = {len(ins) + i: i for i in range(2)}
        ins += [(value, hbm()) for value in older]
    scratch = [
        pltpu.VMEM((2, 4, block, width), BF),
        pltpu.VMEM((2, 4, block, width), F32),
        DMA((8,)),
        DMA((2,)),
    ]
    kernel = functools.partial(collect_kernel, tuple(rows_at))
    return call(kernel, ins, outs, scratch, aliases, cost(1_000_000, 2_000_000))


def half_kernel(info, returned, second, out, wide, sem):
    @pl.when(info[0] % 2 == 0)
    def _():
        wide[...] = returned[...].astype(F32)
        copy = pltpu.make_async_copy(wide, out, sem)
        copy.start()
        copy.wait()


def choose_half(info, returned, second):
    ins = [(info, smem()), (returned, vmem()), (second, hbm())]
    outs = [(shape(second.shape, F32), hbm())]
    scratch = [pltpu.VMEM(second.shape, F32), DMA]
    return call(half_kernel, ins, outs, scratch, {2: 0}, cost(1_000_000, 2_000_000))[0]


def flip(bits):
    return lambda i, n: i ^ bits


def later(value, *ended):
    return lax.optimization_barrier((value, ended))[0]


def my_half(chunk, dp_part):
    half = chunk.shape[0] // 2
    return lax.dynamic_slice_in_dim(chunk, dp_part % 2 * half, half, 0)


def trade(packs, which):
    others = [
        within(pack, "tensor", which, flip(bits)) for pack, bits in zip(packs[1:], FLIPS[1:])
    ]
    return (packs[0], *others)


def trade_shared(packs, s, rows):
    group = trade(packs, (s,))
    passed = within(group[2][:rows], "tensor", (s,), flip(1))
    return (*group, passed)


def two_steps(s, info, sums, passed, rows):
    joined = add_passed(s, info, sums[2], passed, rows)
    near = within(sums[1], "tensor", (s,), flip(1))
    mirror = within(joined, "tensor", (s,), flip(3))
    return (later(sums[0], joined), near, mirror)


def rope_tables(length):
    halfdim = HEAD_DIM // 2
    power = np.float32(-math.log(10000.0) * 2.0) * np.arange(halfdim, dtype=np.float32)
    inverse = np.exp(power / np.float32(HEAD_DIM))
    turn = np.arange(length, dtype=np.float32)[:, None] * inverse[None, :]
    cosine, sine = np.cos(turn), np.sin(turn)
    return np.tile(cosine, (1, 4)), np.tile(np.concatenate([-sine, sine], axis=1), (1, 2))


def body(clean, noise, times, flags, cotangent, w_main, w_half, w_mod):
    section = lax.axis_index("section")
    part = lax.axis_index("tensor")
    dp_part = lax.axis_index("dp")
    local_seqs, length, width = clean.shape
    columns = w_main.shape[3]
    halfdim = HEAD_DIM // 2

    def mine(values):
        return lax.dynamic_index_in_dim(values, part, 0, keepdims=False)

    theta = math.pi / 2 * (mine(times).astype(F32) + 1.0) / (TSTEPS + 1.0)
    noisy = jnp.cos(theta) * mine(clean).astype(F32) + jnp.sin(theta) * mine(noise).astype(F32)
    target = mine(cotangent)
    info = jnp.stack([section, part, dp_part % 2, mine(flags)]).astype(jnp.int32)

    halfwidth = width // 2
    freqs = jnp.exp(-math.log(10000.0) * jnp.arange(halfwidth, dtype=F32) / halfwidth)
    angles = times.astype(F32)[:, None] * freqs[None, :]
    temb = jnp.concatenate([jnp.sin(angles), jnp.cos(angles)], axis=1)
    mode_part = jnp.einsum("nd,dpc->pnc", temb, w_mod[0].astype(F32), precision=HIGHEST)
    mode_part = mode_part.reshape(3, 4 * columns)
    mode_high = lax.reduce_precision(mode_part, 8, 7)
    own_modes = jnp.concatenate(
        [mode_high, mode_part - mode_high, jnp.zeros((MODE_ROWS - 6, 4 * columns), F32)], axis=0
    ).astype(BF)

    main_local = w_main[0].reshape(width, 4 * columns)
    half_local = w_half[0]
    half_other = swap(half_local, "section", 1)
    second_local = jnp.concatenate([half_other, half_local], axis=0)
    odd = (1, 3)

    def odd_flip(value, axis, bits):
        return within(value, axis, odd, flip(bits))

    one = jnp.concatenate([my_half(main_local, dp_part), own_modes], axis=0)
    one_near = swap(one, "tensor", 1)
    one_mirror = swap(one, "tensor", 3)
    temb_turn = jnp.stack(
        [lax.dynamic_index_in_dim(temb, part ^ i, 0, keepdims=False) for i in FLIPS]
    )
    cosine, sine = (jnp.asarray(table) for table in rope_tables(length))
    one_near, (noisy, temb_turn, info, second_local) = lax.optimization_barrier(
        (one_near, (noisy, temb_turn, info, second_local))
    )
    one_near_x = swap(one_near, "dp", 1)
    one_far = swap(one_mirror, "tensor", 1)
    one_mirror_x = swap(one_mirror, "dp", 1)
    two_half = my_half(second_local, dp_part)
    two_mirror = odd_flip(later(two_half, one_mirror, one_near_x), "tensor", 3)
    one_far_x = swap(one_far, "dp", 1)
    two_near = odd_flip(later(second_local, one_far, one_mirror_x), "tensor", 1)
    two_far = odd_flip(two_mirror, "tensor", 1)
    two_mirror_x = odd_flip(later(two_mirror, one_far_x), "dp", 1)
    two_far_x = odd_flip(two_far, "dp", 1)
    first = place(info, None, 0, [main_local], False)
    first = place(info, first, 1, [one_near, one_near_x], False)
    first = place(info, first, 2, [one_mirror, one_mirror_x], False)
    first = place(info, first, 3, [one_far, one_far_x], False)
    second = place(info, None, 0, [second_local], True)
    second = place(info, second, 1, [two_near], True)
    second = place(info, second, 2, [two_mirror, two_mirror_x], True)
    second = place(info, second, 3, [two_far, two_far_x], True)
    modes = pick_modes(info, [own_modes, one_near, one_mirror, one_far])
    temb_other = swap(temb_turn, "dp", 1)
    temb_pair = jnp.where(
        dp_part % 2 == 0,
        jnp.concatenate([temb_turn, temb_other]),
        jnp.concatenate([temb_other, temb_turn]),
    )

    def attend(s, base, arrived, keep):
        return attention_forward(s, info, base, arrived, modes, cosine, sine, first, keep)

    def feed(s, arrived, keep, chain=None):
        return mlp_forward(s, info, arrived, modes, first, second, keep, chain)

    def feed_back(s, grad, kept, keep, chain=None):
        return mlp_back(s, info, grad, modes, kept, first, second, keep, chain)

    def attend_back(s, grad, kept, chain, message):
        return attention_back(
            s, info, grad, modes, cosine, sine, kept, first, chain, message
        )

    def after(value, earlier):
        return lax.optimization_barrier((value, earlier))

    def across(value, *which):
        return within(value, "dp", which, flip(1))

    value = attend(0, noisy, None, False)[0]
    value = feed(1, section_hop(value, 0, 1), None)[0]
    value = attend(2, None, section_hop(value, 1, 1), False)[0]
    value = feed(3, section_hop(value, 2, 1), None)[0]
    guess = cyclic(value, "section", 1)

    noisy, temb_pair = after(noisy, temb_pair)
    kept_0 = attend(0, noisy, guess, True)
    stream_1 = section_hop(kept_0[0], 0, 1)
    normed_0 = across(kept_0[6], 0)
    kept_1 = feed(1, later(stream_1, normed_0), "packs")
    stream_2 = section_hop(kept_1[0], 1, 1)
    pack_1, stream_2 = after(kept_1[4:8], stream_2)
    early_1 = trade_shared(pack_1, 1, length)
    kept_2 = attend(2, None, stream_2, True)
    stream_3 = section_hop(kept_2[0], 2, 1)
    normed_2 = across(kept_2[6], 2)
    kept_3 = feed(3, later(stream_3, normed_2), "message", kept_2[7:])

    back_3 = feed_back(3, later(target, early_1[1:3]), kept_3, "message", kept_3[7:])
    grad_2 = section_hop(back_3[0], 3, -1)
    message_3, grad_2 = after(back_3[2], grad_2)
    other_3 = across(message_3, 3)
    back_2 = attend_back(2, grad_2, kept_2, back_3[5:], None)
    grad_1 = lax.ppermute(back_2[0], "section", [(2, 1)])
    rows_high = trade((back_2[5], later(back_2[6], grad_1), *back_2[7:]), (2, 3))
    back_1 = feed_back(1, later(grad_1, rows_high[2:]), kept_1, "packs")
    grad_0 = section_hop(later(back_1[0], early_1[3:]), 1, -1)
    grad_0 = later(grad_0, other_3)
    back_0 = attend_back(0, grad_0, kept_0, kept_0[7:], back_2[2])
    other_even = across(back_0[2], 0, 2)
    other_0, other_2 = (normed_0, other_even), (normed_2, other_even)

    def pass_on(far, s):
        return within(far, "tensor", (s,), flip(1))

    def other_pairs(value, s):
        size = lax.axis_size("dp")
        bit = 2
        while bit < size:
            partner = within(value, "dp", (s,), lambda i, n: i ^ bit)
            value = (value.astype(F32) + partner.astype(F32)).astype(BF)
            bit *= 2
        return value

    def finished(s, own):
        own = other_pairs(own, s)
        return (own, across(own, s))

    (far_3,) = mlp_sums(3, info, kept_3, back_3, later(other_3, back_0[0]), (3,))
    passed_3 = later(pass_on(far_3, 3), rows_high)
    sums_3 = mlp_sums(3, info, kept_3, back_3, later(other_3, far_3), (0, 1, 2))
    late_1 = trade_shared(later(back_1[2:], back_0[0]), 1, length)
    group_3 = two_steps(3, info, sums_3, passed_3, width)
    own_3 = total_parts(3, info, group_3, width)
    other_0, other_2 = later((other_0, other_2), late_1[:4], own_3)
    block = length // 4
    places = [(pack, pack.shape[0] - block) for pack in early_1[:4]]
    places += [(pack, pack.shape[0] - MODE_ROWS - block) for pack in late_1[:4]]
    places_high = [(rows, 0) for rows in rows_high] + [(rows, block) for rows in rows_high]
    groups = [((1,), places), ((2, 3), places_high)]
    results = collect(info, groups, block, None)
    other_0, results = after(other_0, results)
    (far_0,) = attention_sums(0, info, kept_0, back_0, other_0, (3,), True)
    passed_0 = pass_on(far_0, 0)
    sums_0 = attention_sums(0, info, kept_0, back_0, later(other_0, far_0), (0, 1, 2), True)
    pair_3 = finished(3, own_3)
    group_0 = two_steps(0, info, sums_0, later(passed_0, pair_3), width // 2)
    (far_2,) = attention_sums(2, info, kept_2, back_2, other_2, (3,), False)
    passed_2 = pass_on(far_2, 2)
    sums_2 = attention_sums(2, info, kept_2, back_2, later(other_2, far_2), (0, 1, 2), False)
    group_2 = two_steps(2, info, sums_2, later(passed_2, group_0[0]), width // 2)
    own_1 = mlp_grads(1, info, early_1, late_1, length)
    own_0 = total_parts(0, info, group_0, width // 2)
    places = rest_at(group_0, width // 2, 0) + rest_at(group_0, width // 2, block)
    outputs, in_grads = collect(info, [((0,), places)], block, results)
    own_2 = total_parts(2, info, group_2, width // 2)
    pair_0, pair_1, pair_2 = finished(0, own_0), finished(1, own_1), finished(2, own_2)
    pairs = [pair_0, pair_1, pair_2, pair_3]
    pairs, outputs, in_grads = lax.optimization_barrier((pairs, outputs, in_grads))
    main_total, lent, second_total, mode_grads = finish(info, pairs, width)
    returned = swap(lent, "section", 1)
    mode_total = jnp.einsum("nd,npc->dpc", temb_pair, mode_grads, precision=HIGHEST)
    bit = 2
    while bit < lax.axis_size("dp"):
        mode_total = mode_total + swap(mode_total, "dp", bit)
        bit *= 2
    main_total = main_total.reshape(1, width, 4, columns)
    returned, main_total, mode_total = lax.optimization_barrier(
        (returned, main_total, mode_total)
    )
    half_total = choose_half(info, returned, second_total)
    return (
        outputs[None],
        in_grads[None],
        main_total,
        half_total[None],
        mode_total[None],
    )


def solution(mesh):
    in_specs = (
        P("dp", None, None),
        P("dp", None, None),
        P("dp"),
        P("dp"),
        P("dp", None, None),
        P("section", None, None, "tensor"),
        P("section", "tensor", None),
        P("section", None, None, "tensor"),
    )
    out_specs = (
        P("section", "dp", "tensor", None),
        P("section", "dp", "tensor", None),
        P("section", None, None, "tensor"),
        P("section", "tensor", None),
        P("section", None, None, "tensor"),
    )
    return jax.shard_map(body, mesh=mesh, in_specs=in_specs, out_specs=out_specs, check_vma=False)
```

```python
import functools
import math

import jax
import jax.numpy as jnp
import numpy as np
from jax import lax
from jax.experimental import pallas as pl
from jax.experimental.pallas import tpu as pltpu
from jax.sharding import PartitionSpec as P

HEAD_DIM = 64
TSTEPS = 1000
EPSILON = 1e-05
HIGHEST = lax.Precision.HIGHEST
BF = jnp.bfloat16
F32 = jnp.float32
VMEM_BYTES = 32 * 1024 * 1024
WEIGHT_SIZE = 4 * 768 * 768
FLIPS = (0, 1, 3, 2)
GELU_C = math.sqrt(2.0 / math.pi)
GELU_A = 0.044715


def cyclic(value, axis, by):
    size = lax.axis_size(axis)
    return lax.ppermute(value, axis, [(i, (i + by) % size) for i in range(size)])


def swap(value, axis, bit):
    size = lax.axis_size(axis)
    return lax.ppermute(value, axis, [(i, i ^ bit) for i in range(size)])


def within(value, axis, which, route):
    size = lax.axis_size(axis)
    pairs = [(s * size + i, s * size + route(i, size)) for s in which for i in range(size)]
    return lax.ppermute(value, ("section", axis), pairs)


def section_hop(value, source, by):
    target = source + by
    if source // 2 == target // 2:
        return swap(value, "section", 1)
    return cyclic(value, "section", by)


def dot(left, right):
    return lax.dot_general(left, right, (((1,), (0,)), ((), ())), preferred_element_type=F32)


def dot_nt(left, right):
    return lax.dot_general(left, right, (((1,), (1,)), ((), ())), preferred_element_type=F32)


def dot_tn(left, right):
    return lax.dot_general(left, right, (((0,), (0,)), ((), ())), preferred_element_type=F32)


def standardize(stream):
    centred = stream - jnp.mean(stream, axis=-1, keepdims=True)
    variance = jnp.mean(centred * centred, axis=-1, keepdims=True)
    inverse = lax.rsqrt(variance + EPSILON)
    return centred * inverse, inverse


def swap_halves(block, first):
    return jnp.where(first, pltpu.roll(block, 96, 1), pltpu.roll(block, 32, 1))


def first_mask(rows):
    lane = lax.broadcasted_iota(jnp.int32, (rows, 128), 1)
    return (lane % HEAD_DIM) < HEAD_DIM // 2


def norm_back(normed_grad, stream, scale, grad):
    hat, inverse = standardize(stream)
    shift_grad = jnp.sum(normed_grad, axis=0, keepdims=True)
    scale_grad = jnp.sum(normed_grad * hat, axis=0, keepdims=True)
    hat_grad = normed_grad * (1.0 + scale)
    mean_one = jnp.mean(hat_grad, axis=-1, keepdims=True)
    mean_two = jnp.mean(hat_grad * hat, axis=-1, keepdims=True)
    in_grad = grad + inverse * (hat_grad - mean_one - hat * mean_two)
    return in_grad, shift_grad, scale_grad


def start_all(copies):
    for copy in copies:
        copy.start()


def wait_all(copies):
    for copy in copies:
        copy.wait()


def slot_rows(info, slot, block):
    return pl.ds(pl.multiple_of(slot_part(info, slot) * block, block), block)


def send_halves(send, source, target, at):
    for k in range(2):
        send(source.at[k], target.at[at + k])


def put_halves(ref, value):
    half = ref.shape[2]
    ref[0] = value[:, :half]
    ref[1] = value[:, half:]


MODE_ROWS = 16


def put_mode_grads(ref, values):
    joined = jnp.concatenate(values, axis=0)
    high = joined.astype(BF)
    rest = (joined - high.astype(F32)).astype(BF)
    filler = jnp.zeros((MODE_ROWS - 6, joined.shape[1]), BF)
    both = jnp.concatenate([high, rest, filler], axis=0)
    columns = both.shape[1] // 4
    ref[...] = jnp.zeros_like(ref)
    for part in range(4):
        ref[part, :, :columns] = both[:, part * columns : (part + 1) * columns]


def slot_part(info, slot):
    return info[1] ^ FLIPS[slot]


def send_rows(send, source, info, outs, second):
    block = source.shape[0] // 4
    for slot, out in enumerate(outs):
        target = out.at[pl.ds(block if second else 0, block)]
        send(source.at[slot_rows(info, slot, block)], target)


def row_outs(rows, width):
    return [(shape((rows // 2, width), BF), hbm())] * 4


def vmem():
    return pl.BlockSpec(memory_space=pltpu.VMEM)


def smem():
    return pl.BlockSpec(memory_space=pltpu.SMEM)


def hbm():
    return pl.BlockSpec(memory_space=pltpu.HBM)


def anywhere():
    return pl.BlockSpec(memory_space=pl.ANY)


def params(limit):
    return pltpu.CompilerParams(vmem_limit_bytes=limit)


def cost(flops, nbytes):
    return pl.CostEstimate(flops=flops, bytes_accessed=nbytes, transcendentals=0)


def call(kernel, ins, outs, scratch, aliases, estimate, limit=VMEM_BYTES):
    def placed(value, spec):
        if spec.memory_space is pltpu.HBM:
            return pltpu.with_memory_space_constraint(value, pltpu.HBM)
        if value.size >= WEIGHT_SIZE:
            return pltpu.with_memory_space_constraint(value, pltpu.VMEM)
        return value

    def result(value, spec):
        if spec.memory_space is pltpu.HBM:
            return pltpu.HBM(value.shape, value.dtype)
        if math.prod(value.shape) >= WEIGHT_SIZE:
            return pltpu.VMEM(value.shape, value.dtype)
        return value

    return pl.pallas_call(
        kernel,
        out_shape=[result(*pair) for pair in outs],
        in_specs=[spec for _, spec in ins],
        out_specs=[spec for _, spec in outs],
        scratch_shapes=scratch,
        input_output_aliases=aliases,
        compiler_params=params(limit),
        cost_estimate=estimate,
    )(*[placed(*pair) for pair in ins])


def shape(dims, dtype):
    return jax.ShapeDtypeStruct(dims, dtype)


DMA = pltpu.SemaphoreType.DMA


def place_kernel(slot, odd_only, *refs):
    info, pieces, (out, sems) = refs[0], refs[1:-3], refs[-2:]
    rows = out.shape[1] // len(pieces)

    def copy_all():
        copies = []
        for i, piece in enumerate(pieces):
            begin = 0
            if len(pieces) == 2:
                begin = pl.multiple_of((info[2] if i == 0 else 1 - info[2]) * rows, rows)
            target = out.at[slot, pl.ds(begin, rows)]
            copies.append(pltpu.make_async_copy(piece.at[pl.ds(0, rows)], target, sems.at[i]))
        start_all(copies)
        wait_all(copies)

    if odd_only:
        pl.when(info[0] % 2 == 1)(copy_all)
    else:
        copy_all()


def first_kernel(odd_only, info, piece, out, sems):
    place_kernel(0, odd_only, info, piece, None, out, sems)


def place(info, weight, slot, pieces, odd_only):
    ins = [(info, smem())] + [(piece, anywhere()) for piece in pieces]
    width = pieces[0].shape[1]
    aliases = {}
    if weight is None:
        kernel = functools.partial(first_kernel, odd_only)
    else:
        kernel = functools.partial(place_kernel, slot, odd_only)
        aliases = {len(ins): 0}
        ins.append((weight, vmem()))
    outs = [(shape((4, width, width), BF), vmem())]
    estimate = cost(1_000_000, 2_000_000)
    return call(kernel, ins, outs, [DMA((2,))], aliases, estimate, 1024 * 1024)[0]


def modes_kernel(*refs):
    info, pieces, (modes, mode_ref, sems) = refs[0], refs[1:5], refs[5:]
    copies = [
        pltpu.make_async_copy(
            piece.at[pl.ds(piece.shape[0] - MODE_ROWS, MODE_ROWS)], mode_ref.at[i], sems.at[i]
        )
        for i, piece in enumerate(pieces)
    ]
    start_all(copies)
    wait_all(copies)
    columns = modes.shape[1] // 4
    for part in range(4):
        bits = info[1] ^ part
        block = mode_ref[bits ^ (bits >> 1)].astype(F32)
        value = block[0:3] + block[3:6]
        chosen = jnp.zeros((3, columns), F32)
        for sequence in range(4):
            here = value[:, sequence * columns : (sequence + 1) * columns]
            chosen = jnp.where(info[1] == sequence, here, chosen)
        modes[:, part * columns : (part + 1) * columns] = chosen


def pick_modes(info, pieces):
    width = pieces[0].shape[1]
    ins = [(info, smem())] + [(piece, anywhere()) for piece in pieces]
    outs = [(shape((3, width), F32), vmem())]
    scratch = [pltpu.VMEM((4, MODE_ROWS, width), BF), DMA((4,))]
    estimate = cost(1_000_000, 1_000_000)
    return call(modes_kernel, ins, outs, scratch, {}, estimate, 2 * 1024 * 1024)[0]


def head_parts(heads, head):
    j, at = head // 3, head % 3 * HEAD_DIM
    return tuple(heads[j, :, at + 192 * i : at + 192 * i + HEAD_DIM] for i in range(3))


def attention_forward_kernel(s, has_base, has_arrived, keep, *refs):
    refs = list(refs)
    info = refs.pop(0)
    base = refs.pop(0) if has_base else None
    arrived = refs.pop(0) if has_arrived else None
    modes, cosine, sine, w = refs[:4]
    refs = refs[4:]
    result = refs.pop(0)
    if keep:
        heads_out, lse_out, attended_out, branch_out, stream_out = refs[:5]
        normed_out = refs[5]
        row_out = refs[6:10]
        refs = refs[10:]
    normed, branch, heads, attended_ref, scores_ref = refs[:5]
    if keep:
        stream_ref, lse, halves, osems = refs[5:]

    def load_stream():
        if not has_base:
            return arrived[...].astype(F32)
        if not has_arrived:
            return base[...]
        return base[...] + info[3].astype(F32) * arrived[...].astype(F32)

    @pl.when(info[0] == s)
    def _():
        outs = []

        def send(source, target):
            copy = pltpu.make_async_copy(source, target, osems.at[len(outs)])
            copy.start()
            outs.append(copy)

        stream = load_stream()
        hat, _ = standardize(stream)
        normed[...] = (hat * (1.0 + modes[1:2, :]) + modes[0:1, :]).astype(BF)
        rows = normed.shape[0]
        if keep:
            stream_ref[...] = stream
            send(stream_ref, stream_out)
            put_halves(halves, normed[...])
            send_halves(send, halves, normed_out, 0)
        first = first_mask(rows)
        low = lax.broadcasted_iota(jnp.int32, (rows, 128), 1) < HEAD_DIM
        for j in range(4):
            raw = dot(normed[...], w[j, :, :576])
            turned = []
            for unit in range(3):
                block = raw[:, unit * 128 : (unit + 1) * 128]
                block = block * cosine[...] + swap_halves(block, first) * sine[...]
                if unit == 0:
                    block = block * 0.125
                if unit == 1:
                    block = jnp.where(low, block * 0.125, block)
                turned.append(block)
            heads[j] = jnp.concatenate(turned + [raw[:, 384:576]], axis=1).astype(BF)
            if keep:
                send(heads.at[j], heads_out.at[j])
        for head in range(12):
            q, k, _ = head_parts(heads, head)
            scores_ref[head] = dot_nt(k, q)
        for j in range(4):
            pieces_t = [jnp.zeros((HEAD_DIM, rows), BF)]
            for head in range(3 * j, 3 * j + 3):
                _, _, v = head_parts(heads, head)
                scores = scores_ref[head]
                top = jnp.max(scores, axis=0, keepdims=True)
                raised = jnp.exp(scores - top)
                total = jnp.sum(raised, axis=0, keepdims=True)
                if keep:
                    lse[head : head + 1, :] = top + jnp.log(total)
                mixed = dot_tn(v, raised.astype(BF)) * (1.0 / total)
                pieces_t.append(mixed.astype(BF))
            attended_ref[j] = jnp.concatenate(pieces_t, axis=0).T
            if keep:
                send(attended_ref.at[j], attended_out.at[j])
        for j in range(4):
            part = dot_nt(attended_ref[j], w[j, :, 512:768])
            branch[...] = part if j == 0 else branch[...] + part
        result[...] = (load_stream() + modes[2:3, :] * branch[...]).astype(BF)
        if keep:
            send(lse, lse_out)
            send(branch, branch_out)
            send_rows(send, result, info, row_out, False)
            wait_all(outs)


def attention_forward(s, info, base, arrived, modes, cosine, sine, weights, keep):
    width = modes.shape[1]
    rows = cosine.shape[0]
    ins = [(info, smem())]
    for value in (base, arrived):
        if value is not None:
            ins.append((value, vmem()))
    ins += [(modes, vmem()), (cosine, vmem()), (sine, vmem()), (weights, vmem())]
    outs = [(shape((rows, width), BF), vmem())]
    scratch = [
        pltpu.VMEM((rows, width), BF),
        pltpu.VMEM((rows, width), F32),
        pltpu.VMEM((4, rows, 576), BF),
        pltpu.VMEM((4, rows, 256), BF),
        pltpu.VMEM((12, rows, rows), F32),
    ]
    if keep:
        outs += [
            (shape((4, rows, 576), BF), hbm()),
            (shape((12, rows), F32), hbm()),
            (shape((4, rows, 256), BF), hbm()),
            (shape((rows, width), F32), hbm()),
            (shape((rows, width), F32), hbm()),
            (shape((2, rows, width // 2), BF), hbm()),
        ]
        outs += row_outs(rows, width)
        scratch += [
            pltpu.VMEM((rows, width), F32),
            pltpu.VMEM((12, rows), F32),
            pltpu.VMEM((2, rows, width // 2), BF),
            DMA((19,)),
        ]
    kernel = functools.partial(
        attention_forward_kernel, s, base is not None, arrived is not None, keep
    )
    return call(kernel, ins, outs, scratch, {}, cost(2_000_000_000, 6_000_000))


def attention_back_kernel(s, shared, *refs):
    info, grad, modes, cosine, sine, w = refs[:6]
    heads_in, lse_in, attended_in, branch_in, stream_in = refs[6:11]
    refs = refs[15 + shared :]
    in_grad, mode_out, message, pack_out, bg_out = refs[:5]
    row_out = refs[5:9]
    heads, lse, attended_ref, branch, stream, bg, ng, halves, pack_ref = refs[9:18]
    att_grad, scores_ref, prob_grads, probs_ref, ds_ref, raw_ref = refs[18:24]
    mode_ref, isems, osems = refs[24:]

    @pl.when(info[0] == s)
    def _():
        loads = []
        for source, target in (
            (heads_in, heads),
            (lse_in, lse),
            (attended_in, attended_ref),
            (stream_in, stream),
            (branch_in, branch),
        ):
            copy = pltpu.make_async_copy(source, target, isems.at[len(loads)])
            loads.append(copy)
        start_all(loads)
        outs = []

        def send(source, target):
            copy = pltpu.make_async_copy(source, target, osems.at[len(outs)])
            copy.start()
            outs.append(copy)

        g = grad[...].astype(F32)
        rows = g.shape[0]
        bg[...] = (modes[2:3, :] * g).astype(BF)
        put_halves(halves, bg[...])
        send_halves(send, halves, bg_out, 0)
        send_halves(send, halves, message, 0)
        first = first_mask(rows)
        for j in range(4):
            att_grad[j] = dot(bg[...], w[j, :, 512:768]).astype(BF)
        wait_all(loads[:2])
        for head in range(12):
            q, k, _ = head_parts(heads, head)
            scores_ref[head] = dot_nt(k, q)
        for head in range(12):
            _, _, v = head_parts(heads, head)
            at = 64 + head % 3 * HEAD_DIM
            prob_grads[head] = dot_nt(v, att_grad[head // 3, :, at : at + HEAD_DIM])
        for head in range(12):
            probs = jnp.exp(scores_ref[head] - lse[head : head + 1, :])
            inner = jnp.sum(prob_grads[head] * probs, axis=0, keepdims=True)
            probs_ref[head] = probs.astype(BF)
            ds_ref[head] = (probs * (prob_grads[head] - inner)).astype(BF)
        wait_all(loads[2:])
        for j in range(4):
            dq, dk, dv = [], [], []
            for head in range(3 * j, 3 * j + 3):
                q, k, _ = head_parts(heads, head)
                at = 64 + head % 3 * HEAD_DIM
                dv.append(dot(probs_ref[head], att_grad[j, :, at : at + HEAD_DIM]))
                dk.append(dot(ds_ref[head], q))
                dq.append(dot_tn(k, ds_ref[head]))
            dq_all = (jnp.concatenate(dq, axis=0) * 0.125).T
            both = jnp.concatenate([dq_all] + dk, axis=1)
            turned = []
            for unit in range(3):
                block = both[:, unit * 128 : (unit + 1) * 128]
                turned.append(block * cosine[...] - swap_halves(block, first) * sine[...])
            raw = jnp.concatenate(turned + dv, axis=1).astype(BF)
            raw_ref[j] = raw
            pack_ref[j, 0] = raw[:, :384]
            pack_ref[j, 1] = jnp.concatenate([raw[:, 384:576], attended_ref[j, :, 64:256]], axis=1)
            send(pack_ref.at[j, info[2]], pack_out.at[j])
            send(pack_ref.at[j, 1 - info[2]], message.at[2 + j])
        for j in range(4):
            part = dot_nt(raw_ref[j], w[j, :, :576])
            ng[...] = part if j == 0 else ng[...] + part
        total, shift_grad, scale_grad = norm_back(
            ng[...], stream[...], modes[1:2, :], grad[...].astype(F32)
        )
        in_grad[...] = total.astype(BF)
        send_rows(send, in_grad, info, row_out, True)
        gate_grad = jnp.sum(grad[...].astype(F32) * branch[...], axis=0, keepdims=True)
        put_mode_grads(mode_ref, (shift_grad, scale_grad, gate_grad))
        send(mode_ref, mode_out)
        wait_all(outs)


def attention_back(s, info, grad, modes, cosine, sine, kept, weights, chain, message):
    rows, width = grad.shape
    ins = [(info, smem()), (grad, vmem()), (modes, vmem()), (cosine, vmem()), (sine, vmem())]
    ins += [(weights, vmem())]
    ins += [(value, hbm()) for value in kept[1:6]]
    outs = [
        (shape((rows, width), BF), vmem()),
        (shape((4, MODE_ROWS, 256), BF), hbm()),
        (shape((6, rows, width // 2), BF), hbm()),
        (shape((4, rows, width // 2), BF), hbm()),
        (shape((2, rows, width // 2), BF), hbm()),
    ]
    outs += row_outs(rows, width)
    aliases = {len(ins) + i: len(outs) - 4 + i for i in range(4)}
    ins += [(value, hbm()) for value in chain]
    if message is not None:
        aliases[len(ins)] = 2
        ins.append((message, hbm()))
    scratch = [
        pltpu.VMEM((4, rows, 576), BF),
        pltpu.VMEM((12, rows), F32),
        pltpu.VMEM((4, rows, 256), BF),
        pltpu.VMEM((rows, width), F32),
        pltpu.VMEM((rows, width), F32),
        pltpu.VMEM((rows, width), BF),
        pltpu.VMEM((rows, width), F32),
        pltpu.VMEM((2, rows, width // 2), BF),
        pltpu.VMEM((4, 2, rows, width // 2), BF),
        pltpu.VMEM((4, rows, 256), BF),
        pltpu.VMEM((12, rows, rows), F32),
        pltpu.VMEM((12, rows, rows), F32),
        pltpu.VMEM((12, rows, rows), BF),
        pltpu.VMEM((12, rows, rows), BF),
        pltpu.VMEM((4, rows, 576), BF),
        pltpu.VMEM((4, MODE_ROWS, 256), BF),
        DMA((5,)),
        DMA((17,)),
    ]
    kernel = functools.partial(attention_back_kernel, s, 0 if message is None else 1)
    return call(kernel, ins, outs, scratch, aliases, cost(3_000_000_000, 10_000_000))


def mlp_forward_kernel(s, keep, *refs):
    info, arrived, modes, w1, w2 = refs[:5]
    refs = refs[5 + (4 if keep == "message" else 0) :]
    result = refs[0]
    refs = refs[1:]
    if keep:
        slope_out, branch_out, stream_out = refs[:3]
        refs = refs[3:]
    if keep == "packs":
        packs = refs[:4]
        refs = refs[4:]
    if keep == "message":
        act_out, normed_out, message = refs[:3]
        row_out = refs[3:7]
        refs = refs[7:]
    normed, branch = refs[:2]
    if keep:
        act_ref, slope_ref, halves, osems = refs[2:]

    @pl.when(info[0] == s)
    def _():
        outs = []

        def send(source, target):
            copy = pltpu.make_async_copy(source, target, osems.at[len(outs)])
            copy.start()
            outs.append(copy)

        hat, _ = standardize(arrived[...].astype(F32))
        normed[...] = (hat * (1.0 + modes[1:2, :]) + modes[0:1, :]).astype(BF)
        rows = normed.shape[0]
        if keep:
            send(arrived, stream_out)
        if keep == "packs":
            for pack in packs[:3]:
                send(normed, pack.at[pl.ds(0, rows)])
        if keep == "message":
            put_halves(halves, normed[...])
            send_halves(send, halves, normed_out, 0)
            send_halves(send, halves, message, 0)
        hidden_next = dot(normed[...], w1[0])
        for j in range(4):
            hidden = hidden_next
            if j < 3:
                hidden_next = dot(normed[...], w1[j + 1])
            square = hidden * hidden
            bend = jnp.tanh(GELU_C * hidden * (1.0 + GELU_A * square))
            act = (0.5 * hidden * (1.0 + bend)).astype(BF)
            if keep:
                slope = 0.5 * (1.0 + bend) + (0.5 * GELU_C) * hidden * (1.0 - bend * bend) * (
                    1.0 + (3.0 * GELU_A) * square
                )
                slope_ref[j] = slope.astype(BF)
                send(slope_ref.at[j], slope_out.at[j])
            if keep == "packs":
                act_ref[j] = act
                send(act_ref.at[j], packs[j].at[pl.ds(rows if j < 3 else 0, rows)])
            if keep == "message":
                put_halves(act_ref.at[j], act)
                send(act_ref.at[j, info[2]], act_out.at[j])
                send(act_ref.at[j, 1 - info[2]], message.at[8 + j])
            part = dot(act, w2[j])
            branch[...] = part if j == 0 else branch[...] + part
        result[...] = (arrived[...].astype(F32) + modes[2:3, :] * branch[...]).astype(BF)
        if keep:
            send(branch, branch_out)
            block = rows // 4
            if keep == "packs":
                for slot, pack in enumerate(packs):
                    target = pack.at[pl.ds(pack.shape[0] - block, block)]
                    send(result.at[slot_rows(info, slot, block)], target)
            else:
                send_rows(send, result, info, row_out, False)
            wait_all(outs)


def mlp_forward(s, info, arrived, modes, first, second, keep, chain=None):
    rows, width = arrived.shape
    ins = [(info, smem()), (arrived, vmem()), (modes, vmem())]
    ins += [(first, vmem()), (second, vmem())]
    outs = [(shape((rows, width), BF), vmem())]
    scratch = [
        pltpu.VMEM((rows, width), BF),
        pltpu.VMEM((rows, width), F32),
    ]
    if keep:
        outs += [
            (shape((4, rows, width), BF), hbm()),
            (shape((rows, width), F32), hbm()),
            (shape((rows, width), BF), hbm()),
        ]
        if keep == "packs":
            outs += [(shape((2 * rows + rows // 4, width), BF), hbm())] * 3
            outs += [(shape((rows + rows // 4, width), BF), hbm())]
        else:
            outs += [
                (shape((4, rows, width // 2), BF), hbm()),
                (shape((2, rows, width // 2), BF), hbm()),
                (shape((12, rows, width // 2), BF), hbm()),
            ]
            outs += row_outs(rows, width)
        wide = (4, rows, width) if keep == "packs" else (4, 2, rows, width // 2)
        scratch += [
            pltpu.VMEM(wide, BF),
            pltpu.VMEM((4, rows, width), BF),
            pltpu.VMEM((2, rows, width // 2), BF),
            DMA((24,)),
        ]
    aliases = {}
    if keep == "message":
        aliases = {len(ins) + i: len(outs) - 4 + i for i in range(4)}
        ins += [(value, hbm()) for value in chain]
    kernel = functools.partial(mlp_forward_kernel, s, keep)
    return call(kernel, ins, outs, scratch, aliases, cost(2_400_000_000, 10_000_000))


def mlp_back_kernel(s, keep, *refs):
    info, grad, modes, slope_in, branch_in, stream_in, w1, w2 = refs[:8]
    if keep == "packs":
        in_grad, mode_out = refs[8:10]
        packs = refs[10:14]
        refs = refs[14:]
    else:
        in_grad, mode_out, message, hidden_out, bg_out = refs[13:18]
        row_out = refs[18:22]
        refs = refs[22:]
    slope, branch, stream, bg, ng, halves, hidden_ref = refs[:7]
    mode_ref, isems, osems = refs[7:]

    @pl.when(info[0] == s)
    def _():
        loads = [
            pltpu.make_async_copy(source, target, isems.at[i])
            for i, (source, target) in enumerate(
                ((slope_in, slope), (stream_in, stream), (branch_in, branch))
            )
        ]
        start_all(loads)
        outs = []

        def send(source, target):
            copy = pltpu.make_async_copy(source, target, osems.at[len(outs)])
            copy.start()
            outs.append(copy)

        g = grad[...].astype(F32)
        rows = g.shape[0]
        bg[...] = (modes[2:3, :] * g).astype(BF)
        if keep == "packs":
            for pack in packs[:3]:
                send(bg, pack.at[pl.ds(0, rows)])
        else:
            put_halves(halves, bg[...])
            send_halves(send, halves, bg_out, 0)
            send_halves(send, halves, message, 2)
        act_grad_next = dot_nt(bg[...], w2[0])
        for j in range(4):
            act_grad = act_grad_next
            if j < 3:
                act_grad_next = dot_nt(bg[...], w2[j + 1])
            if j == 0:
                loads[0].wait()
            hidden_grad = (act_grad * slope[j].astype(F32)).astype(BF)
            if keep == "packs":
                hidden_ref[j] = hidden_grad
                send(hidden_ref.at[j], packs[j].at[pl.ds(rows if j < 3 else 0, rows)])
            else:
                put_halves(hidden_ref.at[j], hidden_grad)
                send(hidden_ref.at[j, info[2]], hidden_out.at[j])
                send(hidden_ref.at[j, 1 - info[2]], message.at[4 + j])
            part = dot_nt(hidden_grad, w1[j])
            ng[...] = part if j == 0 else ng[...] + part
        wait_all(loads[1:])
        total, shift_grad, scale_grad = norm_back(
            ng[...], stream[...].astype(F32), modes[1:2, :], grad[...].astype(F32)
        )
        in_grad[...] = total.astype(BF)
        block = rows // 4
        if keep == "packs":
            for slot, pack in enumerate(packs):
                at = pack.shape[0] - MODE_ROWS - block
                send(in_grad.at[slot_rows(info, slot, block)], pack.at[pl.ds(at, block)])
        else:
            send_rows(send, in_grad, info, row_out, True)
        gate_grad = jnp.sum(grad[...].astype(F32) * branch[...], axis=0, keepdims=True)
        put_mode_grads(mode_ref, (shift_grad, scale_grad, gate_grad))
        send(mode_ref, mode_out)
        if keep == "packs":
            for slot, pack in enumerate(packs):
                send(
                    mode_ref.at[slot_part(info, slot)],
                    pack.at[pl.ds(pack.shape[0] - MODE_ROWS, MODE_ROWS), pl.ds(0, 256)],
                )
        wait_all(outs)


def mlp_back(s, info, grad, modes, kept, first, second, keep, chain=None):
    rows, width = grad.shape
    ins = [(info, smem()), (grad, vmem()), (modes, vmem())]
    ins += [(value, hbm()) for value in kept[1:4]]
    ins += [(first, vmem()), (second, vmem())]
    outs = [
        (shape((rows, width), BF), vmem()),
        (shape((4, MODE_ROWS, 256), BF), hbm()),
    ]
    aliases = {}
    if keep == "packs":
        rest = rows // 4 + MODE_ROWS
        outs += [(shape((2 * rows + rest, width), BF), hbm())] * 3
        outs += [(shape((rows + rest, width), BF), hbm())]
    else:
        aliases = {len(ins): 2}
        ins += [(kept[6], hbm())]
        outs += [
            (shape(kept[6].shape, BF), hbm()),
            (shape((4, rows, width // 2), BF), hbm()),
            (shape((2, rows, width // 2), BF), hbm()),
        ]
        outs += row_outs(rows, width)
        aliases.update({len(ins) + i: len(outs) - 4 + i for i in range(4)})
        ins += [(value, hbm()) for value in chain]
    wide = (4, rows, width) if keep == "packs" else (4, 2, rows, width // 2)
    scratch = [
        pltpu.VMEM((4, rows, width), BF),
        pltpu.VMEM((rows, width), F32),
        pltpu.VMEM((rows, width), BF),
        pltpu.VMEM((rows, width), BF),
        pltpu.VMEM((rows, width), F32),
        pltpu.VMEM((2, rows, width // 2), BF),
        pltpu.VMEM(wide, BF),
        pltpu.VMEM((4, MODE_ROWS, 256), BF),
        DMA((3,)),
        DMA((18,)),
    ]
    kernel = functools.partial(mlp_back_kernel, s, keep)
    return call(kernel, ins, outs, scratch, aliases, cost(2_400_000_000, 12_000_000))


def row_copies(group, row, target, sems):
    rows = target.shape[0] // 4
    return [
        pltpu.make_async_copy(
            pack.at[pl.ds(row, rows)], target.at[pl.ds(i * rows, rows)], sems.at[i]
        )
        for i, pack in enumerate(group)
    ]


def rest_to_slots(slots, row_ref, mode_ref, outs, at, info, sems):
    copies = []
    for slot, out in zip(slots, outs):
        row = at
        if row_ref is not None:
            block = row_ref.shape[1]
            target = out.at[pl.ds(row, block)]
            copies.append(pltpu.make_async_copy(row_ref.at[slot], target, sems.at[0, slot]))
            row += block
        target = out.at[pl.ds(row, MODE_ROWS), pl.ds(0, 256)]
        copies.append(
            pltpu.make_async_copy(mode_ref.at[slot_part(info, slot)], target, sems.at[1, slot])
        )
    return copies


def two_sequences(own, other, at, target, sems, which):
    rows = own.shape[1]
    copies = []
    for j in which:
        copies += [
            pltpu.make_async_copy(own.at[j], target.at[j, pl.ds(0, rows)], sems.at[j, 0]),
            pltpu.make_async_copy(
                other.at[at + j], target.at[j, pl.ds(rows, rows)], sems.at[j, 1]
            ),
        ]
    return copies


def attention_sums_kernel(s, slots, with_rows, *refs):
    info, normed_in, bg_in, pack_in, other_normed, other, mode_in = refs[:7]
    row_in = refs[7 : 7 + with_rows]
    refs = refs[7 + with_rows :]
    outs = refs[: len(slots)]
    refs = refs[len(slots) :]
    n_ref, b_ref, p_ref, held, row_ref, mode_ref = refs[:6]
    nsems, bsems, psems, osems, lsems, rsems = refs[6:]
    half = held.shape[1]

    @pl.when(info[0] == s)
    def _():
        loads = [pltpu.make_async_copy(mode_in, mode_ref, lsems.at[4])]
        for i, value in enumerate(row_in):
            loads.append(pltpu.make_async_copy(value, row_ref.at[i], lsems.at[i]))
        rows = row_ref if with_rows else None
        moves = rest_to_slots(slots, rows, mode_ref, outs, half, info, rsems)
        copies = (
            two_sequences(normed_in, other_normed, 0, n_ref, nsems, range(2))
            + two_sequences(pack_in, other, 2, p_ref, psems, slots)
            + two_sequences(bg_in, other, 0, b_ref, bsems, range(2))
        )
        start_all(copies + loads)
        wait_all(copies + loads)
        start_all(moves)
        tokens = jnp.concatenate([n_ref[0], n_ref[1]], axis=1)
        branch = jnp.concatenate([b_ref[0], b_ref[1]], axis=1)
        for j, out in zip(slots, outs):
            held[j] = dot_tn(p_ref[j], tokens).astype(BF)

            @pl.when(info[2] == 1)
            def _():
                outward = dot_tn(p_ref[j, :, 128:], branch)
                held[j, half // 2 :, :] = outward[half // 2 - 128 :].astype(BF)

            copy = pltpu.make_async_copy(held.at[j], out.at[pl.ds(0, half)], osems.at[j])
            copy.start()
            moves.append(copy)
        wait_all(moves)


def attention_sums(s, info, kept, back, other, slots, with_rows):
    rows = kept[6].shape[1]
    half = kept[6].shape[2]
    width = 2 * half
    ins = [(info, smem())]
    ins += [
        (kept[6], hbm()),
        (back[4], hbm()),
        (back[3], hbm()),
        (other[0], anywhere()),
        (other[1], anywhere()),
        (back[1], hbm()),
    ]
    rest = MODE_ROWS
    if with_rows:
        ins += [(value, hbm()) for value in back[5:9]]
        rest += rows // 2
    outs = [(shape((half + rest, width), BF), hbm())] * len(slots)
    scratch = [
        pltpu.VMEM((2, 2 * rows, half), BF),
        pltpu.VMEM((2, 2 * rows, half), BF),
        pltpu.VMEM((4, 2 * rows, half), BF),
        pltpu.VMEM((4, half, width), BF),
        pltpu.VMEM((4, rows // 2, width), BF),
        pltpu.VMEM((4, MODE_ROWS, 256), BF),
        DMA((2, 2)),
        DMA((2, 2)),
        DMA((4, 2)),
        DMA((4,)),
        DMA((5,)),
        DMA((2, 4)),
    ]
    kernel = functools.partial(attention_sums_kernel, s, slots, 4 if with_rows else 0)
    return call(kernel, ins, outs, scratch, {}, cost(1_300_000_000, 8_000_000))


def mlp_sums_kernel(s, slots, *refs):
    info, normed_in, bg_in, hidden_in, act_in, other, mode_in = refs[:7]
    outs = refs[7 : 7 + len(slots)]
    refs = refs[7 + len(slots) :]
    n_ref, b_ref, h_ref, a_ref, held, mode_ref = refs[:6]
    nsems, bsems, hsems, asems, osems, lsems, rsems = refs[6:]
    half = held.shape[1] // 2

    @pl.when(info[0] == s)
    def _():
        loads = [pltpu.make_async_copy(mode_in, mode_ref, lsems.at[4])]
        moves = rest_to_slots(slots, None, mode_ref, outs, 2 * half, info, rsems)
        left = two_sequences(normed_in, other, 0, n_ref, nsems, range(2))
        left += two_sequences(hidden_in, other, 4, h_ref, hsems, slots)
        right = two_sequences(bg_in, other, 2, b_ref, bsems, range(2))
        right += two_sequences(act_in, other, 8, a_ref, asems, slots)
        start_all(left + right + loads)
        wait_all(left)
        tokens = jnp.concatenate([n_ref[0], n_ref[1]], axis=1)
        for j in slots:
            held[j, :half] = dot_tn(h_ref[j], tokens).astype(BF)
        wait_all(right + loads)
        start_all(moves)
        branch = jnp.concatenate([b_ref[0], b_ref[1]], axis=1)
        for j, out in zip(slots, outs):
            held[j, half:] = dot_tn(a_ref[j], branch).astype(BF)
            copy = pltpu.make_async_copy(held.at[j], out.at[pl.ds(0, 2 * half)], osems.at[j])
            copy.start()
            moves.append(copy)
        wait_all(moves)


def mlp_sums(s, info, kept, back, other, slots):
    rows = kept[5].shape[1]
    half = kept[5].shape[2]
    width = 2 * half
    ins = [(info, smem())]
    ins += [
        (kept[5], hbm()),
        (back[4], hbm()),
        (back[3], hbm()),
        (kept[4], hbm()),
        (other, anywhere()),
        (back[1], hbm()),
    ]
    outs = [(shape((width + MODE_ROWS, width), BF), hbm())] * len(slots)
    scratch = [
        pltpu.VMEM((2, 2 * rows, half), BF),
        pltpu.VMEM((2, 2 * rows, half), BF),
        pltpu.VMEM((4, 2 * rows, half), BF),
        pltpu.VMEM((4, 2 * rows, half), BF),
        pltpu.VMEM((4, width, width), BF),
        pltpu.VMEM((4, MODE_ROWS, 256), BF),
        DMA((2, 2)),
        DMA((2, 2)),
        DMA((4, 2)),
        DMA((4, 2)),
        DMA((4,)),
        DMA((5,)),
        DMA((2, 4)),
    ]
    kernel = functools.partial(mlp_sums_kernel, s, slots)
    return call(kernel, ins, outs, scratch, {}, cost(2_600_000_000, 12_000_000))


def add_passed_kernel(s, *refs):
    info, own, passed, out, held, total, sems = refs
    rows = total.shape[0]
    rest = own.shape[0] - rows

    @pl.when(info[0] == s)
    def _():
        copies = [
            pltpu.make_async_copy(value, held.at[i], sems.at[i])
            for i, value in enumerate((own, passed))
        ]
        start_all(copies)
        wait_all(copies)
        moves = [
            pltpu.make_async_copy(
                held.at[i, pl.ds(rows, rest)], out.at[pl.ds(rows + i * rest, rest)], sems.at[2 + i]
            )
            for i in range(2)
        ]
        start_all(moves)
        total[...] = (held[0, :rows].astype(F32) + held[1, :rows].astype(F32)).astype(BF)
        moves.append(pltpu.make_async_copy(total, out.at[pl.ds(0, rows)], sems.at[4]))
        moves[2].start()
        wait_all(moves)


def add_passed(s, info, own, passed, rows):
    length, width = own.shape
    ins = [(info, smem()), (own, hbm()), (passed, anywhere())]
    outs = [(shape((2 * length - rows, width), BF), hbm())]
    scratch = [pltpu.VMEM((2, length, width), BF), pltpu.VMEM((rows, width), BF), DMA((5,))]
    kernel = functools.partial(add_passed_kernel, s)
    return call(kernel, ins, outs, scratch, {}, cost(10_000_000, 5_000_000))[0]


def rest_at(group, rows, at):
    rest = group[0].shape[0] - rows
    own, near, mirror = group
    return [(own, rows + at), (near, rows + at), (mirror, rows + at), (mirror, rows + rest + at)]


def join_modes(held, columns):
    return jnp.concatenate([held[i, :, :columns] for i in range(4)], axis=1)


def total_kernel(s, at, *refs):
    info = refs[0]
    parts = refs[1:-4]
    out, held, mode_ref, sems = refs[-4:]
    rows = held.shape[1]

    @pl.when(info[0] == s)
    def _():
        copies = []
        for i, part in enumerate(parts):
            copies.append(
                pltpu.make_async_copy(part.at[pl.ds(0, rows)], held.at[i], sems.at[0, i])
            )
        for i, (part, row) in enumerate(rest_at(parts, rows, at)):
            modes = part.at[pl.ds(row, MODE_ROWS), pl.ds(0, 256)]
            copies.append(pltpu.make_async_copy(modes, mode_ref.at[i], sems.at[1, i]))
        start_all(copies)
        wait_all(copies)
        total = held[0].astype(F32)
        for i in range(1, len(parts)):
            total = total + held[i].astype(F32)
        out[:rows] = total.astype(BF)
        out[rows:] = join_modes(mode_ref, out.shape[1] // 4)


def total_parts(s, info, group, rows):
    width = group[0].shape[1]
    at = group[0].shape[0] - MODE_ROWS - rows
    ins = [(info, smem())] + [(value, anywhere()) for value in group]
    outs = [(shape((rows + MODE_ROWS, width), BF), vmem())]
    scratch = [
        pltpu.VMEM((len(group), rows, width), BF),
        pltpu.VMEM((4, MODE_ROWS, 256), BF),
        DMA((2, 4)),
    ]
    kernel = functools.partial(total_kernel, s, at)
    return call(kernel, ins, outs, scratch, {}, cost(10_000_000, 5_000_000))[0]


def mlp_grads_kernel(s, *refs):
    info = refs[0]
    early, late = refs[1:6], refs[6:11]
    out = refs[11]
    a_ref, n_ref, h_ref, b_ref, mode_ref, sems = refs[12:]
    rows = n_ref.shape[0] // 4

    def places(group):
        shared = [(pack, 0) for pack in (*group[:3], group[4])]
        columns = [(pack, rows) for pack in group[:3]] + [(group[3], 0)]
        return shared, columns

    @pl.when(info[0] == s)
    def _():
        copies = []
        for k, (target, wanted) in enumerate(
            zip((n_ref, a_ref, b_ref, h_ref), places(early) + places(late))
        ):
            for i, (pack, row) in enumerate(wanted):
                copies.append(
                    pltpu.make_async_copy(
                        pack.at[pl.ds(row, rows)], target.at[pl.ds(i * rows, rows)], sems.at[k, i]
                    )
                )
        for i, pack in enumerate(late[:4]):
            modes = pack.at[pl.ds(pack.shape[0] - MODE_ROWS, MODE_ROWS), pl.ds(0, 256)]
            copies.append(pltpu.make_async_copy(modes, mode_ref.at[i], sems.at[4, i]))
        start_all(copies)
        wait_all(copies)
        width = n_ref.shape[1]
        out[pl.ds(2 * width, MODE_ROWS), :] = join_modes(mode_ref, width // 4)
        for c in range(width // 256):
            part = pl.ds(c * 256, 256)
            out[part, :] = dot_tn(h_ref[:, part], n_ref[...]).astype(BF)
            out[pl.ds(width + c * 256, 256), :] = dot_tn(a_ref[:, part], b_ref[...]).astype(BF)


def mlp_grads(s, info, early, late, rows):
    width = late[0].shape[1]
    ins = [(info, smem())]
    ins += [(value, anywhere()) for value in (*early, *late)]
    outs = [(shape((2 * width + MODE_ROWS, width), BF), vmem())]
    scratch = [pltpu.VMEM((4 * rows, width), BF)] * 4
    scratch += [pltpu.VMEM((4, MODE_ROWS, 256), BF), DMA((5, 4))]
    kernel = functools.partial(mlp_grads_kernel, s)
    return call(kernel, ins, outs, scratch, {}, cost(2_600_000_000, 10_000_000))[0]


def finish_kernel(*refs):
    info = refs[0]
    pairs = [refs[1 + 2 * s : 3 + 2 * s] for s in range(4)]
    main, lent, second_out, modes, held, mode_ref, second, sems = refs[9:]
    width = main.shape[0]
    half = width // 2
    here = pl.ds(pl.multiple_of(info[2] * half, half), half)
    there = pl.ds(pl.multiple_of((1 - info[2]) * half, half), half)

    def mode_copies(s):
        copies = []
        for i, value in enumerate(pairs[s]):
            rows = value.at[pl.ds(value.shape[0] - MODE_ROWS, MODE_ROWS)]
            which = info[2] if i == 0 else 1 - info[2]
            copies.append(pltpu.make_async_copy(rows, mode_ref.at[which], sems.at[4 + i]))
        return copies

    def halves(s):
        own, other = pairs[s]
        copies = mode_copies(s)
        for k in range(own.shape[0] // half):
            part = pl.ds(k * half, half)
            copies += [
                pltpu.make_async_copy(own.at[part], held.at[k, here], sems.at[2 * k]),
                pltpu.make_async_copy(other.at[part], held.at[k, there], sems.at[2 * k + 1]),
            ]
        start_all(copies)
        wait_all(copies)
        main[...] = held[0].astype(F32).T
        if own.shape[0] > width:
            lent[...] = held[1, :half]
            second[...] = held[1, half:].astype(F32)
            copy = pltpu.make_async_copy(second, second_out, sems.at[6])
            copy.start()
            copy.wait()

    for s in (0, 2, 3):

        @pl.when(info[0] == s)
        def _():
            halves(s)

    @pl.when(info[0] == 1)
    def _():
        copies = mode_copies(1)
        for i, value in enumerate(pairs[1]):
            for k in range(2):
                part = value.at[pl.ds(k * width, width)]
                copies.append(
                    pltpu.make_async_copy(part, held.at[2 * i + k], sems.at[2 * i + k])
                )
        start_all(copies)
        wait_all(copies)
        main[...] = (held[0].astype(F32) + held[2].astype(F32)).T
        lent[...] = (held[1, :half].astype(F32) + held[3, :half].astype(F32)).astype(BF)
        second[...] = held[1, half:].astype(F32) + held[3, half:].astype(F32)
        copy = pltpu.make_async_copy(second, second_out, sems.at[6])
        copy.start()
        copy.wait()

    columns = width // 4
    for i in range(2):
        value = mode_ref[i].astype(F32)
        value = value[0:3] + value[3:6]
        for j in range(4):
            modes[4 * i + j] = value[:, j * columns : (j + 1) * columns]


def finish(info, pairs, width):
    ins = [(info, smem())] + [(value, anywhere()) for pair in pairs for value in pair]
    outs = [
        (shape((width, width), F32), vmem()),
        (shape((width // 2, width), BF), vmem()),
        (shape((width // 2, width), F32), hbm()),
        (shape((8, 3, width // 4), F32), vmem()),
    ]
    scratch = [
        pltpu.VMEM((4, width, width), BF),
        pltpu.VMEM((2, MODE_ROWS, width), BF),
        pltpu.VMEM((width // 2, width), F32),
        DMA((7,)),
    ]
    return call(finish_kernel, ins, outs, scratch, {}, cost(10_000_000, 10_000_000))


def collect_kernel(rows_at, *refs):
    info = refs[0]
    outs = refs[-6:-4]
    held, wide, sems, osems = refs[-4:]
    block = held.shape[2]
    begin = 1
    for sections, rows in rows_at:
        group = refs[begin : begin + 8]
        begin += 8
        chosen = info[0] == sections[0]
        for s in sections[1:]:
            chosen = jnp.logical_or(chosen, info[0] == s)

        @pl.when(chosen)
        def _():
            copies = []
            for i, (pack, row) in enumerate(zip(group, rows)):
                copies.append(
                    pltpu.make_async_copy(
                        pack.at[pl.ds(row, block)], held.at[i // 4, i % 4], sems.at[i]
                    )
                )
            start_all(copies)
            wait_all(copies)
            moves = []
            for k in range(2):
                for i in range(4):
                    wide[k, slot_part(info, i)] = held[k, i].astype(F32)
                moves.append(pltpu.make_async_copy(wide.at[k], outs[k], osems.at[k]))
                moves[k].start()
            wait_all(moves)


def collect(info, groups, block, older):
    ins = [(info, smem())]
    rows_at = []
    for sections, places in groups:
        ins += [(value, anywhere()) for value, _ in places]
        rows_at.append((sections, tuple(row for _, row in places)))
    width = groups[0][1][0][0].shape[1]
    outs = [(shape((4, block, width), F32), hbm())] * 2
    aliases = {}
    if older is not None:
        aliases = {len(ins) + i: i for i in range(2)}
        ins += [(value, hbm()) for value in older]
    scratch = [
        pltpu.VMEM((2, 4, block, width), BF),
        pltpu.VMEM((2, 4, block, width), F32),
        DMA((8,)),
        DMA((2,)),
    ]
    kernel = functools.partial(collect_kernel, tuple(rows_at))
    return call(kernel, ins, outs, scratch, aliases, cost(1_000_000, 2_000_000))


def half_kernel(info, returned, second, out, wide, sem):
    @pl.when(info[0] % 2 == 0)
    def _():
        wide[...] = returned[...].astype(F32)
        copy = pltpu.make_async_copy(wide, out, sem)
        copy.start()
        copy.wait()


def choose_half(info, returned, second):
    ins = [(info, smem()), (returned, vmem()), (second, hbm())]
    outs = [(shape(second.shape, F32), hbm())]
    scratch = [pltpu.VMEM(second.shape, F32), DMA]
    return call(half_kernel, ins, outs, scratch, {2: 0}, cost(1_000_000, 2_000_000))[0]


def flip(bits):
    return lambda i, n: i ^ bits


def later(value, *ended):
    return lax.optimization_barrier((value, ended))[0]


def my_half(chunk, dp_part):
    half = chunk.shape[0] // 2
    return lax.dynamic_slice_in_dim(chunk, dp_part % 2 * half, half, 0)


def trade(packs, which):
    others = [
        within(pack, "tensor", which, flip(bits)) for pack, bits in zip(packs[1:], FLIPS[1:])
    ]
    return (packs[0], *others)


def trade_shared(packs, s, rows):
    group = trade(packs, (s,))
    passed = within(group[2][:rows], "tensor", (s,), flip(1))
    return (*group, passed)


def two_steps(s, info, sums, passed, rows):
    joined = add_passed(s, info, sums[2], passed, rows)
    near = within(sums[1], "tensor", (s,), flip(1))
    mirror = within(joined, "tensor", (s,), flip(3))
    return (later(sums[0], joined), near, mirror)


def rope_tables(length):
    halfdim = HEAD_DIM // 2
    power = np.float32(-math.log(10000.0) * 2.0) * np.arange(halfdim, dtype=np.float32)
    inverse = np.exp(power / np.float32(HEAD_DIM))
    turn = np.arange(length, dtype=np.float32)[:, None] * inverse[None, :]
    cosine, sine = np.cos(turn), np.sin(turn)
    return np.tile(cosine, (1, 4)), np.tile(np.concatenate([-sine, sine], axis=1), (1, 2))


def body(clean, noise, times, flags, cotangent, w_main, w_half, w_mod):
    section = lax.axis_index("section")
    part = lax.axis_index("tensor")
    dp_part = lax.axis_index("dp")
    local_seqs, length, width = clean.shape
    columns = w_main.shape[3]
    halfdim = HEAD_DIM // 2

    def mine(values):
        return lax.dynamic_index_in_dim(values, part, 0, keepdims=False)

    theta = math.pi / 2 * (mine(times).astype(F32) + 1.0) / (TSTEPS + 1.0)
    noisy = jnp.cos(theta) * mine(clean).astype(F32) + jnp.sin(theta) * mine(noise).astype(F32)
    target = mine(cotangent)
    info = jnp.stack([section, part, dp_part % 2, mine(flags)]).astype(jnp.int32)

    halfwidth = width // 2
    freqs = jnp.exp(-math.log(10000.0) * jnp.arange(halfwidth, dtype=F32) / halfwidth)
    angles = times.astype(F32)[:, None] * freqs[None, :]
    temb = jnp.concatenate([jnp.sin(angles), jnp.cos(angles)], axis=1)
    mode_part = jnp.einsum("nd,dpc->pnc", temb, w_mod[0].astype(F32), precision=HIGHEST)
    mode_part = mode_part.reshape(3, 4 * columns)
    mode_high = lax.reduce_precision(mode_part, 8, 7)
    own_modes = jnp.concatenate(
        [mode_high, mode_part - mode_high, jnp.zeros((MODE_ROWS - 6, 4 * columns), F32)], axis=0
    ).astype(BF)

    main_local = w_main[0].reshape(width, 4 * columns)
    half_local = w_half[0]
    half_other = swap(half_local, "section", 1)
    second_local = jnp.concatenate([half_other, half_local], axis=0)
    odd = (1, 3)

    def odd_flip(value, axis, bits):
        return within(value, axis, odd, flip(bits))

    one = jnp.concatenate([my_half(main_local, dp_part), own_modes], axis=0)
    one_near = swap(one, "tensor", 1)
    one_mirror = swap(one, "tensor", 3)
    temb_turn = jnp.stack(
        [lax.dynamic_index_in_dim(temb, part ^ i, 0, keepdims=False) for i in FLIPS]
    )
    cosine, sine = (jnp.asarray(table) for table in rope_tables(length))
    one_near, (noisy, temb_turn, info, second_local) = lax.optimization_barrier(
        (one_near, (noisy, temb_turn, info, second_local))
    )
    one_near_x = swap(one_near, "dp", 1)
    one_far = swap(one_mirror, "tensor", 1)
    one_mirror_x = swap(one_mirror, "dp", 1)
    two_half = my_half(second_local, dp_part)
    two_mirror = odd_flip(later(two_half, one_mirror, one_near_x), "tensor", 3)
    one_far_x = swap(one_far, "dp", 1)
    two_near = odd_flip(later(second_local, one_far, one_mirror_x), "tensor", 1)
    two_far = odd_flip(two_mirror, "tensor", 1)
    two_mirror_x = odd_flip(later(two_mirror, one_far_x), "dp", 1)
    two_far_x = odd_flip(two_far, "dp", 1)
    first = place(info, None, 0, [main_local], False)
    first = place(info, first, 1, [one_near, one_near_x], False)
    first = place(info, first, 2, [one_mirror, one_mirror_x], False)
    first = place(info, first, 3, [one_far, one_far_x], False)
    second = place(info, None, 0, [second_local], True)
    second = place(info, second, 1, [two_near], True)
    second = place(info, second, 2, [two_mirror, two_mirror_x], True)
    second = place(info, second, 3, [two_far, two_far_x], True)
    modes = pick_modes(info, [own_modes, one_near, one_mirror, one_far])
    temb_other = swap(temb_turn, "dp", 1)
    temb_pair = jnp.where(
        dp_part % 2 == 0,
        jnp.concatenate([temb_turn, temb_other]),
        jnp.concatenate([temb_other, temb_turn]),
    )

    def attend(s, base, arrived, keep):
        return attention_forward(s, info, base, arrived, modes, cosine, sine, first, keep)

    def feed(s, arrived, keep, chain=None):
        return mlp_forward(s, info, arrived, modes, first, second, keep, chain)

    def feed_back(s, grad, kept, keep, chain=None):
        return mlp_back(s, info, grad, modes, kept, first, second, keep, chain)

    def attend_back(s, grad, kept, chain, message):
        return attention_back(
            s, info, grad, modes, cosine, sine, kept, first, chain, message
        )

    def after(value, earlier):
        return lax.optimization_barrier((value, earlier))

    def across(value, *which):
        return within(value, "dp", which, flip(1))

    value = attend(0, noisy, None, False)[0]
    value = feed(1, section_hop(value, 0, 1), None)[0]
    value = attend(2, None, section_hop(value, 1, 1), False)[0]
    value = feed(3, section_hop(value, 2, 1), None)[0]
    guess = cyclic(value, "section", 1)

    noisy, temb_pair = after(noisy, temb_pair)
    kept_0 = attend(0, noisy, guess, True)
    stream_1 = section_hop(kept_0[0], 0, 1)
    normed_0 = across(kept_0[6], 0)
    kept_1 = feed(1, later(stream_1, normed_0), "packs")
    stream_2 = section_hop(kept_1[0], 1, 1)
    pack_1, stream_2 = after(kept_1[4:8], stream_2)
    early_1 = trade_shared(pack_1, 1, length)
    kept_2 = attend(2, None, stream_2, True)
    stream_3 = section_hop(kept_2[0], 2, 1)
    normed_2 = across(kept_2[6], 2)
    kept_3 = feed(3, later(stream_3, normed_2), "message", kept_2[7:])

    back_3 = feed_back(3, later(target, early_1[1:3]), kept_3, "message", kept_3[7:])
    grad_2 = section_hop(back_3[0], 3, -1)
    message_3, grad_2 = after(back_3[2], grad_2)
    other_3 = across(message_3, 3)
    back_2 = attend_back(2, grad_2, kept_2, back_3[5:], None)
    grad_1 = lax.ppermute(back_2[0], "section", [(2, 1)])
    rows_high = trade((back_2[5], later(back_2[6], grad_1), *back_2[7:]), (2, 3))
    back_1 = feed_back(1, later(grad_1, rows_high[2:]), kept_1, "packs")
    grad_0 = section_hop(back_1[0], 1, -1)
    grad_0 = later(grad_0, other_3, early_1[3:])
    back_0 = attend_back(0, grad_0, kept_0, kept_0[7:], back_2[2])
    other_even = across(back_0[2], 0, 2)
    other_0, other_2 = (normed_0, other_even), (normed_2, other_even)

    def pass_on(far, s):
        return within(far, "tensor", (s,), flip(1))

    def other_pairs(value, s):
        size = lax.axis_size("dp")
        bit = 2
        while bit < size:
            partner = within(value, "dp", (s,), lambda i, n: i ^ bit)
            value = (value.astype(F32) + partner.astype(F32)).astype(BF)
            bit *= 2
        return value

    def finished(s, own):
        own = other_pairs(own, s)
        return (own, across(own, s))

    (far_3,) = mlp_sums(3, info, kept_3, back_3, later(other_3, back_0[0]), (3,))
    passed_3 = later(pass_on(far_3, 3), rows_high)
    sums_3 = mlp_sums(3, info, kept_3, back_3, later(other_3, far_3), (0, 1, 2))
    late_1 = trade_shared(later(back_1[2:], back_0[0]), 1, length)
    group_3 = two_steps(3, info, sums_3, passed_3, width)
    own_3 = total_parts(3, info, group_3, width)
    other_0, other_2 = later((other_0, other_2), late_1[:4], own_3)
    block = length // 4
    places = [(pack, pack.shape[0] - block) for pack in early_1[:4]]
    places += [(pack, pack.shape[0] - MODE_ROWS - block) for pack in late_1[:4]]
    places_high = [(rows, 0) for rows in rows_high] + [(rows, block) for rows in rows_high]
    groups = [((1,), places), ((2, 3), places_high)]
    results = collect(info, groups, block, None)
    other_0, results = after(other_0, results)
    (far_0,) = attention_sums(0, info, kept_0, back_0, other_0, (3,), True)
    passed_0 = pass_on(far_0, 0)
    sums_0 = attention_sums(0, info, kept_0, back_0, later(other_0, far_0), (0, 1, 2), True)
    pair_3 = finished(3, own_3)
    group_0 = two_steps(0, info, sums_0, later(passed_0, pair_3), width // 2)
    (far_2,) = attention_sums(2, info, kept_2, back_2, other_2, (3,), False)
    passed_2 = pass_on(far_2, 2)
    sums_2 = attention_sums(2, info, kept_2, back_2, later(other_2, far_2), (0, 1, 2), False)
    group_2 = two_steps(2, info, sums_2, later(passed_2, group_0[0]), width // 2)
    own_1 = mlp_grads(1, info, early_1, late_1, length)
    own_0 = total_parts(0, info, group_0, width // 2)
    places = rest_at(group_0, width // 2, 0) + rest_at(group_0, width // 2, block)
    outputs, in_grads = collect(info, [((0,), places)], block, results)
    own_2 = total_parts(2, info, group_2, width // 2)
    pair_0, pair_1, pair_2 = finished(0, own_0), finished(1, own_1), finished(2, own_2)
    pairs = [pair_0, pair_1, pair_2, pair_3]
    pairs, outputs, in_grads = lax.optimization_barrier((pairs, outputs, in_grads))
    main_total, lent, second_total, mode_grads = finish(info, pairs, width)
    returned = swap(lent, "section", 1)
    mode_total = jnp.einsum("nd,npc->dpc", temb_pair, mode_grads, precision=HIGHEST)
    bit = 2
    while bit < lax.axis_size("dp"):
        mode_total = mode_total + swap(mode_total, "dp", bit)
        bit *= 2
    main_total = main_total.reshape(1, width, 4, columns)
    returned, main_total, mode_total = lax.optimization_barrier(
        (returned, main_total, mode_total)
    )
    half_total = choose_half(info, returned, second_total)
    return (
        outputs[None],
        in_grads[None],
        main_total,
        half_total[None],
        mode_total[None],
    )


def solution(mesh):
    in_specs = (
        P("dp", None, None),
        P("dp", None, None),
        P("dp"),
        P("dp"),
        P("dp", None, None),
        P("section", None, None, "tensor"),
        P("section", "tensor", None),
        P("section", None, None, "tensor"),
    )
    out_specs = (
        P("section", "dp", "tensor", None),
        P("section", "dp", "tensor", None),
        P("section", None, None, "tensor"),
        P("section", "tensor", None),
        P("section", None, None, "tensor"),
    )
    return jax.shard_map(body, mesh=mesh, in_specs=in_specs, out_specs=out_specs, check_vma=False)
```
